32 devices in a mesh: clip: 8 (over z, core), col: 4 (over y, x).
Axes of the slice: x: 2, y: 2, z: 4, core: 2. Of those that a mesh axis runs over, the one named last changes fastest.
Arguments:
- frames: bfloat16 [128, 256, 768], P('clip', 'col'), may hold values from -6 to 6
- cotangent: bfloat16 [128, 256, 768], P('clip', 'col'), may hold values from -6 to 6
- frame_len: int32 [128], P('clip'), may hold values from 64 to 256, as said below
- column_rank: int32 [256], replicated, may hold values from 0 to 255, each once
- gain_one: bfloat16 [768], replicated, may hold values from 0.25 to 1.75
- shift_one: bfloat16 [768], replicated, may hold values from -4 to 4
- w_qkv: bfloat16 [768, 2304], replicated, may hold values from -0.3125 to 0.3125
- bias_qv: bfloat16 [1536], replicated, may hold values from -4 to 4
- w_out: bfloat16 [768, 768], replicated, may hold values from -0.4375 to 0.4375
- bias_out: bfloat16 [768], replicated, may hold values from -4 to 4
- gain_two: bfloat16 [768], replicated, may hold values from 0.25 to 1.75
- shift_two: bfloat16 [768], replicated, may hold values from -4 to 4
- w_up: bfloat16 [768, 3072], replicated, may hold values from -0.21875 to 0.21875
- bias_up: bfloat16 [3072], replicated, may hold values from -4 to 4
- w_down: bfloat16 [3072, 768], replicated, may hold values from -0.109375 to 0.109375
- bias_down: bfloat16 [768], replicated, may hold values from -4 to 4
Outputs:
- output: bfloat16 [128, 256, 768], P('clip', 'col')
- grad_input: float32 [128, 256, 768], P('clip', 'col')
- grad_gain_one: float32 [768], P('col')
- grad_shift_one: float32 [768], P('col')
- grad_w_qkv: float32 [768, 2304], P(None, 'col')
- grad_bias_qv: float32 [1536], P('col')
- grad_w_out: float32 [768, 768], P(None, 'col')
- grad_bias_out: float32 [768], P('col')
- grad_gain_two: float32 [768], P('col')
- grad_shift_two: float32 [768], P('col')
- grad_w_up: float32 [768, 3072], P(None, 'col')
- grad_bias_up: float32 [3072], P('col')
- grad_w_down: float32 [3072, 768], P(None, 'col')
- grad_bias_down: float32 [768], P('col')
The draws below stay inside these ranges and needn't reach their ends.
Inputs may be any that keep to these rules, and one draw needn't show every extreme that they name: `frame_len`: every frame holds 256 or 64 live tokens; among the 16 frames of each index of clip at least one holds 256.
All inputs are finite; a program needn't handle non-finite values.
Results may differ from the reference program's by a relative error of at most 0.02.
Values may be sent and summed in bfloat16 or wider, within the bound.
No kernel may reach another device: no remote copies, remote signals or barrier semaphores. Data moves between devices by JAX's collectives and lax.ppermute only.
A program may use at most 512 MiB of HBM per device.

```python
import math
import jax
import jax.numpy as jnp
from jax import lax

D = 768
HEADS = 12
HD = 64
FF = 3072
FR_DEV = 16
FRAME = 256
FRAMES = 128


def draw_frame_len(key, part):
    key = jax.random.fold_in(key, 11)
    toss_key, pick_key = jax.random.split(key)
    tosses = jax.random.randint(toss_key, (FRAMES,), 0, 3)
    chosen = jax.random.randint(pick_key, (FRAMES // FR_DEV,), 0, FR_DEV)
    places = jnp.arange(FRAMES, dtype=jnp.int32) % FR_DEV
    forced = places == jnp.repeat(chosen, FR_DEV, total_repeat_length=FRAMES)
    whole_frame = jnp.logical_or(tosses == 0, forced)
    return jnp.where(whole_frame, FRAME, FRAME // 4).astype(jnp.int32)


def shard_levels(rng, extent, shards, smallest, largest):
    def one(axis_at, blocks):
        steps = jax.random.uniform(jax.random.fold_in(jax.random.fold_in(rng, 6), axis_at), (blocks,), jnp.float32, smallest / len(shards), largest / len(shards))
        return jnp.repeat(jnp.exp(steps), extent[axis_at] // blocks).reshape((-1,) + (1,) * (len(extent) - axis_at - 1))

    factor_of = one(*shards[0])
    for cut in shards[1:]:
        factor_of = factor_of * one(*cut)
    return factor_of


def scatter_about(key, dims, width, limit, cuts=(), kind=jnp.bfloat16):
    array = width * jax.random.normal(key, dims, jnp.float32)
    if cuts:
        array = array * shard_levels(key, dims, cuts, -0.22, 0.18)
    return jnp.clip(array, -limit, limit).astype(kind)


def setup_inputs(seed: int = 0) -> dict:
    keys = jax.random.split(jax.random.key(seed), 17)
    return {
        "frames": scatter_about(keys[0], (FRAMES, FRAME, D), 1.0, 6.0, ((0, 8), (1, 4))),
        "cotangent": scatter_about(keys[1], (FRAMES, FRAME, D), 1.0, 6.0, ((0, 8), (1, 4))),
        "frame_len": draw_frame_len(jax.random.fold_in(keys[16], 71), 0),
        "column_rank": jax.random.permutation(keys[3], FRAME).astype(jnp.int32),
        "gain_one": jnp.clip(1.0 + 0.15 * jax.random.normal(keys[4], (D,), jnp.float32), 0.25, 1.75).astype(jnp.bfloat16),
        "shift_one": scatter_about(keys[5], (D,), 0.3, 4.0),
        "w_qkv": scatter_about(keys[6], (D, 3 * D), (D // 2) ** -0.5, 0.3125),
        "bias_qv": scatter_about(keys[7], (2 * D,), 0.3, 4.0),
        "w_out": scatter_about(keys[8], (D, D), (D // 4) ** -0.5, 0.4375),
        "bias_out": scatter_about(keys[9], (D,), 0.3, 4.0),
        "gain_two": jnp.clip(1.0 + 0.15 * jax.random.normal(keys[10], (D,), jnp.float32), 0.25, 1.75).astype(jnp.bfloat16),
        "shift_two": scatter_about(keys[11], (D,), 0.3, 4.0),
        "w_up": scatter_about(keys[12], (D, FF), D ** -0.5, 0.21875),
        "bias_up": scatter_about(keys[13], (FF,), 0.3, 4.0),
        "w_down": scatter_about(keys[14], (FF, D), FF ** -0.5, 0.109375),
        "bias_down": scatter_about(keys[15], (D,), 0.3, 4.0),
    }


@jax.custom_vjp
def low(v):
    return lax.optimization_barrier(v.astype(jnp.bfloat16)).astype(jnp.float32)

@jax.custom_vjp
def low_back(v):
    return v

def low_keep(v):
    return (low(v), None)

def low_pass(kept, grad):
    return (grad,)

def back_keep(v):
    return (v, None)

def back_low(kept, grad):
    return (low(grad),)
low.defvjp(low_keep, low_pass)
low_back.defvjp(back_keep, back_low)
EPSILON = 1e-06
MASKED = -1e+30
HIGHEST = lax.Precision.HIGHEST

def norm_rows(inputs, gain_vec, offset):
    average = lax.optimization_barrier(jnp.mean(inputs, axis=-1, keepdims=True))
    centred = inputs - average
    variance = lax.optimization_barrier(jnp.mean(centred * centred, axis=-1, keepdims=True))
    return centred * lax.rsqrt(variance + EPSILON) * gain_vec + offset

def matmul(left, right):
    return jnp.dot(left, right, precision=HIGHEST)

def layer_group(params, block, lengths, ranks):
    gain_one, shift_one, w_qkv, bias_qv, w_out, bias_out, gain_two, shift_two, w_up, bias_up, w_down, bias_down = params
    frames_here = block.shape[0]
    rows = block.reshape(-1, D)
    normed = low(norm_rows(rows, gain_one, shift_one))
    projected = matmul(normed, w_qkv)
    queries = low_back(low(projected[:, :D] + bias_qv[:D]))
    keys_now = low_back(low(projected[:, D:2 * D]))
    values = low_back(low(projected[:, 2 * D:] + bias_qv[D:]))
    head_shape = (frames_here, FRAME, HEADS, HD)
    scores = jnp.einsum('fqhd,fkhd->fhqk', queries.reshape(head_shape), keys_now.reshape(head_shape), precision=HIGHEST) * HD ** (-0.5)
    live = ranks[None, :] < lengths[:, None]
    scores = jnp.where(live[:, None, None, :], low_back(scores), MASKED)
    probs = jax.nn.softmax(scores, axis=-1)
    mixed = jnp.einsum('fhqk,fkhd->fqhd', low(probs), values.reshape(head_shape), precision=HIGHEST)
    mixed = low_back(low(mixed.reshape(-1, D)))
    middle = rows + low_back(matmul(mixed, w_out) + bias_out)
    normed_two = low(norm_rows(middle, gain_two, shift_two))
    hidden = low_back(matmul(normed_two, w_up) + bias_up)
    active = low(jax.nn.gelu(hidden, approximate=False))
    return (middle + matmul(active, w_down) + bias_down).reshape(block.shape)

def reference(frames, cotangent, frame_len, column_rank, gain_one, shift_one, w_qkv, bias_qv, w_out, bias_out, gain_two, shift_two, w_up, bias_up, w_down, bias_down):
    per_step = math.gcd(FRAMES, max(1, 4096 // FRAME))
    params = tuple((weight.astype(jnp.float32) for weight in (gain_one, shift_one, w_qkv, bias_qv, w_out, bias_out, gain_two, shift_two, w_up, bias_up, w_down, bias_down)))
    inputs = frames.astype(jnp.float32)
    lens_blocks = frame_len.reshape(FRAMES // per_step, per_step)

    def forward(values_in, weights):

        def one_group(packed):
            return layer_group(weights, packed[0], packed[1], column_rank)
        blocks = values_in.reshape(FRAMES // per_step, per_step, FRAME, D)
        outputs = lax.map(jax.checkpoint(one_group), (blocks, lens_blocks))
        return outputs.reshape(FRAMES, FRAME, D)
    output, pullback = jax.vjp(forward, inputs, params)
    grad_input, weight_grads = pullback(cotangent.astype(jnp.float32))
    return (output.astype(jnp.bfloat16), grad_input, weight_grads[0], weight_grads[1], weight_grads[2], weight_grads[3], weight_grads[4], weight_grads[5], weight_grads[6], weight_grads[7], weight_grads[8], weight_grads[9], weight_grads[10], weight_grads[11])
```

```python
import functools
import jax
import jax.numpy as jnp
from jax import lax
from jax.experimental import pallas as pl
from jax.experimental.pallas import tpu as pltpu
from jax.sharding import PartitionSpec as P

HEADS = 12
EPSILON = 1e-06
MASKED = -1e30
F32 = jnp.float32
BF16 = jnp.bfloat16
INV_SQRT2 = 0.5**0.5
INV_SQRT_2PI = 0.3989422804014327
MIB = 1 << 20
GAIN_ONE, SHIFT_ONE, BIAS_OUT, GAIN_TWO, SHIFT_TWO, BIAS_DOWN, BIAS_Q, BIAS_V, BIAS_UP = range(9)


def dot(left, right):
    return lax.dot_general(left, right, (((1,), (0,)), ((), ())), preferred_element_type=F32)


def dot_nt(left, right):
    return lax.dot_general(left, right, (((1,), (1,)), ((), ())), preferred_element_type=F32)


def add_low(left, right):
    return (left.astype(F32) + right.astype(F32)).astype(BF16)


def whole(shape):
    return pl.BlockSpec(shape, lambda *_: (0,) * len(shape), pipeline_mode=pl.Buffered(1))


def lanes(rows, size):
    return pl.BlockSpec((rows, size), lambda f, *_: (0, f))


def params(limit, steps=1):
    return pltpu.CompilerParams(
        vmem_limit_bytes=limit * MIB, dimension_semantics=("arbitrary",) * steps
    )


def standardise(value):
    centred = value - jnp.mean(value, axis=0, keepdims=True)
    root = lax.rsqrt(jnp.mean(centred * centred, axis=0, keepdims=True) + EPSILON)
    return centred * root, root


def standardise_back(grad, gain, xhat, root):
    scaled = grad * gain
    first = jnp.mean(scaled, axis=0, keepdims=True)
    second = jnp.mean(scaled * xhat, axis=0, keepdims=True)
    return root * (scaled - first - xhat * second)


def lane_sums(value):
    total = value[:, :128]
    for at in range(128, value.shape[1], 128):
        total = total + value[:, at : at + 128]
    return total


def to_row(partial):
    return jnp.sum(partial.T, axis=0, keepdims=True)


def pair_diagonal(upper, lower):
    zero = jnp.zeros_like(upper)
    return jnp.concatenate(
        [jnp.concatenate([upper, zero], axis=0), jnp.concatenate([zero, lower], axis=0)], axis=1
    )


def token_rows(pieces):
    return jnp.concatenate([piece[0] for piece in pieces], axis=0)


def attend_kernel(ncol, block, lens, *refs):
    pieces = refs[:ncol]
    ranks, cols, wqkv_t, wout_t = refs[ncol : ncol + 4]
    normed_t, qkv_t, kv_n, mixed_t, middle_t, second_t, lse = refs[ncol + 4 :]
    model, size = normed_t.shape
    head = model // HEADS
    rows_t = token_rows(pieces).astype(F32).T
    xhat, _ = standardise(rows_t)
    normed = (xhat * cols[:, GAIN_ONE : GAIN_ONE + 1] + cols[:, SHIFT_ONE : SHIFT_ONE + 1]).astype(BF16)
    normed_t[...] = normed
    queries = (dot(wqkv_t[:model], normed) + cols[:, BIAS_Q : BIAS_Q + 1]).astype(BF16)
    qkv_t[:model] = queries * BF16(head**-0.5)
    keys = dot(wqkv_t[model : 2 * model], normed)
    qkv_t[model : 2 * model] = keys.astype(BF16)
    kv_n[:, :model] = keys.T.astype(BF16)
    values = dot(wqkv_t[2 * model :], normed) + cols[:, BIAS_V : BIAS_V + 1]
    qkv_t[2 * model :] = values.astype(BF16)
    kv_n[:, model:] = values.T.astype(BF16)
    bias = jnp.where(ranks[...] < lens[pl.program_id(0)], 0.0, MASKED)

    def one(pair, at):
        low, high = pair * 2 * head, (pair * 2 + 1) * head
        where = pl.ds(at, block)
        right = pair_diagonal(qkv_t[pl.ds(low, head), where], qkv_t[pl.ds(high, head), where])
        scores = dot(kv_n[:, pl.ds(low, 2 * head)], right) + bias
        top = jnp.max(scores, axis=0, keepdims=True)
        weight = jnp.exp(scores - top)
        total = jnp.sum(weight, axis=0, keepdims=True)
        probs = (weight * (1.0 / total)).astype(BF16)
        stats = top + jnp.log(total)
        for side, start in enumerate((low, high)):
            cut = slice(side * block, (side + 1) * block)
            lse[0, pl.ds(pair * 2 + side, 1), where] = stats[:, cut]
            value = qkv_t[pl.ds(2 * model + start, head), :]
            mixed_t[pl.ds(start, head), where] = dot(value, probs[:, cut]).astype(BF16)

    pairs_and_blocks(size, block, one)
    middle = rows_t + dot(wout_t[...], mixed_t[...]) + cols[:, BIAS_OUT : BIAS_OUT + 1]
    middle_t[...] = middle
    xhat, _ = standardise(middle)
    second_t[...] = (
        xhat * cols[:, GAIN_TWO : GAIN_TWO + 1] + cols[:, SHIFT_TWO : SHIFT_TWO + 1]
    ).astype(BF16)


def pairs_and_blocks(size, block, one):
    if size == block:
        for pair in range(HEADS // 2):
            one(pair, 0)
    else:

        @pl.loop(0, HEADS // 2 * (size // block))
        def _(step):
            blocks = size // block
            pair = step // blocks
            one(pair, pl.multiple_of((step - pair * blocks) * block, block))


def attend_call(pieces, ranks, lens, cols, wqkv_t, wout_t):
    ncol = len(pieces)
    per, width, model = pieces[0].shape
    size = ncol * width
    tokens = per * size
    block = min(size, 256)
    piece = pl.BlockSpec((1, width, model), lambda f, *_: (f, 0, 0))
    outs = [
        (model, BF16),
        (3 * model, BF16),
        None,
        (model, BF16),
        (model, F32),
        (model, BF16),
    ]
    out_shape = [jax.ShapeDtypeStruct((o[0], tokens), o[1]) if o else jax.ShapeDtypeStruct((tokens, 2 * model), BF16) for o in outs]
    out_specs = [lanes(o[0], size) if o else pl.BlockSpec((size, 2 * model), lambda f, *_: (f, 0)) for o in outs]
    out_shape.append(jax.ShapeDtypeStruct((per, 16, size), F32))
    out_specs.append(pl.BlockSpec((1, 16, size), lambda f, *_: (f, 0, 0)))
    return pl.pallas_call(
        functools.partial(attend_kernel, ncol, block),
        grid_spec=pltpu.PrefetchScalarGridSpec(
            num_scalar_prefetch=1,
            grid=(per,),
            in_specs=[piece] * ncol
            + [whole(ranks.shape), whole(cols.shape), whole(wqkv_t.shape), whole(wout_t.shape)],
            out_specs=out_specs,
        ),
        out_shape=out_shape,
        compiler_params=params(56),
        name="attend",
    )(lens, *pieces, ranks, cols, wqkv_t, wout_t)


def mlp_kernel(ncol, rows, second_t, middle_t, cols, wup_t, wdown_t, active_t, slope_t, *outs):
    model, size = middle_t.shape
    hidden_size = wup_t.shape[0]
    second = second_t[...]
    total = middle_t[...] + cols[:, BIAS_DOWN : BIAS_DOWN + 1]
    for at in range(0, hidden_size, rows):
        column, row = BIAS_UP + at // model, at % model
        hidden = dot(wup_t[at : at + rows], second) + cols[row : row + rows, column : column + 1]
        half = 0.5 + 0.5 * lax.erf(hidden * INV_SQRT2)
        active = (hidden * half).astype(BF16)
        active_t[at : at + rows] = active
        bell = jnp.exp(hidden * hidden * -0.5) * INV_SQRT_2PI
        slope_t[at : at + rows] = (half + hidden * bell).astype(BF16)
        total = total + dot(wdown_t[:, at : at + rows], active)
    result = total.T.astype(BF16)
    width = size // ncol
    for k in range(ncol):
        outs[k][0] = result[k * width : (k + 1) * width]


def mlp_call(ncol, per, second_t, middle_t, cols, wup_t, wdown_t):
    model, tokens = middle_t.shape
    size = tokens // per
    width = size // ncol
    hidden_size = wup_t.shape[0]
    return pl.pallas_call(
        functools.partial(mlp_kernel, ncol, min(256, model)),
        grid=(per,),
        in_specs=[lanes(model, size), lanes(model, size), whole(cols.shape), whole(wup_t.shape), whole(wdown_t.shape)],
        out_specs=[lanes(hidden_size, size)] * 2
        + [pl.BlockSpec((1, width, model), lambda f: (f, 0, 0))] * ncol,
        out_shape=[jax.ShapeDtypeStruct((hidden_size, tokens), BF16)] * 2
        + [jax.ShapeDtypeStruct((per, width, model), BF16)] * ncol,
        compiler_params=params(56),
        name="mlp",
    )(second_t, middle_t, cols, wup_t, wdown_t)


def mlp_back_kernel(ncol, rows, *refs):
    pieces = refs[:ncol]
    slope_t, middle_t, cols, w_up, w_down = refs[ncol : ncol + 5]
    hidden_t, gmiddle_t, gattended_t, sums, up_sums, mid_sums = refs[ncol + 5 :]
    model, size = middle_t.shape
    hidden_size = w_down.shape[0]
    step = pl.program_id(0)

    @pl.when(step == 0)
    def _():
        sums[...] = jnp.zeros_like(sums)
        up_sums[...] = jnp.zeros_like(up_sums)
        mid_sums[...] = jnp.zeros_like(mid_sums)

    cot = token_rows(pieces)
    grad = jnp.zeros((model, size), F32)
    for at in range(0, hidden_size, rows):
        grad_hidden = dot_nt(w_down[at : at + rows], cot) * slope_t[at : at + rows].astype(F32)
        low = grad_hidden.astype(BF16)
        hidden_t[at : at + rows] = low
        up_sums[at : at + rows] += lane_sums(low.astype(F32))
        grad = grad + dot(w_up[:, at : at + rows], low)
    xhat, root = standardise(middle_t[...])
    mid_sums[:model] += lane_sums(grad * xhat)
    mid_sums[model : 2 * model] += lane_sums(grad)
    cot_f32 = cot.astype(F32)
    grad_middle = cot_f32.T + standardise_back(grad, cols[:, GAIN_TWO : GAIN_TWO + 1], xhat, root)
    gmiddle_t[...] = grad_middle
    low = grad_middle.astype(BF16)
    gattended_t[...] = low
    mid_sums[2 * model :] += lane_sums(low.astype(F32))
    sums[3:4] += jnp.sum(cot_f32, axis=0, keepdims=True)

    @pl.when(step == pl.num_programs(0) - 1)
    def _():
        for i in range(3):
            sums[i : i + 1] = to_row(mid_sums[i * model : (i + 1) * model])
        for i in range(hidden_size // model):
            sums[4 + i : 5 + i] = to_row(up_sums[i * model : (i + 1) * model])


def mlp_back_call(pieces, slope_t, middle_t, cols, w_up, w_down):
    ncol = len(pieces)
    per, width, model = pieces[0].shape
    size = ncol * width
    tokens = per * size
    hidden_size = w_down.shape[0]
    piece = pl.BlockSpec((1, width, model), lambda f: (f, 0, 0))
    return pl.pallas_call(
        functools.partial(mlp_back_kernel, ncol, min(256, model)),
        grid=(per,),
        in_specs=[piece] * ncol
        + [lanes(hidden_size, size), lanes(model, size), whole(cols.shape), whole(w_up.shape), whole(w_down.shape)],
        out_specs=[lanes(hidden_size, size), lanes(model, size), lanes(model, size), whole((16, model))],
        out_shape=[
            jax.ShapeDtypeStruct((hidden_size, tokens), BF16),
            jax.ShapeDtypeStruct((model, tokens), F32),
            jax.ShapeDtypeStruct((model, tokens), BF16),
            jax.ShapeDtypeStruct((16, model), F32),
        ],
        scratch_shapes=[pltpu.VMEM((hidden_size, 128), F32), pltpu.VMEM((3 * model, 128), F32)],
        compiler_params=params(56),
        name="mlp_back",
    )(*pieces, slope_t, middle_t, cols, w_up, w_down)


def attend_back_kernel(ncol, block, lens, *refs):
    pieces = refs[:ncol]
    ranks, cols, w_qkv, w_out, qkv_t, kv_n, lse, gattended_t, gmiddle_t = refs[ncol : ncol + 9]
    gproj_t, sums = refs[ncol + 9 : ncol + 11]
    outs = refs[ncol + 11 : 2 * ncol + 11]
    gmixed_t, gacc, vec_sums = refs[2 * ncol + 11 :]
    model, size = gmiddle_t.shape
    head = model // HEADS
    step = pl.program_id(0)

    @pl.when(step == 0)
    def _():
        sums[...] = jnp.zeros_like(sums)
        vec_sums[...] = jnp.zeros_like(vec_sums)

    gmixed_t[...] = dot(w_out[...], gattended_t[...]).astype(BF16)
    bias = jnp.where(ranks[...] < lens[step], 0.0, MASKED)
    many = size != block
    if many:
        gacc[...] = jnp.zeros_like(gacc)

    def one(pair, at):
        low, high = pair * 2 * head, (pair * 2 + 1) * head
        where = pl.ds(at, block)
        right = pair_diagonal(qkv_t[pl.ds(low, head), where], qkv_t[pl.ds(high, head), where])
        scores = dot(kv_n[:, pl.ds(low, 2 * head)], right) + bias
        stats = jnp.concatenate([lse[0, pl.ds(pair * 2 + i, 1), where] for i in range(2)], axis=1)
        probs = jnp.exp(scores - stats)
        probs_low = probs.astype(BF16)
        right = pair_diagonal(gmixed_t[pl.ds(low, head), where], gmixed_t[pl.ds(high, head), where])
        grad_probs = dot(kv_n[:, pl.ds(model + low, 2 * head)], right)
        inner = jnp.sum(probs * grad_probs, axis=0, keepdims=True)
        grad_scores = (probs * (grad_probs - inner)).astype(BF16)
        for side, start in enumerate((low, high)):
            cut = slice(side * block, (side + 1) * block)
            grad_side = grad_scores[:, cut]
            grad_q = dot(qkv_t[pl.ds(model + start, head), :], grad_side) * head**-0.5
            grad_k = dot_nt(qkv_t[pl.ds(start, head), where], grad_side)
            grad_v = dot_nt(gmixed_t[pl.ds(start, head), where], probs_low[:, cut])
            gproj_t[pl.ds(start, head), where] = grad_q.astype(BF16)
            if many:
                gacc[pl.ds(start, head), :] += grad_k
                gacc[pl.ds(model + start, head), :] += grad_v
            else:
                gproj_t[pl.ds(model + start, head), :] = grad_k.astype(BF16)
                gproj_t[pl.ds(2 * model + start, head), :] = grad_v.astype(BF16)

    pairs_and_blocks(size, block, one)
    if many:
        gproj_t[model:] = gacc[...].astype(BF16)
    vec_sums[2 * model : 3 * model] += lane_sums(gproj_t[:model].astype(F32))
    vec_sums[3 * model :] += lane_sums(gproj_t[2 * model :].astype(F32))
    grad = dot(w_qkv[...], gproj_t[...])
    xhat, root = standardise(token_rows(pieces).astype(F32).T)
    vec_sums[:model] += lane_sums(grad * xhat)
    vec_sums[model : 2 * model] += lane_sums(grad)
    total = gmiddle_t[...] + standardise_back(grad, cols[:, GAIN_ONE : GAIN_ONE + 1], xhat, root)
    result = total.T.astype(BF16)
    width = size // ncol
    for k in range(ncol):
        outs[k][0] = result[k * width : (k + 1) * width]

    @pl.when(step == pl.num_programs(0) - 1)
    def _():
        for i in range(4):
            sums[i : i + 1] = to_row(vec_sums[i * model : (i + 1) * model])


def attend_back_call(pieces, ranks, lens, cols, w_qkv, w_out, qkv_t, kv_n, lse, gattended_t, gmiddle_t):
    ncol = len(pieces)
    per, width, model = pieces[0].shape
    size = ncol * width
    tokens = per * size
    block = min(size, 256)
    piece = pl.BlockSpec((1, width, model), lambda f, *_: (f, 0, 0))
    acc = (2 * model, size) if size != block else (8, 128)
    return pl.pallas_call(
        functools.partial(attend_back_kernel, ncol, block),
        grid_spec=pltpu.PrefetchScalarGridSpec(
            num_scalar_prefetch=1,
            grid=(per,),
            in_specs=[piece] * ncol
            + [
                whole(ranks.shape),
                whole(cols.shape),
                whole(w_qkv.shape),
                whole(w_out.shape),
                lanes(3 * model, size),
                pl.BlockSpec((size, 2 * model), lambda f, *_: (f, 0)),
                pl.BlockSpec((1, 16, size), lambda f, *_: (f, 0, 0)),
                lanes(model, size),
                lanes(model, size),
            ],
            out_specs=[lanes(3 * model, size), whole((16, model))] + [piece] * ncol,
            scratch_shapes=[
                pltpu.VMEM((model, size), BF16),
                pltpu.VMEM(acc, F32),
                pltpu.VMEM((4 * model, 128), F32),
            ],
        ),
        out_shape=[
            jax.ShapeDtypeStruct((3 * model, tokens), BF16),
            jax.ShapeDtypeStruct((16, model), F32),
        ]
        + [jax.ShapeDtypeStruct((per, width, model), BF16)] * ncol,
        compiler_params=params(56),
        name="attend_back",
    )(lens, *pieces, ranks, cols, w_qkv, w_out, qkv_t, kv_n, lse, gattended_t, gmiddle_t)


def pick(array, index, axis):
    return lax.dynamic_index_in_dim(array, index, axis, keepdims=False)


class Comm:
    def __init__(self, mesh):
        self.ncol = mesh.shape["col"]
        self.nclip = mesh.shape["clip"]
        self.nz = self.nclip // 2
        self.me = lax.axis_index("col")
        self.clip = lax.axis_index("clip")
        self.core = lax.rem(self.clip, 2)
        self.z = lax.div(self.clip, 2)

    def col_swap(self, array, distance):
        return lax.ppermute(array, "col", [(i, i ^ distance) for i in range(self.ncol)])

    def core_swap(self, array):
        return lax.ppermute(array, "clip", [(i, i ^ 1) for i in range(self.nclip)])

    def z_move(self, array, pairs):
        moves = [(2 * a + c, 2 * b + c) for a, b in pairs for c in range(2)]
        return lax.ppermute(array, "clip", moves)

    def scatter_frames(self, array):
        frames = array.shape[0] // self.ncol
        blocks = array.reshape((self.ncol, frames) + array.shape[1:])
        return [
            self.col_swap(pick(blocks, lax.bitwise_xor(self.me, k), 0), k)
            if k
            else pick(blocks, self.me, 0)
            for k in range(self.ncol)
        ]

    def gather_frames(self, pieces, dtype):
        landed = [self.col_swap(p, k) if k else p for k, p in enumerate(pieces)]
        out = jnp.zeros((self.ncol,) + landed[0].shape, dtype)
        for k, piece in enumerate(landed):
            out = lax.dynamic_update_index_in_dim(
                out, piece.astype(dtype), lax.bitwise_xor(self.me, k), 0
            )
        return out.reshape((-1,) + landed[0].shape[1:])

    def halve(self, terms, bits):
        nbits = self.ncol.bit_length() - 1
        present = list(range(nbits - 1, -1, -1))
        for bit in bits:
            axis = present.index(bit)
            mine = lax.rem(lax.shift_right_logical(self.me, bit), 2)
            away = [pick(t, 1 - mine, axis) for t in terms]
            total = away[0]
            if len(away) > 1:
                total = add_low(away[0], away[1])
            landed = self.col_swap(total, 1 << bit)
            near = [pick(t, mine, axis) for t in terms]
            if len(near) > 1:
                near = [add_low(near[0], near[1])]
            terms = [near[0], landed]
            present.pop(axis)
        return add_low(terms[0], terms[1])

    def reduce_rows(self, grad):
        rows, depth = grad.shape
        part = rows // self.ncol // 4
        nbits = self.ncol.bit_length() - 1
        split = grad.reshape(self.ncol, 2, 2, part, depth)
        keep = pick(split, self.core, 1)
        landed = self.core_swap(pick(split, 1 - self.core, 1))
        order = list(range(nbits))
        half = nbits // 2
        orders = (order, order[half:] + order[:half])
        done = []
        for side in range(2):
            terms = [
                t[:, side].reshape((2,) * nbits + (part, depth)) for t in (keep, landed)
            ]
            done.append(self.halve(terms, orders[side]))
        total = jnp.concatenate(done, axis=0)
        total = self.sum_line(total)
        other = self.core_swap(total)
        first = self.core == 0
        return jnp.concatenate(
            [jnp.where(first, total, other), jnp.where(first, other, total)], axis=0
        )

    def sum_line(self, total):
        nz = self.nz
        for step in range(nz // 2 - 1):
            total = add_low(total, self.z_move(total, [(step, step + 1), (nz - 1 - step, nz - 2 - step)]))
        low, high = nz // 2 - 1, nz // 2
        total = add_low(total, self.z_move(total, [(low, high), (high, low)]))
        for step in range(nz // 2 - 1, 0, -1):
            landed = self.z_move(total, [(step, step - 1), (nz - 1 - step, nz - step)])
            takes = jnp.logical_or(self.z == step - 1, self.z == nz - step)
            total = jnp.where(takes, landed, total)
        return total


def make(mesh):
    def on_device(
        frames,
        cotangent,
        frame_len,
        column_rank,
        gain_one,
        shift_one,
        w_qkv,
        bias_qv,
        w_out,
        bias_out,
        gain_two,
        shift_two,
        w_up,
        bias_up,
        w_down,
        bias_down,
    ):
        comm = Comm(mesh)
        ncol, me = comm.ncol, comm.me
        count, width, model = frames.shape
        per = count // ncol
        size = ncol * width
        order = lax.bitwise_xor(me, jnp.arange(ncol, dtype=jnp.int32))
        ranks = column_rank.reshape(ncol, width)[order].reshape(size, 1)
        lens = pick(frame_len.reshape(ncol, per), me, 0)
        cols = jnp.concatenate(
            [v.reshape(-1, model) for v in (gain_one, shift_one, bias_out, gain_two, shift_two, bias_down, bias_qv, bias_up)]
        ).T.astype(F32)

        pieces = comm.scatter_frames(frames)
        cots = comm.scatter_frames(cotangent)
        normed_t, qkv_t, kv_n, mixed_t, middle_t, second_t, lse = attend_call(
            pieces, ranks, lens, cols, w_qkv.T, w_out.T
        )
        active_t, slope_t, *outs = mlp_call(ncol, per, second_t, middle_t, cols, w_up.T, w_down.T)
        output = comm.gather_frames(outs, BF16)
        cot = jnp.stack(cots, axis=1).reshape(per * size, model)
        grad_w_down = comm.reduce_rows(
            lax.dot_general(cot, active_t, (((0,), (1,)), ((), ())), preferred_element_type=BF16)
        )
        hidden_t, gmiddle_t, gattended_t, mlp_sums = mlp_back_call(cots, slope_t, middle_t, cols, w_up, w_down)
        grad_w_up = comm.reduce_rows(dot_nt(hidden_t, second_t).astype(BF16))
        gproj_t, attend_sums, *outs = attend_back_call(
            pieces, ranks, lens, cols, w_qkv, w_out, qkv_t, kv_n, lse, gattended_t, gmiddle_t
        )
        grad_w_out = comm.reduce_rows(dot_nt(gattended_t, mixed_t).astype(BF16))
        grad_w_qkv = comm.reduce_rows(dot_nt(gproj_t, normed_t).astype(BF16))
        grad_input = comm.gather_frames(outs, F32)
        sums = jnp.concatenate([mlp_sums, attend_sums]).astype(BF16)
        sums = comm.reduce_rows(jnp.concatenate([sums] * ncol)).astype(F32)

        def own(row, rows=1):
            return pick(sums[row : row + rows].reshape(ncol, -1), me, 0)

        return (
            output,
            grad_input,
            own(16),
            own(17),
            grad_w_qkv.astype(F32).T,
            own(18, 2),
            grad_w_out.astype(F32).T,
            own(2),
            own(0),
            own(1),
            grad_w_up.astype(F32).T,
            own(4, hidden_t.shape[0] // model),
            grad_w_down.astype(F32).T,
            own(3),
        )

    return on_device


def solution(mesh):
    return jax.shard_map(
        make(mesh),
        mesh=mesh,
        in_specs=(P("clip", "col", None), P("clip", "col", None), P("clip")) + (P(),) * 13,
        out_specs=(
            P("clip", "col", None),
            P("clip", "col", None),
            P("col"),
            P("col"),
            P(None, "col"),
            P("col"),
            P(None, "col"),
            P("col"),
            P("col"),
            P("col"),
            P(None, "col"),
            P("col"),
            P(None, "col"),
            P("col"),
        ),
        check_vma=False,
    )
```

```python
import functools
import jax
import jax.numpy as jnp
from jax import lax
from jax.experimental import pallas as pl
from jax.experimental.pallas import tpu as pltpu
from jax.sharding import PartitionSpec as P

HEADS = 12
EPSILON = 1e-06
MASKED = -1e30
F32 = jnp.float32
BF16 = jnp.bfloat16
INV_SQRT2 = 0.5**0.5
INV_SQRT_2PI = 0.3989422804014327
MIB = 1 << 20
PACE = 1_500_000
GAIN_ONE, SHIFT_ONE, BIAS_OUT, GAIN_TWO, SHIFT_TWO, BIAS_DOWN, BIAS_Q, BIAS_V, BIAS_UP = range(9)


def dot(left, right):
    return lax.dot_general(left, right, (((1,), (0,)), ((), ())), preferred_element_type=F32)


def dot_nt(left, right):
    return lax.dot_general(left, right, (((1,), (1,)), ((), ())), preferred_element_type=F32)


def add_low(left, right):
    return (left.astype(F32) + right.astype(F32)).astype(BF16)


def in_hbm(array):
    return pltpu.with_memory_space_constraint(array, pltpu.HBM)


def whole(shape):
    return pl.BlockSpec(shape, lambda *_: (0,) * len(shape), pipeline_mode=pl.Buffered(1))


def lanes(rows, size):
    return pl.BlockSpec((rows, size), lambda f, *_: (0, f))


def tokens_of(size, columns):
    return pl.BlockSpec((size, columns), lambda f, *_: (f, 0))


def params(limit, steps=1):
    return pltpu.CompilerParams(
        vmem_limit_bytes=limit * MIB, dimension_semantics=("arbitrary",) * steps
    )


def cost(micros):
    return pl.CostEstimate(flops=0, bytes_accessed=int(micros * PACE), transcendentals=0)


def standardise(value):
    centred = value - jnp.mean(value, axis=1, keepdims=True)
    root = lax.rsqrt(jnp.mean(centred * centred, axis=1, keepdims=True) + EPSILON)
    return centred * root, root


def standardise_back(grad, gain, xhat, root):
    scaled = grad * gain
    first = jnp.mean(scaled, axis=1, keepdims=True)
    second = jnp.mean(scaled * xhat, axis=1, keepdims=True)
    return root * (scaled - first - xhat * second)


def lane_sums(value):
    total = value[:, :128]
    for at in range(128, value.shape[1], 128):
        total = total + value[:, at : at + 128]
    return total


def row_sum(value):
    return jnp.sum(value, axis=0, keepdims=True)


def pair_diagonal(upper, lower):
    zero = jnp.zeros_like(upper)
    return jnp.concatenate(
        [jnp.concatenate([upper, zero], axis=0), jnp.concatenate([zero, lower], axis=0)], axis=1
    )


def token_rows(pieces):
    return jnp.concatenate([piece[0] for piece in pieces], axis=0)


def pairs_and_blocks(size, block, one):
    if size == block:
        for pair in range(HEADS // 2):
            one(pair, 0)
    else:

        @pl.loop(0, HEADS // 2 * (size // block))
        def _(step):
            blocks = size // block
            pair = step // blocks
            one(pair, pl.multiple_of((step - pair * blocks) * block, block))


def attend_kernel(ncol, block, first, info, lens, *refs):
    pieces = refs[:ncol]
    ranks, vecs, w_qkv, w_out = refs[ncol : ncol + 4]
    qkv_t, mixed_t, middle_n, lse, mixed_f, keys_n = refs[-6:]
    size, model = middle_n.shape
    head = model // HEADS
    rows = token_rows(pieces).astype(F32)
    xhat, _ = standardise(rows)
    normed = (xhat * vecs[GAIN_ONE : GAIN_ONE + 1] + vecs[SHIFT_ONE : SHIFT_ONE + 1]).astype(BF16)
    queries = dot(normed, w_qkv[:, :model]) + vecs[BIAS_Q : BIAS_Q + 1]
    qkv_t[:model] = queries.T.astype(BF16) * BF16(head**-0.5)
    keys = dot(normed, w_qkv[:, model : 2 * model])
    keys_n[...] = keys.astype(BF16)
    qkv_t[model : 2 * model] = keys.T.astype(BF16)
    values = dot(normed, w_qkv[:, 2 * model :]) + vecs[BIAS_V : BIAS_V + 1]
    qkv_t[2 * model :] = values.T.astype(BF16)
    bias = jnp.where(ranks[...] < lens[first + pl.program_id(0)], 0.0, MASKED)

    def one(pair, at):
        low, high = pair * 2 * head, (pair * 2 + 1) * head
        where = pl.ds(at, block)
        right = pair_diagonal(qkv_t[pl.ds(low, head), where], qkv_t[pl.ds(high, head), where])
        scores = dot(keys_n[:, pl.ds(low, 2 * head)], right) + bias
        top = jnp.max(scores, axis=0, keepdims=True)
        weight = jnp.exp(scores - top)
        total = jnp.sum(weight, axis=0, keepdims=True)
        probs = (weight * (1.0 / total)).astype(BF16)
        stats = top + jnp.log(total)
        for side, start in enumerate((low, high)):
            cut = slice(side * block, (side + 1) * block)
            lse[0, pl.ds(pair * 2 + side, 1), where] = stats[:, cut]
            value = qkv_t[pl.ds(2 * model + start, head), :]
            mixed_f[pl.ds(start, head), where] = dot(value, probs[:, cut])

    pairs_and_blocks(size, block, one)
    mixed_t[...] = mixed_f[...].astype(BF16)
    middle = rows + dot(mixed_f[...].T.astype(BF16), w_out[...]) + vecs[BIAS_OUT : BIAS_OUT + 1]
    middle_n[...] = middle


def attend_call(info, lens, pieces, ranks, vecs, w_qkv, w_out, first, frames, per, earlier=()):
    ncol = len(pieces)
    width, model = pieces[1].shape[1:]
    size = ncol * width
    tokens = per * size
    block = min(size, 256)
    own = pl.BlockSpec((1, width, model), lambda f, info, *_: (info[0] * per + first + f, 0, 0))
    other = pl.BlockSpec((1, width, model), lambda f, *_: (f, 0, 0))

    def rows_of(columns):
        return pl.BlockSpec((size, columns), lambda f, *_: (first + f, 0))

    def lanes_of(rows):
        return pl.BlockSpec((rows, size), lambda f, *_: (0, first + f))

    return pl.pallas_call(
        functools.partial(attend_kernel, ncol, block, first),
        grid_spec=pltpu.PrefetchScalarGridSpec(
            num_scalar_prefetch=2,
            grid=(frames,),
            in_specs=[own]
            + [other] * (ncol - 1)
            + [whole(ranks.shape), whole(vecs.shape), whole(w_qkv.shape), whole(w_out.shape)]
            + [pl.BlockSpec(memory_space=pl.ANY)] * len(earlier),
            out_specs=[
                lanes_of(3 * model),
                lanes_of(model),
                rows_of(model),
                pl.BlockSpec((1, 16, size), lambda f, *_: (first + f, 0, 0)),
            ],
            scratch_shapes=[
                pltpu.VMEM((model, size), F32),
                pltpu.VMEM((size, model), BF16),
            ],
        ),
        out_shape=[
            pltpu.HBM((3 * model, tokens), BF16),
            pltpu.HBM((model, tokens), BF16),
            pltpu.HBM((tokens, model), F32),
            pltpu.HBM((per, 16, size), F32),
        ],
        input_output_aliases={ncol + 6 + i: i for i in range(len(earlier))},
        compiler_params=params(40),
        cost_estimate=cost(10),
        name="attend",
    )(info, lens, *pieces, ranks, vecs, in_hbm(w_qkv), in_hbm(w_out), *earlier)


def gather_tokens(pieces, target):
    frames, width = pieces[1].shape[:2]
    at = 0
    for f in range(frames):
        for piece in pieces:
            target[at : at + width] = piece[f]
            at += width


def halves_apart(info, value):
    first, chunk = info[1] == 0, value.shape[1] // 2
    low, high = value[:, :chunk], value[:, chunk:]
    return jnp.where(first, low, high), jnp.where(first, high, low)


def mlp_kernel(middle_n, vecs, w_up, w_down, *refs):
    *outs, active_n, slope_n, second_t, second_n, total = refs
    tokens, model = total.shape
    rows = min(tokens, 256)
    step, steps = pl.program_id(0), pl.num_programs(0)
    bias = vecs[pl.ds(BIAS_UP + step, 1), :]

    @pl.when(step == 0)
    def _():
        for at in range(0, tokens, rows):
            cut = slice(at, at + rows)
            middle = middle_n[cut]
            xhat, _ = standardise(middle)
            second = xhat * vecs[GAIN_TWO : GAIN_TWO + 1] + vecs[SHIFT_TWO : SHIFT_TWO + 1]
            second_n[cut] = second.astype(BF16)
            second_t[:, cut] = second.T.astype(BF16)
            total[cut] = middle + vecs[BIAS_DOWN : BIAS_DOWN + 1]

    for at in range(0, tokens, rows):
        cut = slice(at, at + rows)
        hidden = dot(second_n[cut], w_up[...]) + bias
        half = 0.5 + 0.5 * lax.erf(hidden * INV_SQRT2)
        active = (hidden * half).astype(BF16)
        bell = jnp.exp(hidden * hidden * -0.5) * INV_SQRT_2PI
        slope_n[cut] = (half + hidden * bell).astype(BF16)
        active_n[cut] = active
        total[cut] += dot(active, w_down[...])

    @pl.when(step == steps - 1)
    def _():
        frames, width = outs[0].shape[:2]
        at = 0
        for f in range(frames):
            for out in outs:
                out[f] = total[at : at + width].astype(BF16)
                at += width


def mlp_call(piece, ncol, middle_n, vecs, w_up, w_down):
    tokens, model = middle_n.shape
    hidden_size = w_down.shape[0]
    return pl.pallas_call(
        mlp_kernel,
        grid=(hidden_size // model,),
        in_specs=[
            whole(middle_n.shape),
            whole(vecs.shape),
            pl.BlockSpec((model, model), lambda j: (0, j)),
            pl.BlockSpec((model, model), lambda j: (j, 0)),
        ],
        out_specs=[whole(piece)] * ncol + [lanes(tokens, model)] * 2 + [whole((model, tokens))],
        out_shape=[pltpu.HBM(piece, BF16)] * ncol
        + [pltpu.HBM((tokens, hidden_size), BF16)] * 2
        + [pltpu.HBM((model, tokens), BF16)],
        scratch_shapes=[pltpu.VMEM((tokens, model), BF16), pltpu.VMEM((tokens, model), F32)],
        compiler_params=params(48),
        cost_estimate=cost(16),
        name="mlp",
    )(middle_n, vecs, in_hbm(w_up), in_hbm(w_down))


def down_kernel(ncol, info, *refs):
    pieces = refs[:ncol]
    active_n, keep, send, cot_n, cot_t = refs[ncol:]
    model = cot_t.shape[0]
    part = model // 4

    @pl.when(pl.program_id(0) == 0)
    def _():
        gather_tokens(pieces, cot_n)
        cot_t[...] = cot_n[...].astype(F32).T.astype(BF16)

    kept, sent = halves_apart(info, dot(cot_t[...], active_n[...]).astype(BF16))
    for c in range(4):
        keep[c] = kept[c * part : (c + 1) * part]
        send[c] = sent[c * part : (c + 1) * part]


def down_call(info, pieces, active_n):
    ncol = len(pieces)
    piece = pieces[1].shape
    model = piece[2]
    tokens, hidden_size = active_n.shape
    own = pl.BlockSpec(piece, lambda j, info: (info[0], 0, 0), pipeline_mode=pl.Buffered(1))
    out = jax.ShapeDtypeStruct((4, hidden_size // 4, model // 2), BF16)
    return pl.pallas_call(
        functools.partial(down_kernel, ncol),
        grid_spec=pltpu.PrefetchScalarGridSpec(
            num_scalar_prefetch=1,
            grid=(hidden_size // model,),
            in_specs=[own] + [whole(piece)] * (ncol - 1) + [lanes(tokens, model)],
            out_specs=[pl.BlockSpec((4, model // 4, model // 2), lambda j, info: (0, j, 0))] * 2,
            scratch_shapes=[pltpu.VMEM((tokens, model), BF16), pltpu.VMEM((model, tokens), BF16)],
        ),
        out_shape=[out, out],
        compiler_params=params(24),
        cost_estimate=cost(9),
        name="grad_down",
    )(info, *pieces, active_n)


def mlp_back_kernel(ncol, info, *refs):
    pieces = refs[:ncol]
    middle_in, mixed_in, second_in, vecs, slope_n, w_up, w_down = refs[ncol : ncol + 7]
    gmiddle_out, sums, keep_out, send_out = refs[ncol + 7 : ncol + 11]
    cot_n, middle_n, mixed_t, second_t, hidden_n, grad, gmiddle_n, up_slots, out_slots, in_sems, up_sems, out_sems, g_sems = refs[ncol + 11 :]
    tokens, model = grad.shape
    part = model // 4
    rows = min(tokens, 256)
    step, steps = pl.program_id(0), pl.num_programs(0) - 1
    gain = vecs[GAIN_TWO : GAIN_TWO + 1]
    coming = [
        pltpu.make_async_copy(source, target, in_sems.at[i])
        for i, (source, target) in enumerate(((second_in, second_t), (middle_in, middle_n), (mixed_in, mixed_t)))
    ]

    def up_copies(j):
        return [
            pltpu.make_async_copy(up_slots.at[side, j], target.at[j, pl.ds(0, model), :], up_sems.at[side, j])
            for side, target in enumerate((keep_out, send_out))
        ]

    @pl.when(step == 0)
    def _():
        for copy in coming:
            copy.start()
        sums[...] = jnp.zeros_like(sums)
        gather_tokens(pieces, cot_n)
        for at in range(0, tokens, rows):
            grad[at : at + rows] = jnp.zeros((rows, model), F32)

    @pl.when(step < steps)
    def _():
        for at in range(0, tokens, rows):
            cut = slice(at, at + rows)
            low = (dot_nt(cot_n[cut], w_down[...]) * slope_n[cut].astype(F32)).astype(BF16)
            hidden_n[cut] = low
            sums[pl.ds(4 + step, 1), :] += row_sum(low.astype(F32))
            grad[cut] += dot_nt(low, w_up[...])

        @pl.when(step == 0)
        def _():
            coming[0].wait()

        up_slots[0, step], up_slots[1, step] = halves_apart(info, dot(second_t[...], hidden_n[...]).astype(BF16))
        for copy in up_copies(step):
            copy.start()

    @pl.when(step == steps)
    def _():
        coming[1].wait()
        going = []
        for i, at in enumerate(range(0, tokens, rows)):
            cut = slice(at, at + rows)
            xhat, root = standardise(middle_n[cut])
            cot_f32, back = cot_n[cut].astype(F32), grad[cut]
            grad_middle = cot_f32 + standardise_back(back, gain, xhat, root)
            gmiddle_n[cut] = grad_middle
            copy = pltpu.make_async_copy(gmiddle_n.at[pl.ds(at, rows)], gmiddle_out.at[pl.ds(at, rows)], g_sems.at[i])
            copy.start()
            going.append(copy)
            low = grad_middle.astype(BF16)
            hidden_n[cut] = low
            sums[0:1] += row_sum(back * xhat)
            sums[1:2] += row_sum(back)
            sums[2:3] += row_sum(low.astype(F32))
            sums[3:4] += row_sum(cot_f32)
        coming[2].wait()
        both = halves_apart(info, dot(mixed_t[...], hidden_n[...]).T.astype(BF16))
        for side, target in enumerate((keep_out, send_out)):
            for c in range(4):
                out_slots[side, c] = both[side][c * part : (c + 1) * part]
                copy = pltpu.make_async_copy(
                    out_slots.at[side, c], target.at[c, pl.ds(model, part), :], out_sems.at[side, c]
                )
                copy.start()
                going.append(copy)
        for j in range(keep_out.shape[0]):
            going += up_copies(j)
        for copy in going:
            copy.wait()


def mlp_back_call(info, pieces, middle_n, mixed_t, second_t, vecs, slope_n, w_up, w_down):
    ncol = len(pieces)
    piece = pieces[1].shape
    tokens, model = middle_n.shape
    steps = w_down.shape[0] // model
    part, chunk = model // 4, model // 2
    rows = min(tokens, 256)
    own = pl.BlockSpec(piece, lambda j, info: (info[0], 0, 0), pipeline_mode=pl.Buffered(1))
    stream = pl.BlockSpec((tokens, model), lambda j, info: (0, jnp.minimum(j, steps - 1)))
    shape = (steps, model + part, chunk)
    stays = pl.BlockSpec(memory_space=pltpu.HBM)
    return pl.pallas_call(
        functools.partial(mlp_back_kernel, ncol),
        grid_spec=pltpu.PrefetchScalarGridSpec(
            num_scalar_prefetch=1,
            grid=(steps + 1,),
            in_specs=[own]
            + [whole(piece)] * (ncol - 1)
            + [
                stays,
                stays,
                stays,
                whole(vecs.shape),
                stream,
                pl.BlockSpec((model, model), lambda j, info: (0, jnp.minimum(j, steps - 1))),
                pl.BlockSpec((model, model), lambda j, info: (jnp.minimum(j, steps - 1), 0)),
            ],
            out_specs=[stays, whole((16, model)), stays, stays],
            scratch_shapes=[
                pltpu.VMEM((tokens, model), BF16),
                pltpu.VMEM((tokens, model), F32),
                pltpu.VMEM((model, tokens), BF16),
                pltpu.VMEM((model, tokens), BF16),
                pltpu.VMEM((tokens, model), BF16),
                pltpu.VMEM((tokens, model), F32),
                pltpu.VMEM((tokens, model), F32),
                pltpu.VMEM((2, steps, model, chunk), BF16),
                pltpu.VMEM((2, 4, part, chunk), BF16),
                pltpu.SemaphoreType.DMA((3,)),
                pltpu.SemaphoreType.DMA((2, steps)),
                pltpu.SemaphoreType.DMA((2, 4)),
                pltpu.SemaphoreType.DMA((tokens // rows,)),
            ],
        ),
        out_shape=[
            pltpu.HBM((tokens, model), F32),
            jax.ShapeDtypeStruct((16, model), F32),
            pltpu.HBM(shape, BF16),
            pltpu.HBM(shape, BF16),
        ],
        compiler_params=params(56),
        cost_estimate=cost(26),
        name="mlp_back",
    )(info, *pieces, middle_n, mixed_t, second_t, vecs, slope_n, in_hbm(w_up), in_hbm(w_down))


def attend_back_kernel(ncol, block, first, info, lens, *refs):
    pieces = refs[:ncol]
    ranks, vecs, w_qkv, w_out, qkv_t, lse, gmiddle_n = refs[ncol : ncol + 7]
    gproj_t, normed_n, sums = refs[ncol + 7 : ncol + 10]
    outs = refs[ncol + 10 : 2 * ncol + 10]
    gmixed_t, gacc, columns, kv_n = refs[2 * ncol + 10 :]
    size, model = gmiddle_n.shape
    head = model // HEADS
    step = pl.program_id(0)

    @pl.when(step == 0)
    def _():
        sums[...] = jnp.zeros_like(sums)
        columns[...] = jnp.zeros_like(columns)

    gmixed_t[...] = dot_nt(w_out[...], gmiddle_n[...].astype(BF16)).astype(BF16)
    kv_n[...] = qkv_t[model:].astype(F32).T.astype(BF16)
    bias = jnp.where(ranks[...] < lens[first + step], 0.0, MASKED)
    many = size != block
    if many:
        gacc[...] = jnp.zeros_like(gacc)

    def one(pair, at):
        low, high = pair * 2 * head, (pair * 2 + 1) * head
        where = pl.ds(at, block)
        right = pair_diagonal(qkv_t[pl.ds(low, head), where], qkv_t[pl.ds(high, head), where])
        scores = dot(kv_n[:, pl.ds(low, 2 * head)], right) + bias
        stats = jnp.concatenate([lse[0, pl.ds(pair * 2 + i, 1), where] for i in range(2)], axis=1)
        probs = jnp.exp(scores - stats)
        probs_low = probs.astype(BF16)
        right = pair_diagonal(gmixed_t[pl.ds(low, head), where], gmixed_t[pl.ds(high, head), where])
        grad_probs = dot(kv_n[:, pl.ds(model + low, 2 * head)], right)
        inner = jnp.sum(probs * grad_probs, axis=0, keepdims=True)
        grad_scores = (probs * (grad_probs - inner)).astype(BF16)
        for side, start in enumerate((low, high)):
            cut = slice(side * block, (side + 1) * block)
            grad_side = grad_scores[:, cut]
            grad_q = dot(qkv_t[pl.ds(model + start, head), :], grad_side) * head**-0.5
            grad_k = dot_nt(qkv_t[pl.ds(start, head), where], grad_side)
            grad_v = dot_nt(gmixed_t[pl.ds(start, head), where], probs_low[:, cut])
            gproj_t[pl.ds(start, head), where] = grad_q.astype(BF16)
            if many:
                gacc[pl.ds(start, head), :] += grad_k
                gacc[pl.ds(model + start, head), :] += grad_v
            else:
                gproj_t[pl.ds(model + start, head), :] = grad_k.astype(BF16)
                gproj_t[pl.ds(2 * model + start, head), :] = grad_v.astype(BF16)

    pairs_and_blocks(size, block, one)
    if many:
        gproj_t[model:] = gacc[...].astype(BF16)
    columns[:model] += lane_sums(gproj_t[:model].astype(F32))
    columns[model:] += lane_sums(gproj_t[2 * model :].astype(F32))
    grad = dot(w_qkv[...], gproj_t[...]).T
    xhat, root = standardise(token_rows(pieces).astype(F32))
    gain = vecs[GAIN_ONE : GAIN_ONE + 1]
    normed_n[...] = (xhat * gain + vecs[SHIFT_ONE : SHIFT_ONE + 1]).astype(BF16)
    sums[0:1] += row_sum(grad * xhat)
    sums[1:2] += row_sum(grad)
    total = gmiddle_n[...] + standardise_back(grad, gain, xhat, root)
    result = total.astype(BF16)
    width = size // ncol
    for k in range(ncol):
        outs[k][0] = result[k * width : (k + 1) * width]

    @pl.when(step == pl.num_programs(0) - 1)
    def _():
        for i in range(2):
            sums[2 + i : 3 + i] = row_sum(columns[i * model : (i + 1) * model].T)


def attend_back_call(
    info, lens, pieces, ranks, vecs, w_qkv, w_out, qkv_t, lse, gmiddle_n, first, frames, per
):
    ncol = len(pieces)
    width, model = pieces[1].shape[1:]
    size = ncol * width
    tokens = frames * size
    block = min(size, 256)
    acc = (2 * model, size) if size != block else (8, 128)

    def later(spec_lanes, shape):
        if spec_lanes:
            return pl.BlockSpec(shape, lambda f, *_: (0, first + f))
        return pl.BlockSpec(shape, lambda f, *_: (first + f,) + (0,) * (len(shape) - 1))

    piece = pl.BlockSpec((1, width, model), lambda f, *_: (f, 0, 0))
    own = pl.BlockSpec((1, width, model), lambda f, info, *_: (info[0] * per + first + f, 0, 0))
    return pl.pallas_call(
        functools.partial(attend_back_kernel, ncol, block, first),
        grid_spec=pltpu.PrefetchScalarGridSpec(
            num_scalar_prefetch=2,
            grid=(frames,),
            in_specs=[own]
            + [piece] * (ncol - 1)
            + [
                whole(ranks.shape),
                whole(vecs.shape),
                whole(w_qkv.shape),
                whole(w_out.shape),
                later(True, (3 * model, size)),
                later(False, (1, 16, size)),
                later(False, (size, model)),
            ],
            out_specs=[lanes(3 * model, size), tokens_of(size, model), whole((16, model))] + [piece] * ncol,
            scratch_shapes=[
                pltpu.VMEM((model, size), BF16),
                pltpu.VMEM(acc, F32),
                pltpu.VMEM((2 * model, 128), F32),
                pltpu.VMEM((size, 2 * model), BF16),
            ],
        ),
        out_shape=[
            pltpu.HBM((3 * model, tokens), BF16),
            pltpu.HBM((tokens, model), BF16),
            pltpu.HBM((16, model), F32),
        ]
        + [pltpu.HBM((frames, width, model), BF16)] * ncol,
        compiler_params=params(40),
        cost_estimate=cost(15),
        name="attend_back",
    )(info, lens, *pieces, ranks, vecs, w_qkv, w_out, qkv_t, lse, gmiddle_n)


def take_kernel(info, *refs):
    half = len(refs) // 2
    for source, target in zip(refs[:half], refs[half:]):
        target[...] = source[...]


def take_frames(info, array, ncol, group=0, groups=1):
    per = array.shape[0] // ncol // groups
    shape = (per,) + array.shape[1:]
    specs = [
        pl.BlockSpec(shape, lambda i, info, k=k: (lax.bitwise_xor(info[0], k) * groups + group, 0, 0))
        for k in range(1, ncol)
    ]
    return pl.pallas_call(
        take_kernel,
        grid_spec=pltpu.PrefetchScalarGridSpec(
            num_scalar_prefetch=1,
            grid=(1,),
            in_specs=specs,
            out_specs=[pl.BlockSpec(shape, lambda i, *_: (0, 0, 0))] * (ncol - 1),
        ),
        out_shape=[pltpu.HBM(shape, array.dtype)] * (ncol - 1),
        compiler_params=params(8),
        cost_estimate=cost(1),
        name="take_frames",
    )(info, *[array] * (ncol - 1))


def place_kernel(parts, info, *refs):
    out = refs[-1]
    for k in range((len(refs) - 1) // parts):

        @pl.when(pl.program_id(0) == k)
        def _(k=k):
            at = 0
            for part in refs[k * parts : (k + 1) * parts]:
                out[at : at + part.shape[0]] = part[...].astype(out.dtype)
                at += part.shape[0]


def place_frames(info, pieces, dtype):
    ncol, parts = len(pieces), len(pieces[0])
    flat = [p for group in pieces for p in group]
    per = sum(p.shape[0] for p in pieces[0])
    shape = (per,) + flat[0].shape[1:]
    return pl.pallas_call(
        functools.partial(place_kernel, parts),
        grid_spec=pltpu.PrefetchScalarGridSpec(
            num_scalar_prefetch=1,
            grid=(ncol,),
            in_specs=[whole(p.shape) for p in flat],
            out_specs=pl.BlockSpec(shape, lambda k, info: (lax.bitwise_xor(info[0], k), 0, 0)),
        ),
        out_shape=pltpu.HBM((ncol * per,) + shape[1:], dtype),
        compiler_params=params(12),
        cost_estimate=cost(2),
        name="place_frames",
    )(info, *flat)


def pick(array, index, axis):
    return lax.dynamic_index_in_dim(array, index, axis, keepdims=False)


class Comm:
    def __init__(self, mesh):
        self.ncol = mesh.shape["col"]
        self.nclip = mesh.shape["clip"]
        self.nz = self.nclip // 2
        self.me = lax.axis_index("col")
        self.clip = lax.axis_index("clip")
        self.core = lax.rem(self.clip, 2)
        self.z = lax.div(self.clip, 2)

    def col_swap(self, array, distance):
        return lax.ppermute(array, "col", [(i, i ^ distance) for i in range(self.ncol)])

    def core_swap(self, array):
        return lax.ppermute(array, "clip", [(i, i ^ 1) for i in range(self.nclip)])

    def z_move(self, array, pairs):
        moves = [(2 * a + c, 2 * b + c) for a, b in pairs for c in range(2)]
        return lax.ppermute(array, "clip", moves)

    def z_swap(self, array, distance):
        return lax.ppermute(array, "clip", [(i, i ^ (2 * distance)) for i in range(self.nclip)])

    def halve(self, terms, bits):
        nbits = self.ncol.bit_length() - 1
        present = list(range(nbits - 1, -1, -1))
        for bit in bits:
            axis = present.index(bit)
            mine = lax.rem(lax.shift_right_logical(self.me, bit), 2)
            away = [pick(t, 1 - mine, axis) for t in terms]
            total = away[0]
            if len(away) > 1:
                total = add_low(away[0], away[1])
            landed = self.col_swap(total, 1 << bit)
            near = [pick(t, mine, axis) for t in terms]
            if len(near) > 1:
                near = [add_low(near[0], near[1])]
            terms = [near[0], landed]
            present.pop(axis)
        return add_low(terms[0], terms[1])

    def reduce_rows(self, grad):
        rows, depth = grad.shape
        part = rows // self.ncol // 4
        nbits = self.ncol.bit_length() - 1
        split = grad.reshape(self.ncol, 2, 2, part, depth)
        keep = pick(split, self.core, 1)
        landed = self.core_swap(pick(split, 1 - self.core, 1))
        order = list(range(nbits))
        half = nbits // 2
        orders = (order, order[half:] + order[:half])
        done = []
        for side in range(2):
            terms = [
                t[:, side].reshape((2,) * nbits + (part, depth)) for t in (keep, landed)
            ]
            done.append(self.halve(terms, orders[side]))
        total = jnp.concatenate(done, axis=0)
        total = self.sum_line(total)
        other = self.core_swap(total)
        first = self.core == 0
        return jnp.concatenate(
            [jnp.where(first, total, other), jnp.where(first, other, total)], axis=0
        )

    def sum_line(self, total):
        nz = self.nz
        for step in range(nz // 2 - 1):
            total = add_low(total, self.z_move(total, [(step, step + 1), (nz - 1 - step, nz - 2 - step)]))
        low, high = nz // 2 - 1, nz // 2
        total = add_low(total, self.z_move(total, [(low, high), (high, low)]))
        for step in range(nz // 2 - 1, 0, -1):
            landed = self.z_move(total, [(step, step - 1), (nz - 1 - step, nz - step)])
            takes = jnp.logical_or(self.z == step - 1, self.z == nz - step)
            total = jnp.where(takes, landed, total)
        return total


def qkv_kernel(groups, info, *refs):
    gproj, normed, att = refs[:groups], refs[groups : 2 * groups], refs[2 * groups : 3 * groups]
    mlp_sums, keep, send, total, vectors = refs[3 * groups :]
    c = pl.program_id(0)
    model = mlp_sums.shape[1]
    rows = total.shape[0] // 2
    part = model // 4
    acc = None
    for g, n in zip(gproj, normed):
        term = dot(g[...], n[...])
        acc = term if acc is None else acc + term
    total[...] = acc

    for i in range(4):

        @pl.when(c == i)
        def _(i=i):
            att_sums = att[0][...]
            for more in att[1:]:
                att_sums = att_sums + more[...]
            vectors[...] = jnp.zeros_like(vectors)
            vectors[0, 0:4, :part] = mlp_sums[0:4, i * part : (i + 1) * part]
            vectors[0, 4:5, :] = mlp_sums[4 + i : 5 + i]
            vectors[1, 0:2, :part] = att_sums[0:2, i * part : (i + 1) * part]
            start = i % 2 * 2 * part
            vectors[1, 2:3, : 2 * part] = att_sums[2 + i // 2 : 3 + i // 2, start : start + 2 * part]

    for side, target in enumerate((keep, send)):
        which = lax.bitwise_xor(info[1], side)
        target[0, :rows] = total[pl.ds(pl.multiple_of(which * rows, rows), rows), :].astype(BF16)
        target[0, rows:] = vectors[which].astype(BF16)


VECTOR_ROWS = 32


def qkv_call(info, gproj, normed, att_sums, mlp_sums):
    groups = len(gproj)
    model = mlp_sums.shape[1]
    rows = 3 * model // 4
    block = (1, rows // 2 + VECTOR_ROWS, model)
    out = jax.ShapeDtypeStruct((4,) + block[1:], BF16)
    others = (*normed, *att_sums, mlp_sums)
    return pl.pallas_call(
        functools.partial(qkv_kernel, groups),
        grid_spec=pltpu.PrefetchScalarGridSpec(
            num_scalar_prefetch=1,
            grid=(4,),
            in_specs=[pl.BlockSpec((rows, g.shape[1]), lambda c, info: (c, 0)) for g in gproj]
            + [whole(o.shape) for o in others],
            out_specs=[pl.BlockSpec(block, lambda c, info: (c, 0, 0))] * 2,
            scratch_shapes=[pltpu.VMEM((rows, model), F32), pltpu.VMEM((2, VECTOR_ROWS, model), F32)],
        ),
        out_shape=[out, out],
        compiler_params=params(24),
        cost_estimate=cost(6),
        name="grad_qkv",
    )(info, *gproj, *others)


def sum_core_kernel(info, *refs):
    for i in range(4):
        refs[8 + i][...] = add_low(refs[i][...], refs[4 + i][...])


def sum_core(info, keep, landed):
    rows, depth = keep.shape[1] // 2, keep.shape[2]
    block = (1, rows, depth)

    def by_x(i, info, flip, side):
        return (2 * i + lax.bitwise_xor(info[2], flip), side, 0)

    def by_y(i, info, flip, side):
        return (2 * lax.bitwise_xor(info[3], flip) + i, side, 0)

    specs = [
        pl.BlockSpec(block, functools.partial(lambda i, info, fn, flip, side: fn(i, info, flip, side), fn=fn, flip=flip, side=side))
        for side, fn in enumerate((by_x, by_y))
        for flip in (1, 0)
    ]
    out = jax.ShapeDtypeStruct((2, rows, depth), BF16)
    return pl.pallas_call(
        sum_core_kernel,
        grid_spec=pltpu.PrefetchScalarGridSpec(
            num_scalar_prefetch=1,
            grid=(2,),
            in_specs=specs * 2,
            out_specs=[pl.BlockSpec(block, lambda i, info: (i, 0, 0))] * 4,
        ),
        out_shape=[out] * 4,
        compiler_params=params(16),
        cost_estimate=cost(2),
        name="sum_core",
    )(info, *[keep] * 4, *[landed] * 4)


def sum_first_kernel(info, keep_a, land_a, keep_b, land_b, send_a, stay_a, send_b, stay_b):
    for keep, land, send, stay, mine in (
        (keep_a, land_a, send_a, stay_a, info[3]),
        (keep_b, land_b, send_b, stay_b, info[2]),
    ):
        send[...] = add_low(keep[1 - mine], land[1 - mine])
        stay[...] = add_low(keep[mine], land[mine])


def sum_first(info, keep_a, land_a, keep_b, land_b):
    rows, depth = keep_a.shape[1:]
    out = jax.ShapeDtypeStruct((rows, depth), BF16)
    return pl.pallas_call(
        sum_first_kernel,
        grid_spec=pltpu.PrefetchScalarGridSpec(
            num_scalar_prefetch=1,
            grid=(1,),
            in_specs=[whole(keep_a.shape)] * 4,
            out_specs=[whole((rows, depth))] * 4,
        ),
        out_shape=[out] * 4,
        compiler_params=params(16),
        cost_estimate=cost(1),
        name="sum_first",
    )(info, keep_a, land_a, keep_b, land_b)


def sum_second_kernel(info, stay_a, land_a, stay_b, land_b, own, send):
    low, high = add_low(stay_a[...], land_a[...]), add_low(stay_b[...], land_b[...])
    own[...] = jnp.where(info[4] == 0, low, high)
    send[...] = jnp.where(info[4] == 0, high, low)


def sum_second(info, stay_a, land_a, stay_b, land_b):
    shape = stay_a.shape
    return pl.pallas_call(
        sum_second_kernel,
        grid_spec=pltpu.PrefetchScalarGridSpec(
            num_scalar_prefetch=1, grid=(1,), in_specs=[whole(shape)] * 4, out_specs=[whole(shape)] * 2
        ),
        out_shape=[jax.ShapeDtypeStruct(shape, BF16)] * 2,
        compiler_params=params(16),
        cost_estimate=cost(1),
        name="sum_second",
    )(info, stay_a, land_a, stay_b, land_b)


def collect(info, parts, full):
    rows = parts[0].shape[0]
    for i, part in enumerate(parts):
        at = lax.bitwise_xor(info[4], i % 2) * rows
        full[lax.bitwise_xor(info[1], i // 2), pl.ds(pl.multiple_of(at, rows), rows), :] = part[...]


def finish_down_kernel(info, *refs):
    *parts, down_t, full = refs
    collect(info, parts, full)
    chunk, part = full.shape[2], down_t.shape[0]
    for half in range(2):
        for c in range(full.shape[1] // part):
            at = (c * 2 + half) * chunk
            down_t[:, at : at + chunk] = full[half, c * part : (c + 1) * part].astype(F32)


def finish_up_kernel(info, *refs):
    *parts, up, out_t, full = refs
    collect(info, parts, full)
    model, chunk = up.shape[0], full.shape[2]
    for half in range(2):
        cut = slice(half * chunk, (half + 1) * chunk)
        up[:, cut] = full[half, :model].astype(F32)
        out_t[:, cut] = full[half, model:].astype(F32)


def finish_qkv_kernel(info, *refs):
    *parts, qkv_t, gain_one, shift_one, bias_qv, gain_two, shift_two, bias_out, bias_down, bias_up, full = refs
    collect(info, parts, full)
    rows = qkv_t.shape[0] // 2
    for half in range(2):
        qkv_t[half * rows : (half + 1) * rows] = full[half, :rows].astype(F32)
    mlp_rows = full[0, rows : rows + 16].astype(F32)
    att_rows = full[1, rows : rows + 16].astype(F32)
    for source, targets in ((mlp_rows, (gain_two, shift_two, bias_out, bias_down, bias_up)), (att_rows, (gain_one, shift_one, bias_qv))):
        for i, target in enumerate(targets):
            target[...] = source[i, : target.shape[0]]


def finish(kernel, name, info, parts, shapes):
    rows, depth = parts[0].shape
    return pl.pallas_call(
        kernel,
        grid_spec=pltpu.PrefetchScalarGridSpec(
            num_scalar_prefetch=1,
            grid=(1,),
            in_specs=[whole((rows, depth))] * 4,
            out_specs=[whole(s) for s in shapes],
            scratch_shapes=[pltpu.VMEM((2, 2 * rows, depth), BF16)],
        ),
        out_shape=[pltpu.HBM(s, F32) for s in shapes],
        compiler_params=params(24),
        cost_estimate=cost(2),
        name=name,
    )(info, *parts)


def wait_for(values, *others):
    flat, tree = jax.tree.flatten(values)
    held = lax.optimization_barrier((tuple(flat), others))[0]
    return jax.tree.unflatten(tree, held)


def join(*values):
    flat, tree = jax.tree.flatten(values)
    return jax.tree.unflatten(tree, lax.optimization_barrier(tuple(flat)))


def make(mesh):
    def on_device(
        frames,
        cotangent,
        frame_len,
        column_rank,
        gain_one,
        shift_one,
        w_qkv,
        bias_qv,
        w_out,
        bias_out,
        gain_two,
        shift_two,
        w_up,
        bias_up,
        w_down,
        bias_down,
    ):
        comm = Comm(mesh)
        ncol, me = comm.ncol, comm.me
        count, width, model = frames.shape
        hidden_size = w_down.shape[0]
        per = count // ncol
        size = ncol * width
        groups = 2 if per % 2 == 0 else 1
        part = per // groups
        middle_z = jnp.logical_or(comm.z == 1, comm.z == 2)
        info = jnp.stack([me, comm.core, lax.rem(me, 2), lax.div(me, 2), middle_z.astype(me.dtype)]).astype(jnp.int32)
        order = lax.bitwise_xor(me, jnp.arange(ncol, dtype=jnp.int32))
        ranks = column_rank.reshape(ncol, width)[order].reshape(size, 1)
        lens = pick(frame_len.reshape(ncol, per), me, 0)
        given = [gain_one, shift_one, bias_out, gain_two, shift_two, bias_down, bias_qv, bias_up]
        total, at, vecs = sum(v.size for v in given), 0, 0.0
        for v in given:
            vecs = vecs + jnp.pad(v.astype(F32), (at, total - at - v.size))
            at += v.size
        vecs = vecs.reshape(-1, model)

        def swap(pieces):
            return [comm.col_swap(p, k + 1) for k, p in enumerate(pieces)]

        sends = [take_frames(info, frames, ncol, g, groups) for g in range(groups)]
        sends.append(take_frames(info, cotangent, ncol))
        landed = swap(sends[0])
        landed, sends, ranks, vecs, lens = join(landed, sends, ranks, vecs, lens)
        rows, kept = [], ()
        for g in range(groups):
            rows.append([frames] + landed)
            landed = swap(sends[g + 1])
            kept = attend_call(info, lens, rows[g], ranks, vecs, w_qkv, w_out, g * part, part, per, kept)
            if g + 1 < groups:
                kept, landed, sends = join(kept, landed, sends)
        qkv_t, mixed_t, middle_n, lse = kept
        *outs, active_n, slope_n, second_t = mlp_call((per, width, model), ncol, middle_n, vecs, w_up, w_down)
        landed, outs, active_n, slope_n, second_t = join(landed, outs, active_n, slope_n, second_t)
        cots = [cotangent] + landed
        out_land = swap(outs[1:])
        down_outs = down_call(info, cots, active_n)
        out_land[0], down_outs, slope_n = join(out_land[0], down_outs, slope_n)
        down_keep, down_send = down_outs
        down_land = comm.core_swap(down_send)
        back_outs = mlp_back_call(info, cots, middle_n, mixed_t, second_t, vecs, slope_n, w_up, w_down)
        out_land, down_land, back_outs = join(out_land, down_land, back_outs)
        gmiddle_n, mlp_sums, up_keep, up_send = back_outs

        def back(gmiddle_n, g):
            return attend_back_call(
                info, lens, rows[g], ranks, vecs, w_qkv, w_out, qkv_t, lse, gmiddle_n, g * part, part, per
            )

        if ncol != 4 or comm.nz != 4:
            gproj_t, normed, att_sums, gouts = [], [], 0.0, []
            for g in range(groups):
                gp, nm, sums, *go = back(gmiddle_n, g)
                gproj_t.append(gp)
                normed.append(nm)
                att_sums = att_sums + sums
                gouts.append([go[0]] + swap(go[1:]))
            output = place_frames(info, [[outs[0]]] + [[p] for p in out_land], BF16)
            grad_input = place_frames(info, [list(p) for p in zip(*gouts)], F32)
            first = comm.core == 0
            steps, part = hidden_size // model, model // 4

            def halves(keep, send):
                return jnp.stack([jnp.where(first, keep, send), jnp.where(first, send, keep)])

            def reduced(grad):
                return comm.reduce_rows(grad.astype(BF16)).astype(F32).T

            grad = halves(up_keep, up_send)
            grad_w_up = reduced(grad[:, :, :model].transpose(1, 0, 3, 2).reshape(hidden_size, model))
            grad_w_out = reduced(grad[:, :, model:].transpose(1, 2, 0, 3).reshape(model, model))
            grad = halves(down_keep, down_send).reshape(2, 4, steps, part, model // 2).transpose(1, 3, 2, 0, 4)
            grad_w_down = reduced(grad.reshape(model, hidden_size))
            grad_w_qkv = reduced(dot(jnp.concatenate(gproj_t, axis=1), jnp.concatenate(normed)))
            sums = jnp.concatenate([mlp_sums, att_sums])
            sums = reduced(jnp.concatenate([sums] * ncol)).T

            def own(row, rows=1):
                return pick(sums[row : row + rows].reshape(ncol, -1), me, 0)

            return (
                output, grad_input, own(16), own(17), grad_w_qkv, own(18, 2), grad_w_out, own(2), own(0), own(1),
                grad_w_up, own(4, steps), grad_w_down, own(3),
            )

        class Chunk:
            def core(self, keep, land):
                sa, self.ka, sb, self.kb = sum_core(info, keep, land)
                self.land = [comm.col_swap(sa, 1), comm.col_swap(sb, 2)]

            def first(self):
                sa, self.ka, sb, self.kb = sum_first(info, self.ka, self.land[0], self.kb, self.land[1])
                self.land = [comm.col_swap(sa, 2), comm.col_swap(sb, 1)]

            def second(self):
                self.own, send = sum_second(info, self.ka, self.land[0], self.kb, self.land[1])
                self.land = comm.z_swap(send, 1)

            def inner(self):
                self.own = add_low(self.own, self.land)
                self.land = comm.z_swap(self.own, 3)

            def outer(self):
                self.own = add_low(self.own, self.land)
                self.land = [comm.z_swap(self.own, 1), comm.core_swap(self.own)]

            def swap(self):
                self.parts = [self.own] + self.land
                self.land = comm.core_swap(self.parts[1])

            def last(self, kernel, name, shapes):
                return finish(kernel, name, info, self.parts + [self.land], shapes)

        down, up, qkv = Chunk(), Chunk(), Chunk()
        down.core(down_keep, down_land)
        up_land = comm.core_swap(up_send)
        results = back(wait_for(gmiddle_n, down.ka), 0)
        down.land, up_land, results = join(down.land, up_land, results)
        gproj_a, normed_a, att_sums_a, *gouts_a = results

        down.first()
        up.core(up_keep, wait_for(up_land, down.ka))
        results = back(wait_for(gmiddle_n, up.ka), 1)
        gproj_b, normed_b, att_sums_b, *gouts_b = results
        results_q = qkv_call(info, (gproj_a, gproj_b), (normed_a, normed_b), (att_sums_a, att_sums_b), mlp_sums)
        down.land, up.land, gouts_b, results_q = join(down.land, up.land, gouts_b, results_q)
        qkv_keep, qkv_send = results_q

        qkv_land = comm.core_swap(qkv_send)
        up.first()
        down.second()
        qkv_land, up.land, down.land, down.own = join(qkv_land, up.land, down.land, down.own)

        qkv.core(qkv_keep, qkv_land)
        down.inner()
        up.second()
        output = place_frames(info, [[outs[0]]] + [[p] for p in out_land], BF16)
        qkv.land, down.land, up.land, output, down.own, up.own = join(
            qkv.land, down.land, up.land, output, down.own, up.own
        )

        qkv.first()
        up.inner()
        down.outer()
        qkv.land, down.land, down.own, up.own, gouts_a, gouts_b = join(
            qkv.land, down.land, down.own, up.own, gouts_a, gouts_b
        )

        qkv.second()
        gin_a, gin_b = swap(gouts_a[1:]), swap(gouts_b[1:])
        down.swap()
        qkv.land, down.land, up.land, qkv.own, down.parts = join(qkv.land, down.land, up.land, qkv.own, down.parts)

        qkv.inner()
        up.outer()
        (grad_w_down,) = down.last(finish_down_kernel, "finish_down", [(model // 4, hidden_size)])
        qkv.land, up.land, qkv.own, up.own, gin_a, gin_b, grad_w_down = join(
            qkv.land, up.land, qkv.own, up.own, gin_a, gin_b, grad_w_down
        )

        qkv.outer()
        up.swap()
        grad_input = place_frames(
            info, [[gouts_a[0], gouts_b[0]]] + [[a, b] for a, b in zip(gin_a, gin_b)], F32
        )
        qkv.land, up.land, up.parts, qkv.own, grad_input = join(qkv.land, up.land, up.parts, qkv.own, grad_input)

        qkv.swap()
        grad_w_up, grad_w_out = up.last(
            finish_up_kernel, "finish_up", [(model, hidden_size // 4), (model // 4, model)]
        )
        qkv.land, qkv.parts, grad_w_up = join(qkv.land, qkv.parts, grad_w_up)
        part = model // 4
        vectors = [(part,), (part,), (2 * part,), (part,), (part,), (part,), (part,), (hidden_size // 4,)]
        grad_w_qkv, g_gain_one, g_shift_one, g_bias_qv, g_gain_two, g_shift_two, g_bias_out, g_bias_down, g_bias_up = qkv.last(
            finish_qkv_kernel, "finish_qkv", [(3 * model // 4, model)] + vectors
        )
        grad_w_qkv, grad_w_out, grad_w_down = grad_w_qkv.T, grad_w_out.T, grad_w_down.T
        return (
            output,
            grad_input,
            g_gain_one,
            g_shift_one,
            grad_w_qkv,
            g_bias_qv,
            grad_w_out,
            g_bias_out,
            g_gain_two,
            g_shift_two,
            grad_w_up,
            g_bias_up,
            grad_w_down,
            g_bias_down,
        )

    return on_device


def solution(mesh):
    return jax.shard_map(
        make(mesh),
        mesh=mesh,
        in_specs=(P("clip", "col", None), P("clip", "col", None), P("clip")) + (P(),) * 13,
        out_specs=(
            P("clip", "col", None),
            P("clip", "col", None),
            P("col"),
            P("col"),
            P(None, "col"),
            P("col"),
            P(None, "col"),
            P("col"),
            P("col"),
            P("col"),
            P(None, "col"),
            P("col"),
            P(None, "col"),
            P("col"),
        ),
        check_vma=False,
    )
```

```python
import functools
import jax
import jax.numpy as jnp
from jax import lax
from jax.experimental import pallas as pl
from jax.experimental.pallas import tpu as pltpu
from jax.sharding import PartitionSpec as P

HEADS = 12
EPSILON = 1e-06
MASKED = -1e30
F32 = jnp.float32
BF16 = jnp.bfloat16
INV_SQRT2 = 0.5**0.5
INV_SQRT_2PI = 0.3989422804014327
MIB = 1 << 20
PACE = 1_500_000
GAIN_ONE, SHIFT_ONE, BIAS_OUT, GAIN_TWO, SHIFT_TWO, BIAS_DOWN, BIAS_Q, BIAS_V, BIAS_UP = range(9)


def dot(left, right):
    return lax.dot_general(left, right, (((1,), (0,)), ((), ())), preferred_element_type=F32)


def dot_nt(left, right):
    return lax.dot_general(left, right, (((1,), (1,)), ((), ())), preferred_element_type=F32)


def add_low(left, right):
    return (left.astype(F32) + right.astype(F32)).astype(BF16)


def in_hbm(array):
    return pltpu.with_memory_space_constraint(array, pltpu.HBM)


def whole(shape):
    return pl.BlockSpec(shape, lambda *_: (0,) * len(shape), pipeline_mode=pl.Buffered(1))


def lanes(rows, size):
    return pl.BlockSpec((rows, size), lambda f, *_: (0, f))


def tokens_of(size, columns):
    return pl.BlockSpec((size, columns), lambda f, *_: (f, 0))


def params(limit, steps=1):
    return pltpu.CompilerParams(
        vmem_limit_bytes=limit * MIB, dimension_semantics=("arbitrary",) * steps
    )


def cost(micros):
    return pl.CostEstimate(flops=0, bytes_accessed=int(micros * PACE), transcendentals=0)


def standardise(value):
    centred = value - jnp.mean(value, axis=1, keepdims=True)
    root = lax.rsqrt(jnp.mean(centred * centred, axis=1, keepdims=True) + EPSILON)
    return centred * root, root


def standardise_back(grad, gain, xhat, root):
    scaled = grad * gain
    first = jnp.mean(scaled, axis=1, keepdims=True)
    second = jnp.mean(scaled * xhat, axis=1, keepdims=True)
    return root * (scaled - first - xhat * second)


def lane_sums(value):
    total = value[:, :128]
    for at in range(128, value.shape[1], 128):
        total = total + value[:, at : at + 128]
    return total


def row_sum(value):
    return jnp.sum(value, axis=0, keepdims=True)


def pair_diagonal(upper, lower):
    zero = jnp.zeros_like(upper)
    return jnp.concatenate(
        [jnp.concatenate([upper, zero], axis=0), jnp.concatenate([zero, lower], axis=0)], axis=1
    )


def token_rows(pieces):
    return jnp.concatenate([piece[0] for piece in pieces], axis=0)


def pairs_and_blocks(size, block, stages):
    if size == block:
        for stage in stages:
            for pair in range(HEADS // 2):
                stage(pair, 0, pair)
    else:

        @pl.loop(0, HEADS // 2 * (size // block))
        def _(step):
            blocks = size // block
            pair = step // blocks
            for stage in stages:
                stage(pair, pl.multiple_of((step - pair * blocks) * block, block), 0)


def slots(size, block):
    return HEADS // 2 if size == block else 1


def mask_lanes(ranks, length, target):
    target[...] = jnp.broadcast_to(jnp.where(ranks[...] < length, 0.0, MASKED), target.shape)


def across(value, width):
    return jnp.concatenate([value] * (width // value.shape[1]), axis=1)


def _(step):
            blocks = size // block
            pair = step // blocks
            one(pair, pl.multiple_of((step - pair * blocks) * block, block))


def attend_kernel(ncol, block, first, info, lens, *refs):
    pieces = refs[:ncol]
    ranks, vecs, w_qkv, w_out = refs[ncol : ncol + 4]
    qkv_t, mixed_t, middle_n, lse, mixed_f, keys_n, mask, scores, probs, inverse = refs[-10:]
    size, model = middle_n.shape
    head = model // HEADS
    rows = token_rows(pieces).astype(F32)
    xhat, _ = standardise(rows)
    normed = (xhat * vecs[GAIN_ONE : GAIN_ONE + 1] + vecs[SHIFT_ONE : SHIFT_ONE + 1]).astype(BF16)
    queries = dot(normed, w_qkv[:, :model]) + vecs[BIAS_Q : BIAS_Q + 1]
    qkv_t[:model] = queries.T.astype(BF16) * BF16(head**-0.5)
    keys = dot(normed, w_qkv[:, model : 2 * model])
    keys_n[...] = keys.astype(BF16)
    qkv_t[model : 2 * model] = keys.T.astype(BF16)
    values = dot(normed, w_qkv[:, 2 * model :]) + vecs[BIAS_V : BIAS_V + 1]
    qkv_t[2 * model :] = values.T.astype(BF16)
    mask_lanes(ranks, lens[first + pl.program_id(0)], mask)

    def begin(pair, at, slot):
        low, high = pair * 2 * head, (pair * 2 + 1) * head
        where = pl.ds(at, block)
        right = pair_diagonal(qkv_t[pl.ds(low, head), where], qkv_t[pl.ds(high, head), where])
        scores[slot] = dot(keys_n[:, pl.ds(low, 2 * head)], right)

    def weigh(pair, at, slot):
        value = scores[slot] + across(mask[...], 2 * block)
        top = jnp.max(value, axis=0, keepdims=True)
        weight = jnp.exp(value - top)
        total = jnp.sum(weight, axis=0, keepdims=True)
        probs[slot] = weight.astype(BF16)
        inverse[slot] = 1.0 / total
        stats = top + jnp.log(total)
        for side in range(2):
            lse[0, pl.ds(pair * 2 + side, 1), pl.ds(at, block)] = stats[:, side * block : (side + 1) * block]

    def mix(pair, at, slot):
        for side in range(2):
            start, cut = (pair * 2 + side) * head, slice(side * block, (side + 1) * block)
            value = qkv_t[pl.ds(2 * model + start, head), :]
            mixed_f[pl.ds(start, head), pl.ds(at, block)] = dot(value, probs[slot, :, cut]) * inverse[slot, :, cut]

    pairs_and_blocks(size, block, (begin, weigh, mix))
    mixed_t[...] = mixed_f[...].astype(BF16)
    middle = rows + dot(mixed_f[...].T.astype(BF16), w_out[...]) + vecs[BIAS_OUT : BIAS_OUT + 1]
    middle_n[...] = middle


def attend_call(info, lens, pieces, ranks, vecs, w_qkv, w_out, first, frames, per, earlier=()):
    ncol = len(pieces)
    width, model = pieces[1].shape[1:]
    size = ncol * width
    tokens = per * size
    block = min(size, 256)
    own = pl.BlockSpec((1, width, model), lambda f, info, *_: (info[0] * per + first + f, 0, 0))
    other = pl.BlockSpec((1, width, model), lambda f, *_: (f, 0, 0))

    def rows_of(columns):
        return pl.BlockSpec((size, columns), lambda f, *_: (first + f, 0))

    def lanes_of(rows):
        return pl.BlockSpec((rows, size), lambda f, *_: (0, first + f))

    return pl.pallas_call(
        functools.partial(attend_kernel, ncol, block, first),
        grid_spec=pltpu.PrefetchScalarGridSpec(
            num_scalar_prefetch=2,
            grid=(frames,),
            in_specs=[own]
            + [other] * (ncol - 1)
            + [whole(ranks.shape), whole(vecs.shape), whole(w_qkv.shape), whole(w_out.shape)]
            + [pl.BlockSpec(memory_space=pl.ANY)] * len(earlier),
            out_specs=[
                lanes_of(3 * model),
                lanes_of(model),
                rows_of(model),
                pl.BlockSpec((1, 16, size), lambda f, *_: (first + f, 0, 0)),
            ],
            scratch_shapes=[
                pltpu.VMEM((model, size), F32),
                pltpu.VMEM((size, model), BF16),
                pltpu.VMEM((size, 128), F32),
                pltpu.VMEM((slots(size, block), size, 2 * block), F32),
                pltpu.VMEM((slots(size, block), size, 2 * block), BF16),
                pltpu.VMEM((slots(size, block), 1, 2 * block), F32),
            ],
        ),
        out_shape=[
            pltpu.HBM((3 * model, tokens), BF16),
            pltpu.HBM((model, tokens), BF16),
            pltpu.HBM((tokens, model), F32),
            pltpu.HBM((per, 16, size), F32),
        ],
        input_output_aliases={ncol + 6 + i: i for i in range(len(earlier))},
        compiler_params=params(40),
        cost_estimate=cost(10),
        name="attend",
    )(info, lens, *pieces, ranks, vecs, in_hbm(w_qkv), in_hbm(w_out), *earlier)


def gather_tokens(pieces, target):
    frames, width = pieces[1].shape[:2]
    at = 0
    for f in range(frames):
        for piece in pieces:
            target[at : at + width] = piece[f]
            at += width


def halves_apart(info, value):
    first, chunk = info[1] == 0, value.shape[1] // 2
    low, high = value[:, :chunk], value[:, chunk:]
    return jnp.where(first, low, high), jnp.where(first, high, low)


def mlp_kernel(ncol, info, *refs):
    own_in, *pieces_in = refs[:ncol]
    middle_n, mixed_in, vecs, w_up, w_down = refs[ncol : ncol + 5]
    outs = refs[ncol + 5 : 2 * ncol + 5]
    gmiddle_out, sums, down_keep, down_send, up_keep, up_send = refs[2 * ncol + 5 : 2 * ncol + 11]
    (
        cot_p, cot_n, cot_t, second_n, second_t, active_n, hidden_n, total, grad, mixed_t, up_slots, down_slots, out_slots,
        in_sems, up_sems, down_sems, out_sems, g_sems,
    ) = refs[2 * ncol + 11 :]
    tokens, model = total.shape
    frames, width = outs[0].shape[:2]
    part = model // 4
    rows = min(tokens, 256)
    step, steps = pl.program_id(0), pl.num_programs(0) - 1
    gain = vecs[GAIN_TWO : GAIN_TWO + 1]
    coming = [
        pltpu.make_async_copy(own_in.at[pl.ds(info[0] * frames, frames)], cot_p.at[0], in_sems.at[0]),
        *[pltpu.make_async_copy(p, cot_p.at[i + 1], in_sems.at[i + 1]) for i, p in enumerate(pieces_in)],
        pltpu.make_async_copy(mixed_in, mixed_t, in_sems.at[ncol]),
    ]

    def down_copy(j):
        target = down_keep if j >= 2 else down_send
        return pltpu.make_async_copy(down_slots.at[j], target.at[:, pl.ds(j % 2 * part, part), :], down_sems.at[j])

    def up_copies(j, block):
        return [
            pltpu.make_async_copy(up_slots.at[side, j], target.at[block, pl.ds(0, model), :], up_sems.at[side, j])
            for side, target in enumerate((up_keep, up_send))
        ]

    @pl.when(step == 0)
    def _():
        for copy in coming:
            copy.start()
        sums[...] = jnp.zeros_like(sums)
        for at in range(0, tokens, rows):
            cut = slice(at, at + rows)
            middle = middle_n[cut]
            xhat, _ = standardise(middle)
            second = xhat * gain + vecs[SHIFT_TWO : SHIFT_TWO + 1]
            second_n[cut] = second.astype(BF16)
            second_t[:, cut] = second.T.astype(BF16)
            total[cut] = middle + vecs[BIAS_DOWN : BIAS_DOWN + 1]
            grad[cut] = jnp.zeros((rows, model), F32)
        for copy in coming[:ncol]:
            copy.wait()
        gather_tokens([cot_p.at[i] for i in range(ncol)], cot_n)
        cot_t[...] = cot_n[...].astype(F32).T.astype(BF16)

    @pl.when(step < steps)
    def _():
        block = block_of(step, info)
        bias = vecs[pl.ds(BIAS_UP + block, 1), :]
        for at in range(0, tokens, rows):
            cut = slice(at, at + rows)
            hidden = dot(second_n[cut], w_up[...]) + bias
            half = 0.5 + 0.5 * lax.erf(hidden * INV_SQRT2)
            active = (hidden * half).astype(BF16)
            bell = jnp.exp(hidden * hidden * -0.5) * INV_SQRT_2PI
            slope = half + hidden * bell
            active_n[cut] = active
            total[cut] += dot(active, w_down[...])
            low = (dot_nt(cot_n[cut], w_down[...]) * slope).astype(BF16)
            hidden_n[cut] = low
            sums[pl.ds(4 + block, 1), :] += row_sum(low.astype(F32))
            grad[cut] += dot_nt(low, w_up[...])
        result = dot(cot_t[...], active_n[...]).astype(BF16)
        for c in range(4):
            down_slots[step, c] = result[c * part : (c + 1) * part]
        up_slots[0, step], up_slots[1, step] = halves_apart(info, dot(second_t[...], hidden_n[...]).astype(BF16))
        for copy in up_copies(step, block):
            copy.start()

    for j in range(4):

        @pl.when(step == j)
        def _(j=j):
            down_copy(j).start()

    @pl.when(step == steps)
    def _():
        at = 0
        for f in range(frames):
            for out in outs:
                out[f] = total[at : at + width].astype(BF16)
                at += width
        going = []
        for i, at in enumerate(range(0, tokens, rows)):
            cut = slice(at, at + rows)
            xhat, root = standardise(middle_n[cut])
            cot_f32, back = cot_n[cut].astype(F32), grad[cut]
            grad_middle = cot_f32 + standardise_back(back, gain, xhat, root)
            total[cut] = grad_middle
            copy = pltpu.make_async_copy(total.at[pl.ds(at, rows)], gmiddle_out.at[pl.ds(at, rows)], g_sems.at[i])
            copy.start()
            going.append(copy)
            low = grad_middle.astype(BF16)
            hidden_n[cut] = low
            sums[0:1] += row_sum(back * xhat)
            sums[1:2] += row_sum(back)
            sums[2:3] += row_sum(low.astype(F32))
            sums[3:4] += row_sum(cot_f32)
        coming[ncol].wait()
        both = halves_apart(info, dot(mixed_t[...], hidden_n[...]).T.astype(BF16))
        for side, target in enumerate((up_keep, up_send)):
            for c in range(4):
                out_slots[side, c] = both[side][c * part : (c + 1) * part]
                copy = pltpu.make_async_copy(out_slots.at[side, c], target.at[c, pl.ds(model, part), :], out_sems.at[side, c])
                copy.start()
                going.append(copy)
        for j in range(4):
            going += [down_copy(j), *up_copies(j, block_of(j, info))]
        for copy in going:
            copy.wait()


def block_of(step, info):
    return lax.bitwise_xor(step // 2, 1 - info[1]) * 2 + step % 2


def mlp_call(info, pieces, middle_n, mixed_t, vecs, w_up, w_down):
    ncol = len(pieces)
    piece = pieces[1].shape
    tokens, model = middle_n.shape
    steps = w_down.shape[0] // model
    part, chunk = model // 4, model // 2
    rows = min(tokens, 256)
    stays = pl.BlockSpec(memory_space=pltpu.HBM)

    def block(j, info):
        return block_of(jnp.minimum(j, steps - 1), info)

    down, up = (4, 2 * part, model), (steps, model + part, chunk)
    return pl.pallas_call(
        functools.partial(mlp_kernel, ncol),
        grid_spec=pltpu.PrefetchScalarGridSpec(
            num_scalar_prefetch=1,
            grid=(steps + 1,),
            in_specs=[stays] * ncol
            + [
                whole(middle_n.shape),
                stays,
                whole(vecs.shape),
                pl.BlockSpec((model, model), lambda j, info: (0, block(j, info))),
                pl.BlockSpec((model, model), lambda j, info: (block(j, info), 0)),
            ],
            out_specs=[whole(piece)] * ncol + [stays, whole((16, model))] + [stays] * 4,
            scratch_shapes=[
                pltpu.VMEM((ncol,) + piece, BF16),
                pltpu.VMEM((tokens, model), BF16),
                pltpu.VMEM((model, tokens), BF16),
                pltpu.VMEM((tokens, model), BF16),
                pltpu.VMEM((model, tokens), BF16),
                pltpu.VMEM((tokens, model), BF16),
                pltpu.VMEM((tokens, model), BF16),
                pltpu.VMEM((tokens, model), F32),
                pltpu.VMEM((tokens, model), F32),
                pltpu.VMEM((model, tokens), BF16),
                pltpu.VMEM((2, steps, model, chunk), BF16),
                pltpu.VMEM((steps, 4, part, model), BF16),
                pltpu.VMEM((2, 4, part, chunk), BF16),
                pltpu.SemaphoreType.DMA((ncol + 1,)),
                pltpu.SemaphoreType.DMA((2, steps)),
                pltpu.SemaphoreType.DMA((steps,)),
                pltpu.SemaphoreType.DMA((2, 4)),
                pltpu.SemaphoreType.DMA((tokens // rows,)),
            ],
        ),
        out_shape=[pltpu.HBM(piece, BF16)] * ncol
        + [pltpu.HBM((tokens, model), F32), jax.ShapeDtypeStruct((16, model), F32)]
        + [pltpu.HBM(s, BF16) for s in (down, down, up, up)],
        compiler_params=params(60),
        cost_estimate=cost(40),
        name="mlp",
    )(info, *[in_hbm(p) for p in pieces], in_hbm(middle_n), in_hbm(mixed_t), vecs, in_hbm(w_up), in_hbm(w_down))


def attend_back_kernel(ncol, block, first, info, lens, *refs):
    pieces = refs[:ncol]
    ranks, vecs, w_qkv_in, w_out, qkv_t, lse, mixed_t, gmiddle_n = refs[ncol : ncol + 8]
    gproj_t, normed_n, sums, *outs = refs[-15 - ncol : -12]
    gmixed_t, gacc, columns, kv_n, mask, scores, gprobs, probs, gscores, inner, w_qkv, sem = refs[-12:]
    size, model = gmiddle_n.shape
    head = model // HEADS
    step = pl.program_id(0)

    coming = pltpu.make_async_copy(w_qkv_in, w_qkv, sem.at[0])

    @pl.when(step == 0)
    def _():
        coming.start()
        sums[...] = jnp.zeros_like(sums)
        columns[...] = jnp.zeros_like(columns)

    gmixed_t[...] = dot_nt(w_out[...], gmiddle_n[...].astype(BF16)).astype(BF16)
    kv_n[...] = qkv_t[model:].astype(F32).T.astype(BF16)
    mask_lanes(ranks, lens[first + step], mask)
    product = gmixed_t[...].astype(F32) * mixed_t[...].astype(F32)
    for h in range(HEADS):
        inner[h : h + 1] = row_sum(product[h * head : (h + 1) * head])
    many = size != block
    if many:
        gacc[...] = jnp.zeros_like(gacc)

    def begin(pair, at, slot):
        low, high = pair * 2 * head, (pair * 2 + 1) * head
        where = pl.ds(at, block)
        right = pair_diagonal(qkv_t[pl.ds(low, head), where], qkv_t[pl.ds(high, head), where])
        scores[slot] = dot(kv_n[:, pl.ds(low, 2 * head)], right)
        right = pair_diagonal(gmixed_t[pl.ds(low, head), where], gmixed_t[pl.ds(high, head), where])
        gprobs[slot] = dot(kv_n[:, pl.ds(model + low, 2 * head)], right)

    def weigh(pair, at, slot):
        where = pl.ds(at, block)
        stats, means = (
            jnp.concatenate([rows[pl.ds(pair * 2 + i, 1), where] for i in range(2)], axis=1) for rows in (lse.at[0], inner)
        )
        value = jnp.exp(scores[slot] + across(mask[...], 2 * block) - stats)
        probs[slot] = value.astype(BF16)
        gscores[slot] = (value * (gprobs[slot] - means)).astype(BF16)

    def spread(pair, at, slot):
        where = pl.ds(at, block)
        for side in range(2):
            start, cut = (pair * 2 + side) * head, slice(side * block, (side + 1) * block)
            grad_side = gscores[slot, :, cut]
            grad_q = dot(qkv_t[pl.ds(model + start, head), :], grad_side) * head**-0.5
            grad_k = dot_nt(qkv_t[pl.ds(start, head), where], grad_side)
            grad_v = dot_nt(gmixed_t[pl.ds(start, head), where], probs[slot, :, cut])
            gproj_t[pl.ds(start, head), where] = grad_q.astype(BF16)
            if many:
                gacc[pl.ds(start, head), :] += grad_k
                gacc[pl.ds(model + start, head), :] += grad_v
            else:
                gproj_t[pl.ds(model + start, head), :] = grad_k.astype(BF16)
                gproj_t[pl.ds(2 * model + start, head), :] = grad_v.astype(BF16)

    pairs_and_blocks(size, block, (begin, weigh, spread))
    if many:
        gproj_t[model:] = gacc[...].astype(BF16)
    columns[:model] += lane_sums(gproj_t[:model].astype(F32))
    columns[model:] += lane_sums(gproj_t[2 * model :].astype(F32))

    @pl.when(step == 0)
    def _():
        coming.wait()

    grad = dot(w_qkv[...], gproj_t[...]).T
    xhat, root = standardise(token_rows(pieces).astype(F32))
    gain = vecs[GAIN_ONE : GAIN_ONE + 1]
    normed_n[...] = (xhat * gain + vecs[SHIFT_ONE : SHIFT_ONE + 1]).astype(BF16)
    sums[0:1] += row_sum(grad * xhat)
    sums[1:2] += row_sum(grad)
    total = gmiddle_n[...] + standardise_back(grad, gain, xhat, root)
    result = total.astype(BF16)
    width = size // ncol
    for k in range(ncol):
        outs[k][0] = result[k * width : (k + 1) * width]

    @pl.when(step == pl.num_programs(0) - 1)
    def _():
        for i in range(2):
            sums[2 + i : 3 + i] = row_sum(columns[i * model : (i + 1) * model].T)


def attend_back_call(
    info, lens, pieces, ranks, vecs, w_qkv, w_out, qkv_t, lse, mixed_t, gmiddle_n, first, frames, per, earlier=()
):
    ncol = len(pieces)
    width, model = pieces[1].shape[1:]
    size = ncol * width
    tokens = per * size
    block = min(size, 256)
    acc = (2 * model, size) if size != block else (8, 128)

    def later(spec_lanes, shape):
        if spec_lanes:
            return pl.BlockSpec(shape, lambda f, *_: (0, first + f))
        return pl.BlockSpec(shape, lambda f, *_: (first + f,) + (0,) * (len(shape) - 1))

    own = pl.BlockSpec((1, width, model), lambda f, info, *_: (info[0] * per + first + f, 0, 0))
    piece = later(False, (1, width, model))
    return pl.pallas_call(
        functools.partial(attend_back_kernel, ncol, block, first),
        grid_spec=pltpu.PrefetchScalarGridSpec(
            num_scalar_prefetch=2,
            grid=(frames,),
            in_specs=[own]
            + [piece] * (ncol - 1)
            + [
                whole(ranks.shape),
                whole(vecs.shape),
                pl.BlockSpec(memory_space=pltpu.HBM),
                whole(w_out.shape),
                later(True, (3 * model, size)),
                later(False, (1, 16, size)),
                later(True, (model, size)),
                later(False, (size, model)),
            ]
            + [pl.BlockSpec(memory_space=pl.ANY)] * len(earlier),
            out_specs=[later(True, (3 * model, size)), later(False, (size, model)), whole((16, model))] + [piece] * ncol,
            scratch_shapes=[
                pltpu.VMEM((model, size), BF16),
                pltpu.VMEM(acc, F32),
                pltpu.VMEM((2 * model, 128), F32),
                pltpu.VMEM((size, 2 * model), BF16),
                pltpu.VMEM((size, 128), F32),
                pltpu.VMEM((slots(size, block), size, 2 * block), F32),
                pltpu.VMEM((slots(size, block), size, 2 * block), F32),
                pltpu.VMEM((slots(size, block), size, 2 * block), BF16),
                pltpu.VMEM((slots(size, block), size, 2 * block), BF16),
                pltpu.VMEM((16, size), F32),
                pltpu.VMEM(w_qkv.shape, BF16),
                pltpu.SemaphoreType.DMA((1,)),
            ],
        ),
        out_shape=[
            pltpu.HBM((3 * model, tokens), BF16),
            pltpu.HBM((tokens, model), BF16),
            pltpu.HBM((16, model), F32),
        ]
        + [pltpu.HBM((per, width, model), BF16)] * ncol,
        input_output_aliases={ncol + 10 + i: i + (i > 1) for i in range(len(earlier))},
        compiler_params=params(40 if size == block else 62),
        cost_estimate=cost(15),
        name="attend_back",
    )(info, lens, *pieces, ranks, vecs, in_hbm(w_qkv), in_hbm(w_out), in_hbm(qkv_t), lse, in_hbm(mixed_t), in_hbm(gmiddle_n), *earlier)


def take_kernel(info, *refs):
    half = len(refs) // 2
    for source, target in zip(refs[:half], refs[half:]):
        target[...] = source[...]


def take_frames(info, array, ncol, group=0, groups=1):
    per = array.shape[0] // ncol // groups
    shape = (per,) + array.shape[1:]
    specs = [
        pl.BlockSpec(shape, lambda i, info, k=k: (lax.bitwise_xor(info[0], k) * groups + group, 0, 0))
        for k in range(1, ncol)
    ]
    return pl.pallas_call(
        take_kernel,
        grid_spec=pltpu.PrefetchScalarGridSpec(
            num_scalar_prefetch=1,
            grid=(1,),
            in_specs=specs,
            out_specs=[pl.BlockSpec(shape, lambda i, *_: (0, 0, 0))] * (ncol - 1),
        ),
        out_shape=[pltpu.HBM(shape, array.dtype)] * (ncol - 1),
        compiler_params=params(8),
        cost_estimate=cost(1),
        name="take_frames",
    )(info, *[in_hbm(array)] * (ncol - 1))


def place_kernel(info, *refs):
    *pieces, out = refs
    for k, piece in enumerate(pieces):

        @pl.when(pl.program_id(0) == k)
        def _(piece=piece):
            out[...] = piece[...].astype(out.dtype)


def place_frames(info, pieces, dtype):
    shape = pieces[0].shape
    return pl.pallas_call(
        place_kernel,
        grid_spec=pltpu.PrefetchScalarGridSpec(
            num_scalar_prefetch=1,
            grid=(len(pieces),),
            in_specs=[whole(shape)] * len(pieces),
            out_specs=pl.BlockSpec(shape, lambda k, info: (lax.bitwise_xor(info[0], k), 0, 0)),
        ),
        out_shape=pltpu.HBM((len(pieces) * shape[0],) + shape[1:], dtype),
        compiler_params=params(12),
        cost_estimate=cost(2),
        name="place_frames",
    )(info, *pieces)


def pick(array, index, axis):
    return lax.dynamic_index_in_dim(array, index, axis, keepdims=False)


class Comm:
    def __init__(self, mesh):
        self.ncol = mesh.shape["col"]
        self.nclip = mesh.shape["clip"]
        self.nz = self.nclip // 2
        self.me = lax.axis_index("col")
        self.clip = lax.axis_index("clip")
        self.core = lax.rem(self.clip, 2)
        self.z = lax.div(self.clip, 2)

    def col_swap(self, array, distance):
        return lax.ppermute(array, "col", [(i, i ^ distance) for i in range(self.ncol)])

    def core_swap(self, array):
        return lax.ppermute(array, "clip", [(i, i ^ 1) for i in range(self.nclip)])

    def z_move(self, array, pairs):
        moves = [(2 * a + c, 2 * b + c) for a, b in pairs for c in range(2)]
        return lax.ppermute(array, "clip", moves)

    def z_swap(self, array, distance):
        return lax.ppermute(array, "clip", [(i, i ^ (2 * distance)) for i in range(self.nclip)])

    def halve(self, terms, bits):
        nbits = self.ncol.bit_length() - 1
        present = list(range(nbits - 1, -1, -1))
        for bit in bits:
            axis = present.index(bit)
            mine = lax.rem(lax.shift_right_logical(self.me, bit), 2)
            away = [pick(t, 1 - mine, axis) for t in terms]
            total = away[0]
            if len(away) > 1:
                total = add_low(away[0], away[1])
            landed = self.col_swap(total, 1 << bit)
            near = [pick(t, mine, axis) for t in terms]
            if len(near) > 1:
                near = [add_low(near[0], near[1])]
            terms = [near[0], landed]
            present.pop(axis)
        return add_low(terms[0], terms[1])

    def reduce_rows(self, grad):
        rows, depth = grad.shape
        part = rows // self.ncol // 4
        nbits = self.ncol.bit_length() - 1
        split = grad.reshape(self.ncol, 2, 2, part, depth)
        keep = pick(split, self.core, 1)
        landed = self.core_swap(pick(split, 1 - self.core, 1))
        order = list(range(nbits))
        half = nbits // 2
        orders = (order, order[half:] + order[:half])
        done = []
        for side in range(2):
            terms = [
                t[:, side].reshape((2,) * nbits + (part, depth)) for t in (keep, landed)
            ]
            done.append(self.halve(terms, orders[side]))
        total = jnp.concatenate(done, axis=0)
        total = self.sum_line(total)
        other = self.core_swap(total)
        first = self.core == 0
        return jnp.concatenate(
            [jnp.where(first, total, other), jnp.where(first, other, total)], axis=0
        )

    def sum_line(self, total):
        nz = self.nz
        for step in range(nz // 2 - 1):
            total = add_low(total, self.z_move(total, [(step, step + 1), (nz - 1 - step, nz - 2 - step)]))
        low, high = nz // 2 - 1, nz // 2
        total = add_low(total, self.z_move(total, [(low, high), (high, low)]))
        for step in range(nz // 2 - 1, 0, -1):
            landed = self.z_move(total, [(step, step - 1), (nz - 1 - step, nz - step)])
            takes = jnp.logical_or(self.z == step - 1, self.z == nz - step)
            total = jnp.where(takes, landed, total)
        return total


def qkv_kernel(info, gproj_t, normed_n, mlp_sums, *refs):
    *att, keep, send, total, vectors = refs
    c = pl.program_id(0)
    model = mlp_sums.shape[1]
    rows = total.shape[0] // 2
    part = model // 4
    total[...] = dot(gproj_t[...], normed_n[...])

    for i in range(4):

        @pl.when(c == i)
        def _(i=i):
            att_sums = att[0][...]
            for more in att[1:]:
                att_sums = att_sums + more[...]
            vectors[...] = jnp.zeros_like(vectors)
            vectors[0, 0:4, :part] = mlp_sums[0:4, i * part : (i + 1) * part]
            vectors[0, 4:5, :] = mlp_sums[4 + i : 5 + i]
            vectors[1, 0:2, :part] = att_sums[0:2, i * part : (i + 1) * part]
            start = i % 2 * 2 * part
            vectors[1, 2:3, : 2 * part] = att_sums[2 + i // 2 : 3 + i // 2, start : start + 2 * part]

    for side, target in enumerate((keep, send)):
        which = lax.bitwise_xor(info[1], side)
        target[0, :rows] = total[pl.ds(pl.multiple_of(which * rows, rows), rows), :].astype(BF16)
        target[0, rows:] = vectors[which].astype(BF16)


VECTOR_ROWS = 32


def qkv_call(info, gproj_t, normed_n, mlp_sums, att_sums):
    model = mlp_sums.shape[1]
    rows = 3 * model // 4
    block = (1, rows // 2 + VECTOR_ROWS, model)
    out = jax.ShapeDtypeStruct((4,) + block[1:], BF16)
    others = (normed_n, mlp_sums, *att_sums)
    return pl.pallas_call(
        qkv_kernel,
        grid_spec=pltpu.PrefetchScalarGridSpec(
            num_scalar_prefetch=1,
            grid=(4,),
            in_specs=[pl.BlockSpec((rows, gproj_t.shape[1]), lambda c, info: (c, 0))]
            + [whole(o.shape) for o in others],
            out_specs=[pl.BlockSpec(block, lambda c, info: (c, 0, 0))] * 2,
            scratch_shapes=[pltpu.VMEM((rows, model), F32), pltpu.VMEM((2, VECTOR_ROWS, model), F32)],
        ),
        out_shape=[out, out],
        compiler_params=params(24),
        cost_estimate=cost(6),
        name="grad_qkv",
    )(info, in_hbm(gproj_t), in_hbm(normed_n), *others[1:])


def sum_core_kernel(info, *refs):
    for i in range(4):
        refs[8 + i][...] = add_low(refs[i][...], refs[4 + i][...])


def sum_core(info, keep, landed):
    rows, depth = keep.shape[1] // 2, keep.shape[2]
    block = (1, rows, depth)

    def by_x(i, info, flip, side):
        return (2 * i + lax.bitwise_xor(info[2], flip), side, 0)

    def by_y(i, info, flip, side):
        return (2 * lax.bitwise_xor(info[3], flip) + i, side, 0)

    specs = [
        pl.BlockSpec(block, functools.partial(lambda i, info, fn, flip, side: fn(i, info, flip, side), fn=fn, flip=flip, side=side))
        for side, fn in enumerate((by_x, by_y))
        for flip in (1, 0)
    ]
    out = jax.ShapeDtypeStruct((2, rows, depth), BF16)
    return pl.pallas_call(
        sum_core_kernel,
        grid_spec=pltpu.PrefetchScalarGridSpec(
            num_scalar_prefetch=1,
            grid=(2,),
            in_specs=specs * 2,
            out_specs=[pl.BlockSpec(block, lambda i, info: (i, 0, 0))] * 4,
        ),
        out_shape=[out] * 4,
        compiler_params=params(16),
        cost_estimate=cost(2),
        name="sum_core",
    )(info, *[keep] * 4, *[landed] * 4)


def sum_first_kernel(info, keep_a, land_a, keep_b, land_b, send_a, stay_a, send_b, stay_b):
    for keep, land, send, stay, mine in (
        (keep_a, land_a, send_a, stay_a, info[3]),
        (keep_b, land_b, send_b, stay_b, info[2]),
    ):
        send[...] = add_low(keep[1 - mine], land[1 - mine])
        stay[...] = add_low(keep[mine], land[mine])


def sum_first(info, keep_a, land_a, keep_b, land_b):
    rows, depth = keep_a.shape[1:]
    out = jax.ShapeDtypeStruct((rows, depth), BF16)
    return pl.pallas_call(
        sum_first_kernel,
        grid_spec=pltpu.PrefetchScalarGridSpec(
            num_scalar_prefetch=1,
            grid=(1,),
            in_specs=[whole(keep_a.shape)] * 4,
            out_specs=[whole((rows, depth))] * 4,
        ),
        out_shape=[out] * 4,
        compiler_params=params(16),
        cost_estimate=cost(1),
        name="sum_first",
    )(info, keep_a, land_a, keep_b, land_b)


def sum_second_kernel(info, stay_a, land_a, stay_b, land_b, own, send):
    low, high = add_low(stay_a[...], land_a[...]), add_low(stay_b[...], land_b[...])
    own[...] = jnp.where(info[4] == 0, low, high)
    send[...] = jnp.where(info[4] == 0, high, low)


def sum_second(info, stay_a, land_a, stay_b, land_b):
    shape = stay_a.shape
    return pl.pallas_call(
        sum_second_kernel,
        grid_spec=pltpu.PrefetchScalarGridSpec(
            num_scalar_prefetch=1, grid=(1,), in_specs=[whole(shape)] * 4, out_specs=[whole(shape)] * 2
        ),
        out_shape=[jax.ShapeDtypeStruct(shape, BF16)] * 2,
        compiler_params=params(16),
        cost_estimate=cost(1),
        name="sum_second",
    )(info, stay_a, land_a, stay_b, land_b)


def collect(info, parts, full):
    rows = parts[0].shape[0]
    for i, part in enumerate(parts):
        at = lax.bitwise_xor(info[4], i % 2) * rows
        full[lax.bitwise_xor(info[1], i // 2), pl.ds(pl.multiple_of(at, rows), rows), :] = part[...]


def finish_down_kernel(info, *refs):
    *parts, down_t, full = refs
    collect(info, parts, full)
    model, part = full.shape[2], down_t.shape[0]
    blocks = full.shape[1] // part
    for half in range(2):
        for j in range(blocks):
            at = (half * blocks + j) * model
            down_t[:, at : at + model] = full[half, j * part : (j + 1) * part].astype(F32)


def finish_up_kernel(info, *refs):
    *parts, up, out_t, full = refs
    collect(info, parts, full)
    model, chunk = up.shape[0], full.shape[2]
    for half in range(2):
        cut = slice(half * chunk, (half + 1) * chunk)
        up[:, cut] = full[half, :model].astype(F32)
        out_t[:, cut] = full[half, model:].astype(F32)


def finish_qkv_kernel(info, *refs):
    *parts, qkv_t, gain_one, shift_one, bias_qv, gain_two, shift_two, bias_out, bias_down, bias_up, full = refs
    collect(info, parts, full)
    rows = qkv_t.shape[0] // 2
    for half in range(2):
        qkv_t[half * rows : (half + 1) * rows] = full[half, :rows].astype(F32)
    mlp_rows = full[0, rows : rows + 16].astype(F32)
    att_rows = full[1, rows : rows + 16].astype(F32)
    for source, targets in ((mlp_rows, (gain_two, shift_two, bias_out, bias_down, bias_up)), (att_rows, (gain_one, shift_one, bias_qv))):
        for i, target in enumerate(targets):
            target[...] = source[i, : target.shape[0]]


def finish(kernel, name, info, parts, shapes):
    rows, depth = parts[0].shape
    return pl.pallas_call(
        kernel,
        grid_spec=pltpu.PrefetchScalarGridSpec(
            num_scalar_prefetch=1,
            grid=(1,),
            in_specs=[whole((rows, depth))] * 4,
            out_specs=[whole(s) for s in shapes],
            scratch_shapes=[pltpu.VMEM((2, 2 * rows, depth), BF16)],
        ),
        out_shape=[pltpu.HBM(s, F32) for s in shapes],
        compiler_params=params(24),
        cost_estimate=cost(2),
        name=name,
    )(info, *parts)


def wait_for(values, *others):
    flat, tree = jax.tree.flatten(values)
    held = lax.optimization_barrier((tuple(flat), others))[0]
    return jax.tree.unflatten(tree, held)


def join(*values):
    flat, tree = jax.tree.flatten(values)
    return jax.tree.unflatten(tree, lax.optimization_barrier(tuple(flat)))


def make(mesh):
    def on_device(
        frames,
        cotangent,
        frame_len,
        column_rank,
        gain_one,
        shift_one,
        w_qkv,
        bias_qv,
        w_out,
        bias_out,
        gain_two,
        shift_two,
        w_up,
        bias_up,
        w_down,
        bias_down,
    ):
        comm = Comm(mesh)
        ncol, me = comm.ncol, comm.me
        count, width, model = frames.shape
        hidden_size = w_down.shape[0]
        per = count // ncol
        size = ncol * width
        groups = 2 if per % 2 == 0 else 1
        part = per // groups
        middle_z = jnp.logical_or(comm.z == 1, comm.z == 2)
        info = jnp.stack([me, comm.core, lax.rem(me, 2), lax.div(me, 2), middle_z.astype(me.dtype)]).astype(jnp.int32)
        order = lax.bitwise_xor(me, jnp.arange(ncol, dtype=jnp.int32))
        ranks = column_rank.reshape(ncol, width)[order].reshape(size, 1)
        lens = pick(frame_len.reshape(ncol, per), me, 0)
        given = [gain_one, shift_one, bias_out, gain_two, shift_two, bias_down, bias_qv, bias_up]
        total, at, vecs = sum(v.size for v in given), 0, 0.0
        for v in given:
            vecs = vecs + jnp.pad(v.astype(F32), (at, total - at - v.size))
            at += v.size
        vecs = vecs.reshape(-1, model)

        def swap(pieces):
            return [comm.col_swap(p, k + 1) for k, p in enumerate(pieces)]

        paired = ncol == 4 and comm.nz == 4

        class Chunk:
            land = ()

            def core(self, keep, land):
                sa, self.ka, sb, self.kb = sum_core(info, keep, land)
                self.land = [comm.col_swap(sa, 1), comm.col_swap(sb, 2)]

            def first(self):
                sa, self.ka, sb, self.kb = sum_first(info, self.ka, self.land[0], self.kb, self.land[1])
                self.land = [comm.col_swap(sa, 2), comm.col_swap(sb, 1)]

            def second(self):
                self.own, send = sum_second(info, self.ka, self.land[0], self.kb, self.land[1])
                self.land = comm.z_swap(send, 1)

            def inner(self):
                self.own = add_low(self.own, self.land)
                self.land = comm.z_swap(self.own, 3)

            def outer(self):
                self.own = add_low(self.own, self.land)
                self.land = [comm.z_swap(self.own, 1), comm.core_swap(self.own)]

            def swap(self):
                self.parts = [self.own] + self.land
                self.land = comm.core_swap(self.parts[1])

            def last(self, kernel, name, shapes):
                return finish(kernel, name, info, self.parts + [self.land], shapes)

        landed = swap(take_frames(info, frames, ncol))
        cot_send = take_frames(info, cotangent, ncol)
        landed[0], cot_send, ranks, vecs, lens = join(landed[0], cot_send, ranks, vecs, lens)
        cot_land = swap(cot_send)
        rows = [frames, *join(*landed)]
        kept = attend_call(info, lens, rows, ranks, vecs, w_qkv, w_out, 0, per, per)
        kept, landed = join(kept, cot_land)
        qkv_t, mixed_t, middle_n, lse = kept
        cots = [cotangent, *landed]
        results = mlp_call(info, cots, middle_n, mixed_t, vecs, w_up, w_down)
        *outs, gmiddle_n, mlp_sums, down_keep, down_send, up_keep, up_send = join(*results)

        def back(gmiddle_n, g, earlier=()):
            return attend_back_call(
                info, lens, rows, ranks, vecs, w_qkv, w_out, qkv_t, lse, mixed_t, gmiddle_n, g * part, part, per, earlier
            )

        if not paired:
            out_land = swap(outs[1:])
            att_sums, earlier = 0.0, ()
            for g in range(groups):
                gproj_t, normed, sums, *gouts = back(gmiddle_n, g, earlier)
                att_sums, earlier = att_sums + sums, (gproj_t, normed, *gouts)
            output = place_frames(info, [outs[0]] + out_land, BF16)
            grad_input = place_frames(info, [gouts[0]] + swap(gouts[1:]), F32)
            first = comm.core == 0
            steps, part = hidden_size // model, model // 4

            def halves(keep, send):
                return jnp.stack([jnp.where(first, keep, send), jnp.where(first, send, keep)])

            def reduced(grad):
                return comm.reduce_rows(grad.astype(BF16)).astype(F32).T

            grad = halves(up_keep, up_send)
            grad_w_up = reduced(grad[:, :, :model].transpose(1, 0, 3, 2).reshape(hidden_size, model))
            grad_w_out = reduced(grad[:, :, model:].transpose(1, 2, 0, 3).reshape(model, model))
            grad = halves(down_keep, down_send).reshape(2, 4, steps // 2, part, model).transpose(1, 3, 0, 2, 4)
            grad_w_down = reduced(grad.reshape(model, hidden_size))
            grad_w_qkv = reduced(dot(gproj_t, normed))
            sums = jnp.concatenate([mlp_sums, att_sums])
            sums = reduced(jnp.concatenate([sums] * ncol)).T

            def own(row, rows=1):
                return pick(sums[row : row + rows].reshape(ncol, -1), me, 0)

            return (
                output, grad_input, own(16), own(17), grad_w_qkv, own(18, 2), grad_w_out, own(2), own(0), own(1),
                grad_w_up, own(4, steps), grad_w_down, own(3),
            )

        down, up, qkv = Chunk(), Chunk(), Chunk()
        down_land, up_land = comm.core_swap(down_send), comm.core_swap(up_send)
        down.core(down_keep, down_land)
        results = back(wait_for(gmiddle_n, down.ka), 0)
        down.land, up_land, results = join(down.land, up_land, results)
        gproj_t, normed, att_sums_a, *gouts = results

        down.first()
        up.core(up_keep, wait_for(up_land, down.ka))
        results = back(wait_for(gmiddle_n, up.ka), 1, (gproj_t, normed, *gouts))
        gproj_t, normed, att_sums_b, *gouts = results
        results_q = qkv_call(info, gproj_t, normed, mlp_sums, (att_sums_a, att_sums_b))
        down.land, up.land, gouts, results_q = join(down.land, up.land, gouts, results_q)
        qkv_keep, qkv_send = results_q

        qkv_land = comm.core_swap(qkv_send)
        up.land = wait_for(up.land, qkv_send)
        up.first()
        down.land = wait_for(down.land, up.ka)
        down.second()
        qkv_land, up.land, down.land, down.own, outs = join(qkv_land, up.land, down.land, down.own, outs)

        qkv.core(qkv_keep, qkv_land)
        down.land = wait_for(down.land, qkv.ka)
        down.inner()
        up.land = wait_for(up.land, down.own)
        up.second()
        qkv.land, up.land, down.own, up.own, outs = join(qkv.land, up.land, down.own, up.own, outs)

        qkv.first()
        up.land = wait_for(up.land, qkv.ka)
        up.inner()
        out_land = swap(outs[1:])
        qkv.land, down.land, down.own, up.own, gouts = join(qkv.land, down.land, down.own, up.own, gouts)

        qkv.second()
        gouts, down.land = wait_for((gouts, down.land), qkv.own)
        gin_land = swap(gouts[1:])
        down.outer()
        qkv.land, up.land, out_land, qkv.own, down.own = join(qkv.land, up.land, out_land, qkv.own, down.own)

        qkv.inner()
        up.land = wait_for(up.land, qkv.own)
        up.outer()
        down.land = wait_for(down.land, up.own)
        down.swap()
        output = place_frames(info, [outs[0], *wait_for(out_land, up.own)], BF16)
        qkv.land, up.land, down.land, gin_land, qkv.own, up.own, output = join(
            qkv.land, up.land, down.land, gin_land, qkv.own, up.own, output
        )

        qkv.outer()
        up.land = wait_for(up.land, qkv.own)
        up.swap()
        grad_input = place_frames(info, [gouts[0], *wait_for(gin_land, up.parts[1])], F32)
        down.parts, down.land = wait_for((down.parts, down.land), grad_input)
        (grad_w_down,) = down.last(finish_down_kernel, "finish_down", [(model // 4, hidden_size)])
        qkv.land, up.land, up.parts, qkv.own, grad_w_down = join(qkv.land, up.land, up.parts, qkv.own, grad_w_down)

        qkv.swap()
        up.parts, up.land = wait_for((up.parts, up.land), qkv.parts[0])
        grad_w_up, grad_w_out = up.last(
            finish_up_kernel, "finish_up", [(model, hidden_size // 4), (model // 4, model)]
        )
        qkv.land, qkv.parts, grad_w_up = join(qkv.land, qkv.parts, grad_w_up)
        part = model // 4
        vectors = [(part,), (part,), (2 * part,), (part,), (part,), (part,), (part,), (hidden_size // 4,)]
        grad_w_qkv, g_gain_one, g_shift_one, g_bias_qv, g_gain_two, g_shift_two, g_bias_out, g_bias_down, g_bias_up = qkv.last(
            finish_qkv_kernel, "finish_qkv", [(3 * model // 4, model)] + vectors
        )
        grad_w_qkv, grad_w_out, grad_w_down = grad_w_qkv.T, grad_w_out.T, grad_w_down.T
        return (
            output,
            grad_input,
            g_gain_one,
            g_shift_one,
            grad_w_qkv,
            g_bias_qv,
            grad_w_out,
            g_bias_out,
            g_gain_two,
            g_shift_two,
            grad_w_up,
            g_bias_up,
            grad_w_down,
            g_bias_down,
        )

    return on_device


def solution(mesh):
    return jax.shard_map(
        make(mesh),
        mesh=mesh,
        in_specs=(P("clip", "col", None), P("clip", "col", None), P("clip")) + (P(),) * 13,
        out_specs=(
            P("clip", "col", None),
            P("clip", "col", None),
            P("col"),
            P("col"),
            P(None, "col"),
            P("col"),
            P(None, "col"),
            P("col"),
            P("col"),
            P("col"),
            P(None, "col"),
            P("col"),
            P(None, "col"),
            P("col"),
        ),
        check_vma=False,
    )
```

```python
import functools
import jax
import jax.numpy as jnp
from jax import lax
from jax.experimental import pallas as pl
from jax.experimental.pallas import tpu as pltpu
from jax.sharding import PartitionSpec as P

HEADS = 12
EPSILON = 1e-06
MASKED = -1e30
F32 = jnp.float32
BF16 = jnp.bfloat16
INV_SQRT2 = 0.5**0.5
INV_SQRT_2PI = 0.3989422804014327
MIB = 1 << 20
PACE = 1_500_000
GAIN_ONE, SHIFT_ONE, BIAS_OUT, GAIN_TWO, SHIFT_TWO, BIAS_DOWN, BIAS_Q, BIAS_V, BIAS_UP = range(9)


def dot(left, right):
    return lax.dot_general(left, right, (((1,), (0,)), ((), ())), preferred_element_type=F32)


def dot_nt(left, right):
    return lax.dot_general(left, right, (((1,), (1,)), ((), ())), preferred_element_type=F32)


def add_low(left, right):
    return (left.astype(F32) + right.astype(F32)).astype(BF16)


def in_hbm(array):
    return pltpu.with_memory_space_constraint(array, pltpu.HBM)


def whole(shape):
    return pl.BlockSpec(shape, lambda *_: (0,) * len(shape), pipeline_mode=pl.Buffered(1))


def lanes(rows, size):
    return pl.BlockSpec((rows, size), lambda f, *_: (0, f))


def tokens_of(size, columns):
    return pl.BlockSpec((size, columns), lambda f, *_: (f, 0))


def params(limit, steps=1):
    return pltpu.CompilerParams(
        vmem_limit_bytes=limit * MIB, dimension_semantics=("arbitrary",) * steps
    )


def cost(micros):
    return pl.CostEstimate(flops=0, bytes_accessed=int(micros * PACE), transcendentals=0)


def standardise(value):
    centred = value - jnp.mean(value, axis=1, keepdims=True)
    root = lax.rsqrt(jnp.mean(centred * centred, axis=1, keepdims=True) + EPSILON)
    return centred * root, root


def standardise_back(grad, gain, xhat, root):
    scaled = grad * gain
    first = jnp.mean(scaled, axis=1, keepdims=True)
    second = jnp.mean(scaled * xhat, axis=1, keepdims=True)
    return root * (scaled - first - xhat * second)


def lane_sums(value):
    total = value[:, :128]
    for at in range(128, value.shape[1], 128):
        total = total + value[:, at : at + 128]
    return total


def row_sum(value):
    return jnp.sum(value, axis=0, keepdims=True)


def pair_diagonal(upper, lower):
    zero = jnp.zeros_like(upper)
    return jnp.concatenate(
        [jnp.concatenate([upper, zero], axis=0), jnp.concatenate([zero, lower], axis=0)], axis=1
    )


def token_rows(pieces):
    return jnp.concatenate([piece[0] for piece in pieces], axis=0)


def pairs_and_blocks(size, block, stages):
    if size == block:
        for stage in stages:
            for pair in range(HEADS // 2):
                stage(pair, 0, pair)
    else:

        @pl.loop(0, HEADS // 2 * (size // block))
        def _(step):
            blocks = size // block
            pair = step // blocks
            for stage in stages:
                stage(pair, pl.multiple_of((step - pair * blocks) * block, block), 0)


def slots(size, block):
    return HEADS // 2 if size == block else 1


def mask_lanes(ranks, length, target):
    target[...] = jnp.broadcast_to(jnp.where(ranks[...] < length, 0.0, MASKED), target.shape)


def across(value, width):
    return jnp.concatenate([value] * (width // value.shape[1]), axis=1)


def _(step):
            blocks = size // block
            pair = step // blocks
            one(pair, pl.multiple_of((step - pair * blocks) * block, block))


def attend_kernel(ncol, block, first, info, lens, *refs):
    pieces = refs[:ncol]
    ranks, vecs, w_qkv, w_out = refs[ncol : ncol + 4]
    qkv_t, mixed_t, middle_n, lse, mixed_f, keys_n, mask, scores, probs, inverse = refs[-10:]
    size, model = middle_n.shape
    head = model // HEADS
    rows = token_rows(pieces).astype(F32)
    xhat, _ = standardise(rows)
    normed = (xhat * vecs[GAIN_ONE : GAIN_ONE + 1] + vecs[SHIFT_ONE : SHIFT_ONE + 1]).astype(BF16)
    queries = dot(normed, w_qkv[:, :model]) + vecs[BIAS_Q : BIAS_Q + 1]
    qkv_t[:model] = queries.T.astype(BF16) * BF16(head**-0.5)
    keys = dot(normed, w_qkv[:, model : 2 * model])
    keys_n[...] = keys.astype(BF16)
    qkv_t[model : 2 * model] = keys.T.astype(BF16)
    values = dot(normed, w_qkv[:, 2 * model :]) + vecs[BIAS_V : BIAS_V + 1]
    qkv_t[2 * model :] = values.T.astype(BF16)
    mask_lanes(ranks, lens[first + pl.program_id(0)], mask)

    def begin(pair, at, slot):
        low, high = pair * 2 * head, (pair * 2 + 1) * head
        where = pl.ds(at, block)
        right = pair_diagonal(qkv_t[pl.ds(low, head), where], qkv_t[pl.ds(high, head), where])
        scores[slot] = dot(keys_n[:, pl.ds(low, 2 * head)], right)

    def weigh(pair, at, slot):
        value = scores[slot] + across(mask[...], 2 * block)
        top = jnp.max(value, axis=0, keepdims=True)
        weight = jnp.exp(value - top)
        total = jnp.sum(weight, axis=0, keepdims=True)
        probs[slot] = weight.astype(BF16)
        inverse[slot] = 1.0 / total
        stats = top + jnp.log(total)
        for side in range(2):
            lse[0, pl.ds(pair * 2 + side, 1), pl.ds(at, block)] = stats[:, side * block : (side + 1) * block]

    def mix(pair, at, slot):
        for side in range(2):
            start, cut = (pair * 2 + side) * head, slice(side * block, (side + 1) * block)
            value = qkv_t[pl.ds(2 * model + start, head), :]
            mixed_f[pl.ds(start, head), pl.ds(at, block)] = dot(value, probs[slot, :, cut]) * inverse[slot, :, cut]

    pairs_and_blocks(size, block, (begin, weigh, mix))
    mixed_t[...] = mixed_f[...].astype(BF16)
    middle = rows + dot(mixed_f[...].T.astype(BF16), w_out[...]) + vecs[BIAS_OUT : BIAS_OUT + 1]
    middle_n[...] = middle


def attend_call(info, lens, pieces, ranks, vecs, w_qkv, w_out, first, frames, per, earlier=()):
    ncol = len(pieces)
    width, model = pieces[1].shape[1:]
    size = ncol * width
    tokens = per * size
    block = min(size, 256)
    own = pl.BlockSpec((1, width, model), lambda f, info, *_: (info[0] * per + first + f, 0, 0))
    other = pl.BlockSpec((1, width, model), lambda f, *_: (f, 0, 0))

    def rows_of(columns):
        return pl.BlockSpec((size, columns), lambda f, *_: (first + f, 0))

    def lanes_of(rows):
        return pl.BlockSpec((rows, size), lambda f, *_: (0, first + f))

    return pl.pallas_call(
        functools.partial(attend_kernel, ncol, block, first),
        grid_spec=pltpu.PrefetchScalarGridSpec(
            num_scalar_prefetch=2,
            grid=(frames,),
            in_specs=[own]
            + [other] * (ncol - 1)
            + [whole(ranks.shape), whole(vecs.shape), whole(w_qkv.shape), whole(w_out.shape)]
            + [pl.BlockSpec(memory_space=pl.ANY)] * len(earlier),
            out_specs=[
                lanes_of(3 * model),
                lanes_of(model),
                rows_of(model),
                pl.BlockSpec((1, 16, size), lambda f, *_: (first + f, 0, 0)),
            ],
            scratch_shapes=[
                pltpu.VMEM((model, size), F32),
                pltpu.VMEM((size, model), BF16),
                pltpu.VMEM((size, 128), F32),
                pltpu.VMEM((slots(size, block), size, 2 * block), F32),
                pltpu.VMEM((slots(size, block), size, 2 * block), BF16),
                pltpu.VMEM((slots(size, block), 1, 2 * block), F32),
            ],
        ),
        out_shape=[
            pltpu.HBM((3 * model, tokens), BF16),
            pltpu.HBM((model, tokens), BF16),
            pltpu.HBM((tokens, model), F32),
            pltpu.HBM((per, 16, size), F32),
        ],
        input_output_aliases={ncol + 6 + i: i for i in range(len(earlier))},
        compiler_params=params(40),
        cost_estimate=cost(10),
        name="attend",
    )(info, lens, *pieces, ranks, vecs, in_hbm(w_qkv), in_hbm(w_out), *earlier)


def gather_tokens(pieces, target):
    frames, width = pieces[1].shape[:2]
    at = 0
    for f in range(frames):
        for piece in pieces:
            target[at : at + width] = piece[f]
            at += width


def halves_apart(info, value):
    first, chunk = info[1] == 0, value.shape[1] // 2
    low, high = value[:, :chunk], value[:, chunk:]
    return jnp.where(first, low, high), jnp.where(first, high, low)


def mlp_kernel(ncol, info, *refs):
    own_in, *pieces_in = refs[:ncol]
    middle_n, mixed_in, vecs, w_up, w_down = refs[ncol : ncol + 5]
    outs = refs[ncol + 5 : 2 * ncol + 5]
    gmiddle_out, sums, down_keep, down_send, up_keep, up_send = refs[2 * ncol + 5 : 2 * ncol + 11]
    (
        cot_p, cot_n, cot_t, second_n, second_t, active_n, hidden_n, total, grad, mixed_t, up_slots, down_slots, out_slots,
        in_sems, up_sems, down_sems, out_sems, g_sems,
    ) = refs[2 * ncol + 11 :]
    tokens, model = total.shape
    frames, width = outs[0].shape[:2]
    part = model // 4
    rows = min(tokens, 256)
    step, steps = pl.program_id(0), pl.num_programs(0) - 1
    gain = vecs[GAIN_TWO : GAIN_TWO + 1]
    coming = [
        pltpu.make_async_copy(own_in.at[pl.ds(info[0] * frames, frames)], cot_p.at[0], in_sems.at[0]),
        *[pltpu.make_async_copy(p, cot_p.at[i + 1], in_sems.at[i + 1]) for i, p in enumerate(pieces_in)],
        pltpu.make_async_copy(mixed_in, mixed_t, in_sems.at[ncol]),
    ]

    def down_copy(j):
        target = down_keep if j >= 2 else down_send
        return pltpu.make_async_copy(down_slots.at[j], target.at[:, pl.ds(j % 2 * part, part), :], down_sems.at[j])

    def up_copies(j, block):
        return [
            pltpu.make_async_copy(up_slots.at[side, j], target.at[block, pl.ds(0, model), :], up_sems.at[side, j])
            for side, target in enumerate((up_keep, up_send))
        ]

    @pl.when(step == 0)
    def _():
        for copy in coming:
            copy.start()
        sums[...] = jnp.zeros_like(sums)
        for at in range(0, tokens, rows):
            cut = slice(at, at + rows)
            middle = middle_n[cut]
            xhat, _ = standardise(middle)
            second = xhat * gain + vecs[SHIFT_TWO : SHIFT_TWO + 1]
            second_n[cut] = second.astype(BF16)
            second_t[:, cut] = second.T.astype(BF16)
            total[cut] = middle + vecs[BIAS_DOWN : BIAS_DOWN + 1]
            grad[cut] = jnp.zeros((rows, model), F32)
        for copy in coming[:ncol]:
            copy.wait()
        gather_tokens([cot_p.at[i] for i in range(ncol)], cot_n)
        cot_t[...] = cot_n[...].astype(F32).T.astype(BF16)

    @pl.when(step < steps)
    def _():
        block = block_of(step, info)
        bias = vecs[pl.ds(BIAS_UP + block, 1), :]
        for at in range(0, tokens, rows):
            cut = slice(at, at + rows)
            hidden = dot(second_n[cut], w_up[...]) + bias
            half = 0.5 + 0.5 * lax.erf(hidden * INV_SQRT2)
            active = (hidden * half).astype(BF16)
            bell = jnp.exp(hidden * hidden * -0.5) * INV_SQRT_2PI
            slope = half + hidden * bell
            active_n[cut] = active
            total[cut] += dot(active, w_down[...])
            low = (dot_nt(cot_n[cut], w_down[...]) * slope).astype(BF16)
            hidden_n[cut] = low
            sums[pl.ds(4 + block, 1), :] += row_sum(low.astype(F32))
            grad[cut] += dot_nt(low, w_up[...])
        result = dot(cot_t[...], active_n[...]).astype(BF16)
        for c in range(4):
            down_slots[step, c] = result[c * part : (c + 1) * part]
        up_slots[0, step], up_slots[1, step] = halves_apart(info, dot(second_t[...], hidden_n[...]).astype(BF16))
        for copy in up_copies(step, block):
            copy.start()

    for j in range(4):

        @pl.when(step == j)
        def _(j=j):
            down_copy(j).start()

    @pl.when(step == steps)
    def _():
        at = 0
        for f in range(frames):
            for out in outs:
                out[f] = total[at : at + width].astype(BF16)
                at += width
        going = []
        for i, at in enumerate(range(0, tokens, rows)):
            cut = slice(at, at + rows)
            xhat, root = standardise(middle_n[cut])
            cot_f32, back = cot_n[cut].astype(F32), grad[cut]
            grad_middle = cot_f32 + standardise_back(back, gain, xhat, root)
            total[cut] = grad_middle
            copy = pltpu.make_async_copy(total.at[pl.ds(at, rows)], gmiddle_out.at[pl.ds(at, rows)], g_sems.at[i])
            copy.start()
            going.append(copy)
            low = grad_middle.astype(BF16)
            hidden_n[cut] = low
            sums[0:1] += row_sum(back * xhat)
            sums[1:2] += row_sum(back)
            sums[2:3] += row_sum(low.astype(F32))
            sums[3:4] += row_sum(cot_f32)
        coming[ncol].wait()
        both = halves_apart(info, dot(mixed_t[...], hidden_n[...]).T.astype(BF16))
        for side, target in enumerate((up_keep, up_send)):
            for c in range(4):
                out_slots[side, c] = both[side][c * part : (c + 1) * part]
                copy = pltpu.make_async_copy(out_slots.at[side, c], target.at[c, pl.ds(model, part), :], out_sems.at[side, c])
                copy.start()
                going.append(copy)
        for j in range(4):
            going += [down_copy(j), *up_copies(j, block_of(j, info))]
        for copy in going:
            copy.wait()


def block_of(step, info):
    return lax.bitwise_xor(step // 2, 1 - info[1]) * 2 + step % 2


def mlp_call(info, pieces, middle_n, mixed_t, vecs, w_up, w_down):
    ncol = len(pieces)
    piece = pieces[1].shape
    tokens, model = middle_n.shape
    steps = w_down.shape[0] // model
    part, chunk = model // 4, model // 2
    rows = min(tokens, 256)
    stays = pl.BlockSpec(memory_space=pltpu.HBM)

    def block(j, info):
        return block_of(jnp.minimum(j, steps - 1), info)

    down, up = (4, 2 * part, model), (steps, model + part, chunk)
    return pl.pallas_call(
        functools.partial(mlp_kernel, ncol),
        grid_spec=pltpu.PrefetchScalarGridSpec(
            num_scalar_prefetch=1,
            grid=(steps + 1,),
            in_specs=[stays] * ncol
            + [
                whole(middle_n.shape),
                stays,
                whole(vecs.shape),
                pl.BlockSpec((model, model), lambda j, info: (0, block(j, info))),
                pl.BlockSpec((model, model), lambda j, info: (block(j, info), 0)),
            ],
            out_specs=[whole(piece)] * ncol + [stays, whole((16, model))] + [stays] * 4,
            scratch_shapes=[
                pltpu.VMEM((ncol,) + piece, BF16),
                pltpu.VMEM((tokens, model), BF16),
                pltpu.VMEM((model, tokens), BF16),
                pltpu.VMEM((tokens, model), BF16),
                pltpu.VMEM((model, tokens), BF16),
                pltpu.VMEM((tokens, model), BF16),
                pltpu.VMEM((tokens, model), BF16),
                pltpu.VMEM((tokens, model), F32),
                pltpu.VMEM((tokens, model), F32),
                pltpu.VMEM((model, tokens), BF16),
                pltpu.VMEM((2, steps, model, chunk), BF16),
                pltpu.VMEM((steps, 4, part, model), BF16),
                pltpu.VMEM((2, 4, part, chunk), BF16),
                pltpu.SemaphoreType.DMA((ncol + 1,)),
                pltpu.SemaphoreType.DMA((2, steps)),
                pltpu.SemaphoreType.DMA((steps,)),
                pltpu.SemaphoreType.DMA((2, 4)),
                pltpu.SemaphoreType.DMA((tokens // rows,)),
            ],
        ),
        out_shape=[pltpu.HBM(piece, BF16)] * ncol
        + [pltpu.HBM((tokens, model), F32), jax.ShapeDtypeStruct((16, model), F32)]
        + [pltpu.HBM(s, BF16) for s in (down, down, up, up)],
        compiler_params=params(60),
        cost_estimate=cost(40),
        name="mlp",
    )(info, *[in_hbm(p) for p in pieces], in_hbm(middle_n), in_hbm(mixed_t), vecs, in_hbm(w_up), in_hbm(w_down))


def attend_back_kernel(ncol, block, first, info, lens, *refs):
    pieces = refs[:ncol]
    ranks, vecs, w_qkv_in, w_out, qkv_t, lse, mixed_t, gmiddle_n = refs[ncol : ncol + 8]
    gproj_t, normed_n, sums, *outs = refs[-15 - ncol : -12]
    gmixed_t, gacc, columns, kv_n, mask, scores, gprobs, probs, gscores, inner, w_qkv, sem = refs[-12:]
    size, model = gmiddle_n.shape
    head = model // HEADS
    step = pl.program_id(0)

    coming = pltpu.make_async_copy(w_qkv_in, w_qkv, sem.at[0])

    @pl.when(step == 0)
    def _():
        coming.start()
        sums[...] = jnp.zeros_like(sums)
        columns[...] = jnp.zeros_like(columns)

    gmixed_t[...] = dot_nt(w_out[...], gmiddle_n[...].astype(BF16)).astype(BF16)
    kv_n[...] = qkv_t[model:].astype(F32).T.astype(BF16)
    mask_lanes(ranks, lens[first + step], mask)
    product = gmixed_t[...].astype(F32) * mixed_t[...].astype(F32)
    for h in range(HEADS):
        inner[h : h + 1] = row_sum(product[h * head : (h + 1) * head])
    many = size != block
    if many:
        gacc[...] = jnp.zeros_like(gacc)

    def begin(pair, at, slot):
        low, high = pair * 2 * head, (pair * 2 + 1) * head
        where = pl.ds(at, block)
        right = pair_diagonal(qkv_t[pl.ds(low, head), where], qkv_t[pl.ds(high, head), where])
        scores[slot] = dot(kv_n[:, pl.ds(low, 2 * head)], right)
        right = pair_diagonal(gmixed_t[pl.ds(low, head), where], gmixed_t[pl.ds(high, head), where])
        gprobs[slot] = dot(kv_n[:, pl.ds(model + low, 2 * head)], right)

    def weigh(pair, at, slot):
        where = pl.ds(at, block)
        stats, means = (
            jnp.concatenate([rows[pl.ds(pair * 2 + i, 1), where] for i in range(2)], axis=1) for rows in (lse.at[0], inner)
        )
        value = jnp.exp(scores[slot] + across(mask[...], 2 * block) - stats)
        probs[slot] = value.astype(BF16)
        gscores[slot] = (value * (gprobs[slot] - means)).astype(BF16)

    def spread(pair, at, slot):
        where = pl.ds(at, block)
        for side in range(2):
            start, cut = (pair * 2 + side) * head, slice(side * block, (side + 1) * block)
            grad_side = gscores[slot, :, cut]
            grad_q = dot(qkv_t[pl.ds(model + start, head), :], grad_side) * head**-0.5
            grad_k = dot_nt(qkv_t[pl.ds(start, head), where], grad_side)
            grad_v = dot_nt(gmixed_t[pl.ds(start, head), where], probs[slot, :, cut])
            gproj_t[pl.ds(start, head), where] = grad_q.astype(BF16)
            if many:
                gacc[pl.ds(start, head), :] += grad_k
                gacc[pl.ds(model + start, head), :] += grad_v
            else:
                gproj_t[pl.ds(model + start, head), :] = grad_k.astype(BF16)
                gproj_t[pl.ds(2 * model + start, head), :] = grad_v.astype(BF16)

    pairs_and_blocks(size, block, (begin, weigh, spread))
    if many:
        gproj_t[model:] = gacc[...].astype(BF16)
    columns[:model] += lane_sums(gproj_t[:model].astype(F32))
    columns[model:] += lane_sums(gproj_t[2 * model :].astype(F32))

    @pl.when(step == 0)
    def _():
        coming.wait()

    grad = dot(w_qkv[...], gproj_t[...]).T
    xhat, root = standardise(token_rows(pieces).astype(F32))
    gain = vecs[GAIN_ONE : GAIN_ONE + 1]
    normed_n[...] = (xhat * gain + vecs[SHIFT_ONE : SHIFT_ONE + 1]).astype(BF16)
    sums[0:1] += row_sum(grad * xhat)
    sums[1:2] += row_sum(grad)
    total = gmiddle_n[...] + standardise_back(grad, gain, xhat, root)
    result = total.astype(BF16)
    width = size // ncol
    for k in range(ncol):
        outs[k][0] = result[k * width : (k + 1) * width]

    @pl.when(step == pl.num_programs(0) - 1)
    def _():
        for i in range(2):
            sums[2 + i : 3 + i] = row_sum(columns[i * model : (i + 1) * model].T)


def attend_back_call(
    info, lens, pieces, ranks, vecs, w_qkv, w_out, qkv_t, lse, mixed_t, gmiddle_n, first, frames, per, earlier=()
):
    ncol = len(pieces)
    width, model = pieces[1].shape[1:]
    size = ncol * width
    tokens = per * size
    block = min(size, 256)
    acc = (2 * model, size) if size != block else (8, 128)

    def later(spec_lanes, shape):
        if spec_lanes:
            return pl.BlockSpec(shape, lambda f, *_: (0, first + f))
        return pl.BlockSpec(shape, lambda f, *_: (first + f,) + (0,) * (len(shape) - 1))

    own = pl.BlockSpec((1, width, model), lambda f, info, *_: (info[0] * per + first + f, 0, 0))
    piece = later(False, (1, width, model))
    return pl.pallas_call(
        functools.partial(attend_back_kernel, ncol, block, first),
        grid_spec=pltpu.PrefetchScalarGridSpec(
            num_scalar_prefetch=2,
            grid=(frames,),
            in_specs=[own]
            + [piece] * (ncol - 1)
            + [
                whole(ranks.shape),
                whole(vecs.shape),
                pl.BlockSpec(memory_space=pltpu.HBM),
                whole(w_out.shape),
                later(True, (3 * model, size)),
                later(False, (1, 16, size)),
                later(True, (model, size)),
                later(False, (size, model)),
            ]
            + [pl.BlockSpec(memory_space=pl.ANY)] * len(earlier),
            out_specs=[later(True, (3 * model, size)), later(False, (size, model)), whole((16, model))] + [piece] * ncol,
            scratch_shapes=[
                pltpu.VMEM((model, size), BF16),
                pltpu.VMEM(acc, F32),
                pltpu.VMEM((2 * model, 128), F32),
                pltpu.VMEM((size, 2 * model), BF16),
                pltpu.VMEM((size, 128), F32),
                pltpu.VMEM((slots(size, block), size, 2 * block), F32),
                pltpu.VMEM((slots(size, block), size, 2 * block), F32),
                pltpu.VMEM((slots(size, block), size, 2 * block), BF16),
                pltpu.VMEM((slots(size, block), size, 2 * block), BF16),
                pltpu.VMEM((16, size), F32),
                pltpu.VMEM(w_qkv.shape, BF16),
                pltpu.SemaphoreType.DMA((1,)),
            ],
        ),
        out_shape=[
            pltpu.HBM((3 * model, tokens), BF16),
            pltpu.HBM((tokens, model), BF16),
            pltpu.HBM((16, model), F32),
        ]
        + [pltpu.HBM((per, width, model), BF16)] * ncol,
        input_output_aliases={ncol + 10 + i: i + (i > 1) for i in range(len(earlier))},
        compiler_params=params(40 if size == block else 62),
        cost_estimate=cost(15),
        name="attend_back",
    )(info, lens, *pieces, ranks, vecs, in_hbm(w_qkv), in_hbm(w_out), in_hbm(qkv_t), lse, in_hbm(mixed_t), in_hbm(gmiddle_n), *earlier)


def take_kernel(info, *refs):
    half = len(refs) // 2
    for source, target in zip(refs[:half], refs[half:]):
        target[...] = source[...]


def take_frames(info, array, ncol, group=0, groups=1):
    per = array.shape[0] // ncol // groups
    shape = (per,) + array.shape[1:]
    specs = [
        pl.BlockSpec(shape, lambda i, info, k=k: (lax.bitwise_xor(info[0], k) * groups + group, 0, 0))
        for k in range(1, ncol)
    ]
    return pl.pallas_call(
        take_kernel,
        grid_spec=pltpu.PrefetchScalarGridSpec(
            num_scalar_prefetch=1,
            grid=(1,),
            in_specs=specs,
            out_specs=[pl.BlockSpec(shape, lambda i, *_: (0, 0, 0))] * (ncol - 1),
        ),
        out_shape=[pltpu.HBM(shape, array.dtype)] * (ncol - 1),
        compiler_params=params(8),
        cost_estimate=cost(1),
        name="take_frames",
    )(info, *[in_hbm(array)] * (ncol - 1))


def place_kernel(info, *refs):
    *pieces, out = refs
    for k, piece in enumerate(pieces):

        @pl.when(pl.program_id(0) == k)
        def _(piece=piece):
            out[...] = piece[...].astype(out.dtype)


def place_frames(info, pieces, dtype):
    shape = pieces[0].shape
    return pl.pallas_call(
        place_kernel,
        grid_spec=pltpu.PrefetchScalarGridSpec(
            num_scalar_prefetch=1,
            grid=(len(pieces),),
            in_specs=[whole(shape)] * len(pieces),
            out_specs=pl.BlockSpec(shape, lambda k, info: (lax.bitwise_xor(info[0], k), 0, 0)),
        ),
        out_shape=pltpu.HBM((len(pieces) * shape[0],) + shape[1:], dtype),
        compiler_params=params(12),
        cost_estimate=cost(2),
        name="place_frames",
    )(info, *pieces)


def pick(array, index, axis):
    return lax.dynamic_index_in_dim(array, index, axis, keepdims=False)


class Comm:
    def __init__(self, mesh):
        self.ncol = mesh.shape["col"]
        self.nclip = mesh.shape["clip"]
        self.nz = self.nclip // 2
        self.me = lax.axis_index("col")
        self.clip = lax.axis_index("clip")
        self.core = lax.rem(self.clip, 2)
        self.z = lax.div(self.clip, 2)

    def col_swap(self, array, distance):
        return lax.ppermute(array, "col", [(i, i ^ distance) for i in range(self.ncol)])

    def core_swap(self, array):
        return lax.ppermute(array, "clip", [(i, i ^ 1) for i in range(self.nclip)])

    def z_move(self, array, pairs):
        moves = [(2 * a + c, 2 * b + c) for a, b in pairs for c in range(2)]
        return lax.ppermute(array, "clip", moves)

    def z_swap(self, array, distance):
        return lax.ppermute(array, "clip", [(i, i ^ (2 * distance)) for i in range(self.nclip)])

    def halve(self, terms, bits):
        nbits = self.ncol.bit_length() - 1
        present = list(range(nbits - 1, -1, -1))
        for bit in bits:
            axis = present.index(bit)
            mine = lax.rem(lax.shift_right_logical(self.me, bit), 2)
            away = [pick(t, 1 - mine, axis) for t in terms]
            total = away[0]
            if len(away) > 1:
                total = add_low(away[0], away[1])
            landed = self.col_swap(total, 1 << bit)
            near = [pick(t, mine, axis) for t in terms]
            if len(near) > 1:
                near = [add_low(near[0], near[1])]
            terms = [near[0], landed]
            present.pop(axis)
        return add_low(terms[0], terms[1])

    def reduce_rows(self, grad):
        rows, depth = grad.shape
        part = rows // self.ncol // 4
        nbits = self.ncol.bit_length() - 1
        split = grad.reshape(self.ncol, 2, 2, part, depth)
        keep = pick(split, self.core, 1)
        landed = self.core_swap(pick(split, 1 - self.core, 1))
        order = list(range(nbits))
        half = nbits // 2
        orders = (order, order[half:] + order[:half])
        done = []
        for side in range(2):
            terms = [
                t[:, side].reshape((2,) * nbits + (part, depth)) for t in (keep, landed)
            ]
            done.append(self.halve(terms, orders[side]))
        total = jnp.concatenate(done, axis=0)
        total = self.sum_line(total)
        other = self.core_swap(total)
        first = self.core == 0
        return jnp.concatenate(
            [jnp.where(first, total, other), jnp.where(first, other, total)], axis=0
        )

    def sum_line(self, total):
        nz = self.nz
        for step in range(nz // 2 - 1):
            total = add_low(total, self.z_move(total, [(step, step + 1), (nz - 1 - step, nz - 2 - step)]))
        low, high = nz // 2 - 1, nz // 2
        total = add_low(total, self.z_move(total, [(low, high), (high, low)]))
        for step in range(nz // 2 - 1, 0, -1):
            landed = self.z_move(total, [(step, step - 1), (nz - 1 - step, nz - step)])
            takes = jnp.logical_or(self.z == step - 1, self.z == nz - step)
            total = jnp.where(takes, landed, total)
        return total


def qkv_kernel(info, gproj_t, normed_n, mlp_sums, *refs):
    *att, keep, send, total, vectors = refs
    c = pl.program_id(0)
    model = mlp_sums.shape[1]
    rows = total.shape[0] // 2
    part = model // 4
    total[...] = dot(gproj_t[...], normed_n[...])

    for i in range(4):

        @pl.when(c == i)
        def _(i=i):
            att_sums = att[0][...]
            for more in att[1:]:
                att_sums = att_sums + more[...]
            vectors[...] = jnp.zeros_like(vectors)
            vectors[0, 0:4, :part] = mlp_sums[0:4, i * part : (i + 1) * part]
            vectors[0, 4:5, :] = mlp_sums[4 + i : 5 + i]
            vectors[1, 0:2, :part] = att_sums[0:2, i * part : (i + 1) * part]
            start = i % 2 * 2 * part
            vectors[1, 2:3, : 2 * part] = att_sums[2 + i // 2 : 3 + i // 2, start : start + 2 * part]

    for side, target in enumerate((keep, send)):
        which = lax.bitwise_xor(info[1], side)
        target[0, :rows] = total[pl.ds(pl.multiple_of(which * rows, rows), rows), :].astype(BF16)
        target[0, rows:] = vectors[which].astype(BF16)


VECTOR_ROWS = 32


def qkv_call(info, gproj_t, normed_n, mlp_sums, att_sums):
    model = mlp_sums.shape[1]
    rows = 3 * model // 4
    block = (1, rows // 2 + VECTOR_ROWS, model)
    out = jax.ShapeDtypeStruct((4,) + block[1:], BF16)
    others = (normed_n, mlp_sums, *att_sums)
    return pl.pallas_call(
        qkv_kernel,
        grid_spec=pltpu.PrefetchScalarGridSpec(
            num_scalar_prefetch=1,
            grid=(4,),
            in_specs=[pl.BlockSpec((rows, gproj_t.shape[1]), lambda c, info: (c, 0))]
            + [whole(o.shape) for o in others],
            out_specs=[pl.BlockSpec(block, lambda c, info: (c, 0, 0))] * 2,
            scratch_shapes=[pltpu.VMEM((rows, model), F32), pltpu.VMEM((2, VECTOR_ROWS, model), F32)],
        ),
        out_shape=[out, out],
        compiler_params=params(24),
        cost_estimate=cost(6),
        name="grad_qkv",
    )(info, in_hbm(gproj_t), in_hbm(normed_n), *others[1:])


def sum_core_kernel(info, *refs):
    for i in range(4):
        refs[8 + i][...] = add_low(refs[i][...], refs[4 + i][...])


def sum_core(info, keep, landed):
    rows, depth = keep.shape[1] // 2, keep.shape[2]
    block = (1, rows, depth)

    def by_x(i, info, flip, side):
        return (2 * i + lax.bitwise_xor(info[2], flip), side, 0)

    def by_y(i, info, flip, side):
        return (2 * lax.bitwise_xor(info[3], flip) + i, side, 0)

    specs = [
        pl.BlockSpec(block, functools.partial(lambda i, info, fn, flip, side: fn(i, info, flip, side), fn=fn, flip=flip, side=side))
        for side, fn in enumerate((by_x, by_y))
        for flip in (1, 0)
    ]
    out = jax.ShapeDtypeStruct((2, rows, depth), BF16)
    return pl.pallas_call(
        sum_core_kernel,
        grid_spec=pltpu.PrefetchScalarGridSpec(
            num_scalar_prefetch=1,
            grid=(2,),
            in_specs=specs * 2,
            out_specs=[pl.BlockSpec(block, lambda i, info: (i, 0, 0))] * 4,
        ),
        out_shape=[out] * 4,
        compiler_params=params(16),
        cost_estimate=cost(2),
        name="sum_core",
    )(info, *[keep] * 4, *[landed] * 4)


def sum_first_kernel(info, keep_a, land_a, keep_b, land_b, send_a, stay_a, send_b, stay_b):
    for keep, land, send, stay, mine in (
        (keep_a, land_a, send_a, stay_a, info[3]),
        (keep_b, land_b, send_b, stay_b, info[2]),
    ):
        send[...] = add_low(keep[1 - mine], land[1 - mine])
        stay[...] = add_low(keep[mine], land[mine])


def sum_first(info, keep_a, land_a, keep_b, land_b):
    rows, depth = keep_a.shape[1:]
    out = jax.ShapeDtypeStruct((rows, depth), BF16)
    return pl.pallas_call(
        sum_first_kernel,
        grid_spec=pltpu.PrefetchScalarGridSpec(
            num_scalar_prefetch=1,
            grid=(1,),
            in_specs=[whole(keep_a.shape)] * 4,
            out_specs=[whole((rows, depth))] * 4,
        ),
        out_shape=[out] * 4,
        compiler_params=params(16),
        cost_estimate=cost(1),
        name="sum_first",
    )(info, keep_a, land_a, keep_b, land_b)


def sum_second_kernel(info, stay_a, land_a, stay_b, land_b, own, send):
    low, high = add_low(stay_a[...], land_a[...]), add_low(stay_b[...], land_b[...])
    own[...] = jnp.where(info[4] == 0, low, high)
    send[...] = jnp.where(info[4] == 0, high, low)


def sum_second(info, stay_a, land_a, stay_b, land_b):
    shape = stay_a.shape
    return pl.pallas_call(
        sum_second_kernel,
        grid_spec=pltpu.PrefetchScalarGridSpec(
            num_scalar_prefetch=1, grid=(1,), in_specs=[whole(shape)] * 4, out_specs=[whole(shape)] * 2
        ),
        out_shape=[jax.ShapeDtypeStruct(shape, BF16)] * 2,
        compiler_params=params(16),
        cost_estimate=cost(1),
        name="sum_second",
    )(info, stay_a, land_a, stay_b, land_b)


def collect(info, parts, full):
    rows = parts[0].shape[0]
    for i, part in enumerate(parts):
        at = lax.bitwise_xor(info[4], i % 2) * rows
        full[lax.bitwise_xor(info[1], i // 2), pl.ds(pl.multiple_of(at, rows), rows), :] = part[...]


def finish_down_kernel(info, *refs):
    *parts, down_t, full = refs
    collect(info, parts, full)
    model, part = full.shape[2], down_t.shape[0]
    blocks = full.shape[1] // part
    for half in range(2):
        for j in range(blocks):
            at = (half * blocks + j) * model
            down_t[:, at : at + model] = full[half, j * part : (j + 1) * part].astype(F32)


def finish_up_kernel(info, *refs):
    *parts, up, out_t, full = refs
    collect(info, parts, full)
    model, chunk = up.shape[0], full.shape[2]
    for half in range(2):
        cut = slice(half * chunk, (half + 1) * chunk)
        up[:, cut] = full[half, :model].astype(F32)
        out_t[:, cut] = full[half, model:].astype(F32)


def finish_qkv_kernel(info, *refs):
    *parts, qkv_t, gain_one, shift_one, bias_qv, gain_two, shift_two, bias_out, bias_down, bias_up, full = refs
    collect(info, parts, full)
    rows = qkv_t.shape[0] // 2
    for half in range(2):
        qkv_t[half * rows : (half + 1) * rows] = full[half, :rows].astype(F32)
    mlp_rows = full[0, rows : rows + 16].astype(F32)
    att_rows = full[1, rows : rows + 16].astype(F32)
    for source, targets in ((mlp_rows, (gain_two, shift_two, bias_out, bias_down, bias_up)), (att_rows, (gain_one, shift_one, bias_qv))):
        for i, target in enumerate(targets):
            target[...] = source[i, : target.shape[0]]


def finish(kernel, name, info, parts, shapes):
    rows, depth = parts[0].shape
    return pl.pallas_call(
        kernel,
        grid_spec=pltpu.PrefetchScalarGridSpec(
            num_scalar_prefetch=1,
            grid=(1,),
            in_specs=[whole((rows, depth))] * 4,
            out_specs=[whole(s) for s in shapes],
            scratch_shapes=[pltpu.VMEM((2, 2 * rows, depth), BF16)],
        ),
        out_shape=[pltpu.HBM(s, F32) for s in shapes],
        compiler_params=params(24),
        cost_estimate=cost(2),
        name=name,
    )(info, *parts)


def wait_for(values, *others):
    flat, tree = jax.tree.flatten(values)
    held = lax.optimization_barrier((tuple(flat), others))[0]
    return jax.tree.unflatten(tree, held)


def join(*values):
    flat, tree = jax.tree.flatten(values)
    return jax.tree.unflatten(tree, lax.optimization_barrier(tuple(flat)))


def make(mesh):
    def on_device(
        frames,
        cotangent,
        frame_len,
        column_rank,
        gain_one,
        shift_one,
        w_qkv,
        bias_qv,
        w_out,
        bias_out,
        gain_two,
        shift_two,
        w_up,
        bias_up,
        w_down,
        bias_down,
    ):
        comm = Comm(mesh)
        ncol, me = comm.ncol, comm.me
        count, width, model = frames.shape
        hidden_size = w_down.shape[0]
        per = count // ncol
        size = ncol * width
        groups = 2 if per % 2 == 0 else 1
        part = per // groups
        middle_z = jnp.logical_or(comm.z == 1, comm.z == 2)
        info = jnp.stack([me, comm.core, lax.rem(me, 2), lax.div(me, 2), middle_z.astype(me.dtype)]).astype(jnp.int32)
        order = lax.bitwise_xor(me, jnp.arange(ncol, dtype=jnp.int32))
        ranks = column_rank.reshape(ncol, width)[order].reshape(size, 1)
        lens = pick(frame_len.reshape(ncol, per), me, 0)
        given = [gain_one, shift_one, bias_out, gain_two, shift_two, bias_down, bias_qv, bias_up]
        total, at, vecs = sum(v.size for v in given), 0, 0.0
        for v in given:
            vecs = vecs + jnp.pad(v.astype(F32), (at, total - at - v.size))
            at += v.size
        vecs = vecs.reshape(-1, model)

        def swap(pieces):
            return [comm.col_swap(p, k + 1) for k, p in enumerate(pieces)]

        paired = ncol == 4 and comm.nz == 4

        class Chunk:
            land = ()

            def core(self, keep, land):
                sa, self.ka, sb, self.kb = sum_core(info, keep, land)
                self.land = [comm.col_swap(sa, 1), comm.col_swap(sb, 2)]

            def first(self):
                sa, self.ka, sb, self.kb = sum_first(info, self.ka, self.land[0], self.kb, self.land[1])
                self.land = [comm.col_swap(sa, 2), comm.col_swap(sb, 1)]

            def second(self):
                self.own, send = sum_second(info, self.ka, self.land[0], self.kb, self.land[1])
                self.land = comm.z_swap(send, 1)

            def inner(self):
                self.own = add_low(self.own, self.land)
                self.land = comm.z_swap(self.own, 3)

            def outer(self):
                self.own = add_low(self.own, self.land)
                self.land = [comm.z_swap(self.own, 1), comm.core_swap(self.own)]

            def swap(self):
                self.parts = [self.own] + self.land
                self.land = comm.core_swap(self.parts[1])

            def last(self, kernel, name, shapes):
                return finish(kernel, name, info, self.parts + [self.land], shapes)

        landed = swap(take_frames(info, frames, ncol))
        cot_send = take_frames(info, cotangent, ncol)
        landed[0], cot_send, ranks, vecs, lens = join(landed[0], cot_send, ranks, vecs, lens)
        cot_land = swap(cot_send)
        rows = [frames, *join(*landed)]
        kept = attend_call(info, lens, rows, ranks, vecs, w_qkv, w_out, 0, per, per)
        kept, landed = join(kept, cot_land)
        qkv_t, mixed_t, middle_n, lse = kept
        cots = [cotangent, *landed]
        results = mlp_call(info, cots, middle_n, mixed_t, vecs, w_up, w_down)
        *outs, gmiddle_n, mlp_sums, down_keep, down_send, up_keep, up_send = join(*results)

        def back(gmiddle_n, g, earlier=()):
            return attend_back_call(
                info, lens, rows, ranks, vecs, w_qkv, w_out, qkv_t, lse, mixed_t, gmiddle_n, g * part, part, per, earlier
            )

        if not paired:
            out_land = swap(outs[1:])
            att_sums, earlier = 0.0, ()
            for g in range(groups):
                gproj_t, normed, sums, *gouts = back(gmiddle_n, g, earlier)
                att_sums, earlier = att_sums + sums, (gproj_t, normed, *gouts)
            output = place_frames(info, [outs[0]] + out_land, BF16)
            grad_input = place_frames(info, [gouts[0]] + swap(gouts[1:]), F32)
            first = comm.core == 0
            steps, part = hidden_size // model, model // 4

            def halves(keep, send):
                return jnp.stack([jnp.where(first, keep, send), jnp.where(first, send, keep)])

            def reduced(grad):
                return comm.reduce_rows(grad.astype(BF16)).astype(F32).T

            grad = halves(up_keep, up_send)
            grad_w_up = reduced(grad[:, :, :model].transpose(1, 0, 3, 2).reshape(hidden_size, model))
            grad_w_out = reduced(grad[:, :, model:].transpose(1, 2, 0, 3).reshape(model, model))
            grad = halves(down_keep, down_send).reshape(2, 4, steps // 2, part, model).transpose(1, 3, 0, 2, 4)
            grad_w_down = reduced(grad.reshape(model, hidden_size))
            grad_w_qkv = reduced(dot(gproj_t, normed))
            sums = jnp.concatenate([mlp_sums, att_sums])
            sums = reduced(jnp.concatenate([sums] * ncol)).T

            def own(row, rows=1):
                return pick(sums[row : row + rows].reshape(ncol, -1), me, 0)

            return (
                output, grad_input, own(16), own(17), grad_w_qkv, own(18, 2), grad_w_out, own(2), own(0), own(1),
                grad_w_up, own(4, steps), grad_w_down, own(3),
            )

        down, up, qkv = Chunk(), Chunk(), Chunk()
        down_land, up_land = comm.core_swap(down_send), comm.core_swap(up_send)
        down.core(down_keep, down_land)
        results = back(wait_for(gmiddle_n, down.ka), 0)
        down.land, up_land, results = join(down.land, up_land, results)
        gproj_t, normed, att_sums_a, *gouts = results

        down.first()
        up.core(up_keep, wait_for(up_land, down.ka))
        results = back(wait_for(gmiddle_n, up.ka), 1, (gproj_t, normed, *gouts))
        gproj_t, normed, att_sums_b, *gouts = results
        results_q = qkv_call(info, gproj_t, normed, mlp_sums, (att_sums_a, att_sums_b))
        down.land, up.land, gouts, results_q = join(down.land, up.land, gouts, results_q)
        qkv_keep, qkv_send = results_q

        qkv_land = comm.core_swap(qkv_send)
        up.land = wait_for(up.land, qkv_send)
        up.first()
        down.land = wait_for(down.land, up.ka)
        down.second()
        qkv_land, up.land, down.land, down.own, outs = join(qkv_land, up.land, down.land, down.own, outs)

        qkv.core(qkv_keep, qkv_land)
        down.land = wait_for(down.land, qkv.ka)
        down.inner()
        up.land = wait_for(up.land, down.own)
        up.second()
        qkv.land, up.land, down.own, up.own, outs = join(qkv.land, up.land, down.own, up.own, outs)

        qkv.first()
        up.land = wait_for(up.land, qkv.ka)
        up.inner()
        out_land = swap(outs[1:])
        qkv.land, down.land, down.own, up.own, gouts = join(qkv.land, down.land, down.own, up.own, gouts)

        qkv.second()
        gouts, down.land = wait_for((gouts, down.land), qkv.own)
        gin_land = swap(gouts[1:])
        down.outer()
        qkv.land, up.land, out_land, qkv.own, down.own = join(qkv.land, up.land, out_land, qkv.own, down.own)

        qkv.inner()
        up.land = wait_for(up.land, qkv.own)
        up.outer()
        qkv.land, down.land, gin_land, qkv.own, up.own = join(qkv.land, down.land, gin_land, qkv.own, up.own)

        qkv.outer()
        up.land = wait_for(up.land, qkv.own)
        up.swap()
        down.land = wait_for(down.land, up.parts[1])
        down.swap()
        output = place_frames(info, [outs[0], *wait_for(out_land, up.parts[1])], BF16)
        grad_input = place_frames(info, [gouts[0], *wait_for(gin_land, up.parts[1])], F32)
        qkv.land, up.land, down.land, up.parts, down.parts, qkv.own, output, grad_input = join(qkv.land, up.land, down.land, up.parts, down.parts, qkv.own, output, grad_input)

        qkv.swap()
        down.parts, down.land = wait_for((down.parts, down.land), qkv.parts[0])
        (grad_w_down,) = down.last(finish_down_kernel, "finish_down", [(model // 4, hidden_size)])
        up.parts, up.land = wait_for((up.parts, up.land), qkv.parts[0])
        grad_w_up, grad_w_out = up.last(
            finish_up_kernel, "finish_up", [(model, hidden_size // 4), (model // 4, model)]
        )
        qkv.land, qkv.parts, grad_w_up = join(qkv.land, qkv.parts, grad_w_up)
        part = model // 4
        vectors = [(part,), (part,), (2 * part,), (part,), (part,), (part,), (part,), (hidden_size // 4,)]
        grad_w_qkv, g_gain_one, g_shift_one, g_bias_qv, g_gain_two, g_shift_two, g_bias_out, g_bias_down, g_bias_up = qkv.last(
            finish_qkv_kernel, "finish_qkv", [(3 * model // 4, model)] + vectors
        )
        grad_w_qkv, grad_w_out, grad_w_down = grad_w_qkv.T, grad_w_out.T, grad_w_down.T
        return (
            output,
            grad_input,
            g_gain_one,
            g_shift_one,
            grad_w_qkv,
            g_bias_qv,
            grad_w_out,
            g_bias_out,
            g_gain_two,
            g_shift_two,
            grad_w_up,
            g_bias_up,
            grad_w_down,
            g_bias_down,
        )

    return on_device


def solution(mesh):
    return jax.shard_map(
        make(mesh),
        mesh=mesh,
        in_specs=(P("clip", "col", None), P("clip", "col", None), P("clip")) + (P(),) * 13,
        out_specs=(
            P("clip", "col", None),
            P("clip", "col", None),
            P("col"),
            P("col"),
            P(None, "col"),
            P("col"),
            P(None, "col"),
            P("col"),
            P("col"),
            P("col"),
            P(None, "col"),
            P("col"),
            P(None, "col"),
            P("col"),
        ),
        check_vma=False,
    )
```

```python
import functools
import jax
import jax.numpy as jnp
from jax import lax
from jax.experimental import pallas as pl
from jax.experimental.pallas import tpu as pltpu
from jax.sharding import PartitionSpec as P

HEADS = 12
EPSILON = 1e-06
MASKED = -1e30
F32 = jnp.float32
BF16 = jnp.bfloat16
INV_SQRT2 = 0.5**0.5
INV_SQRT_2PI = 0.3989422804014327
MIB = 1 << 20
PACE = 1_500_000
GAIN_ONE, SHIFT_ONE, BIAS_OUT, GAIN_TWO, SHIFT_TWO, BIAS_DOWN, BIAS_Q, BIAS_V, BIAS_UP = range(9)


def dot(left, right):
    return lax.dot_general(left, right, (((1,), (0,)), ((), ())), preferred_element_type=F32)


def dot_nt(left, right):
    return lax.dot_general(left, right, (((1,), (1,)), ((), ())), preferred_element_type=F32)


def add_low(left, right):
    return (left.astype(F32) + right.astype(F32)).astype(BF16)


def in_hbm(array):
    return pltpu.with_memory_space_constraint(array, pltpu.HBM)


def whole(shape):
    return pl.BlockSpec(shape, lambda *_: (0,) * len(shape), pipeline_mode=pl.Buffered(1))


def lanes(rows, size):
    return pl.BlockSpec((rows, size), lambda f, *_: (0, f))


def tokens_of(size, columns):
    return pl.BlockSpec((size, columns), lambda f, *_: (f, 0))


def params(limit, steps=1):
    return pltpu.CompilerParams(
        vmem_limit_bytes=limit * MIB, dimension_semantics=("arbitrary",) * steps
    )


def cost(micros):
    return pl.CostEstimate(flops=0, bytes_accessed=int(micros * PACE), transcendentals=0)


def standardise(value):
    centred = value - jnp.mean(value, axis=1, keepdims=True)
    root = lax.rsqrt(jnp.mean(centred * centred, axis=1, keepdims=True) + EPSILON)
    return centred * root, root


def standardise_back(grad, gain, xhat, root):
    scaled = grad * gain
    first = jnp.mean(scaled, axis=1, keepdims=True)
    second = jnp.mean(scaled * xhat, axis=1, keepdims=True)
    return root * (scaled - first - xhat * second)


def lane_sums(value):
    total = value[:, :128]
    for at in range(128, value.shape[1], 128):
        total = total + value[:, at : at + 128]
    return total


def row_sum(value):
    return jnp.sum(value, axis=0, keepdims=True)


def pair_diagonal(upper, lower):
    zero = jnp.zeros_like(upper)
    return jnp.concatenate(
        [jnp.concatenate([upper, zero], axis=0), jnp.concatenate([zero, lower], axis=0)], axis=1
    )


def token_rows(pieces):
    return jnp.concatenate([piece[0] for piece in pieces], axis=0)


def pairs_and_blocks(size, block, stages):
    if size == block:
        for stage in stages:
            for pair in range(HEADS // 2):
                stage(pair, 0, pair)
    else:

        @pl.loop(0, HEADS // 2 * (size // block))
        def _(step):
            blocks = size // block
            pair = step // blocks
            for stage in stages:
                stage(pair, pl.multiple_of((step - pair * blocks) * block, block), 0)


def slots(size, block):
    return HEADS // 2 if size == block else 1


def mask_lanes(ranks, length, target):
    target[...] = jnp.broadcast_to(jnp.where(ranks[...] < length, 0.0, MASKED), target.shape)


def across(value, width):
    return jnp.concatenate([value] * (width // value.shape[1]), axis=1)


def _(step):
            blocks = size // block
            pair = step // blocks
            one(pair, pl.multiple_of((step - pair * blocks) * block, block))


def attend_kernel(ncol, block, first, info, lens, *refs):
    pieces = refs[:ncol]
    ranks, vecs, w_qkv, w_out = refs[ncol : ncol + 4]
    qkv_t, mixed_t, middle_n, lse, mixed_f, keys_n, mask, scores, probs, inverse = refs[-10:]
    size, model = middle_n.shape
    head = model // HEADS
    rows = token_rows(pieces).astype(F32)
    xhat, _ = standardise(rows)
    normed = (xhat * vecs[GAIN_ONE : GAIN_ONE + 1] + vecs[SHIFT_ONE : SHIFT_ONE + 1]).astype(BF16)
    queries = dot(normed, w_qkv[:, :model]) + vecs[BIAS_Q : BIAS_Q + 1]
    qkv_t[:model] = queries.T.astype(BF16) * BF16(head**-0.5)
    keys = dot(normed, w_qkv[:, model : 2 * model])
    keys_n[...] = keys.astype(BF16)
    qkv_t[model : 2 * model] = keys.T.astype(BF16)
    values = dot(normed, w_qkv[:, 2 * model :]) + vecs[BIAS_V : BIAS_V + 1]
    qkv_t[2 * model :] = values.T.astype(BF16)
    mask_lanes(ranks, lens[first + pl.program_id(0)], mask)

    def begin(pair, at, slot):
        low, high = pair * 2 * head, (pair * 2 + 1) * head
        where = pl.ds(at, block)
        right = pair_diagonal(qkv_t[pl.ds(low, head), where], qkv_t[pl.ds(high, head), where])
        scores[slot] = dot(keys_n[:, pl.ds(low, 2 * head)], right)

    def weigh(pair, at, slot):
        value = scores[slot] + across(mask[...], 2 * block)
        top = jnp.max(value, axis=0, keepdims=True)
        weight = jnp.exp(value - top)
        total = jnp.sum(weight, axis=0, keepdims=True)
        probs[slot] = weight.astype(BF16)
        inverse[slot] = 1.0 / total
        stats = top + jnp.log(total)
        for side in range(2):
            lse[0, pl.ds(pair * 2 + side, 1), pl.ds(at, block)] = stats[:, side * block : (side + 1) * block]

    def mix(pair, at, slot):
        for side in range(2):
            start, cut = (pair * 2 + side) * head, slice(side * block, (side + 1) * block)
            value = qkv_t[pl.ds(2 * model + start, head), :]
            mixed_f[pl.ds(start, head), pl.ds(at, block)] = dot(value, probs[slot, :, cut]) * inverse[slot, :, cut]

    pairs_and_blocks(size, block, (begin, weigh, mix))
    mixed_t[...] = mixed_f[...].astype(BF16)
    middle = rows + dot(mixed_f[...].T.astype(BF16), w_out[...]) + vecs[BIAS_OUT : BIAS_OUT + 1]
    middle_n[...] = middle


def attend_call(info, lens, pieces, ranks, vecs, w_qkv, w_out, first, frames, per, earlier=()):
    ncol = len(pieces)
    width, model = pieces[1].shape[1:]
    size = ncol * width
    tokens = per * size
    block = min(size, 256)
    own = pl.BlockSpec((1, width, model), lambda f, info, *_: (info[0] * per + first + f, 0, 0))
    other = pl.BlockSpec((1, width, model), lambda f, *_: (f, 0, 0))

    def rows_of(columns):
        return pl.BlockSpec((size, columns), lambda f, *_: (first + f, 0))

    def lanes_of(rows):
        return pl.BlockSpec((rows, size), lambda f, *_: (0, first + f))

    return pl.pallas_call(
        functools.partial(attend_kernel, ncol, block, first),
        grid_spec=pltpu.PrefetchScalarGridSpec(
            num_scalar_prefetch=2,
            grid=(frames,),
            in_specs=[own]
            + [other] * (ncol - 1)
            + [whole(ranks.shape), whole(vecs.shape), whole(w_qkv.shape), whole(w_out.shape)]
            + [pl.BlockSpec(memory_space=pl.ANY)] * len(earlier),
            out_specs=[
                lanes_of(3 * model),
                lanes_of(model),
                rows_of(model),
                pl.BlockSpec((1, 16, size), lambda f, *_: (first + f, 0, 0)),
            ],
            scratch_shapes=[
                pltpu.VMEM((model, size), F32),
                pltpu.VMEM((size, model), BF16),
                pltpu.VMEM((size, 128), F32),
                pltpu.VMEM((slots(size, block), size, 2 * block), F32),
                pltpu.VMEM((slots(size, block), size, 2 * block), BF16),
                pltpu.VMEM((slots(size, block), 1, 2 * block), F32),
            ],
        ),
        out_shape=[
            pltpu.HBM((3 * model, tokens), BF16),
            pltpu.HBM((model, tokens), BF16),
            pltpu.HBM((tokens, model), F32),
            pltpu.HBM((per, 16, size), F32),
        ],
        input_output_aliases={ncol + 6 + i: i for i in range(len(earlier))},
        compiler_params=params(40),
        cost_estimate=cost(10),
        name="attend",
    )(info, lens, *pieces, ranks, vecs, in_hbm(w_qkv), in_hbm(w_out), *earlier)


def gather_tokens(pieces, target):
    frames, width = pieces[1].shape[:2]
    at = 0
    for f in range(frames):
        for piece in pieces:
            target[at : at + width] = piece[f]
            at += width


def halves_apart(info, value):
    first, chunk = info[1] == 0, value.shape[1] // 2
    low, high = value[:, :chunk], value[:, chunk:]
    return jnp.where(first, low, high), jnp.where(first, high, low)


def mlp_kernel(ncol, info, *refs):
    own_in, *pieces_in = refs[:ncol]
    middle_n, mixed_in, vecs, w_up, w_down = refs[ncol : ncol + 5]
    outs = refs[ncol + 5 : 2 * ncol + 5]
    gmiddle_out, sums, down_keep, down_send, up_keep, up_send = refs[2 * ncol + 5 : 2 * ncol + 11]
    (
        cot_p, cot_n, cot_t, second_n, second_t, active_n, hidden_n, total, grad, mixed_t, up_slots, down_slots, out_slots,
        in_sems, up_sems, down_sems, out_sems, g_sems,
    ) = refs[2 * ncol + 11 :]
    tokens, model = total.shape
    frames, width = outs[0].shape[:2]
    part = model // 4
    rows = min(tokens, 256)
    step, steps = pl.program_id(0), pl.num_programs(0) - 1
    gain = vecs[GAIN_TWO : GAIN_TWO + 1]
    coming = [
        pltpu.make_async_copy(own_in.at[pl.ds(info[0] * frames, frames)], cot_p.at[0], in_sems.at[0]),
        *[pltpu.make_async_copy(p, cot_p.at[i + 1], in_sems.at[i + 1]) for i, p in enumerate(pieces_in)],
        pltpu.make_async_copy(mixed_in, mixed_t, in_sems.at[ncol]),
    ]

    def down_copy(j):
        target = down_keep if j >= 2 else down_send
        return pltpu.make_async_copy(down_slots.at[j], target.at[:, pl.ds(j % 2 * part, part), :], down_sems.at[j])

    def up_copies(j, block):
        return [
            pltpu.make_async_copy(up_slots.at[side, j], target.at[block, pl.ds(0, model), :], up_sems.at[side, j])
            for side, target in enumerate((up_keep, up_send))
        ]

    @pl.when(step == 0)
    def _():
        for copy in coming:
            copy.start()
        sums[...] = jnp.zeros_like(sums)
        for at in range(0, tokens, rows):
            cut = slice(at, at + rows)
            middle = middle_n[cut]
            xhat, _ = standardise(middle)
            second = xhat * gain + vecs[SHIFT_TWO : SHIFT_TWO + 1]
            second_n[cut] = second.astype(BF16)
            second_t[:, cut] = second.T.astype(BF16)
            total[cut] = middle + vecs[BIAS_DOWN : BIAS_DOWN + 1]
            grad[cut] = jnp.zeros((rows, model), F32)
        for copy in coming[:ncol]:
            copy.wait()
        gather_tokens([cot_p.at[i] for i in range(ncol)], cot_n)
        cot_t[...] = cot_n[...].astype(F32).T.astype(BF16)

    @pl.when(step < steps)
    def _():
        block = block_of(step, info)
        bias = vecs[pl.ds(BIAS_UP + block, 1), :]
        for at in range(0, tokens, rows):
            cut = slice(at, at + rows)
            hidden = dot(second_n[cut], w_up[...]) + bias
            half = 0.5 + 0.5 * lax.erf(hidden * INV_SQRT2)
            active = (hidden * half).astype(BF16)
            bell = jnp.exp(hidden * hidden * -0.5) * INV_SQRT_2PI
            slope = half + hidden * bell
            active_n[cut] = active
            total[cut] += dot(active, w_down[...])
            low = (dot_nt(cot_n[cut], w_down[...]) * slope).astype(BF16)
            hidden_n[cut] = low
            sums[pl.ds(4 + block, 1), :] += row_sum(low.astype(F32))
            grad[cut] += dot_nt(low, w_up[...])
        result = dot(cot_t[...], active_n[...]).astype(BF16)
        for c in range(4):
            down_slots[step, c] = result[c * part : (c + 1) * part]
        up_slots[0, step], up_slots[1, step] = halves_apart(info, dot(second_t[...], hidden_n[...]).astype(BF16))
        for copy in up_copies(step, block):
            copy.start()

    for j in range(4):

        @pl.when(step == j)
        def _(j=j):
            down_copy(j).start()

    @pl.when(step == steps)
    def _():
        at = 0
        for f in range(frames):
            for out in outs:
                out[f] = total[at : at + width].astype(BF16)
                at += width
        going = []
        for i, at in enumerate(range(0, tokens, rows)):
            cut = slice(at, at + rows)
            xhat, root = standardise(middle_n[cut])
            cot_f32, back = cot_n[cut].astype(F32), grad[cut]
            grad_middle = cot_f32 + standardise_back(back, gain, xhat, root)
            total[cut] = grad_middle
            copy = pltpu.make_async_copy(total.at[pl.ds(at, rows)], gmiddle_out.at[pl.ds(at, rows)], g_sems.at[i])
            copy.start()
            going.append(copy)
            low = grad_middle.astype(BF16)
            hidden_n[cut] = low
            sums[0:1] += row_sum(back * xhat)
            sums[1:2] += row_sum(back)
            sums[2:3] += row_sum(low.astype(F32))
            sums[3:4] += row_sum(cot_f32)
        coming[ncol].wait()
        both = halves_apart(info, dot(mixed_t[...], hidden_n[...]).T.astype(BF16))
        for side, target in enumerate((up_keep, up_send)):
            for c in range(4):
                out_slots[side, c] = both[side][c * part : (c + 1) * part]
                copy = pltpu.make_async_copy(out_slots.at[side, c], target.at[c, pl.ds(model, part), :], out_sems.at[side, c])
                copy.start()
                going.append(copy)
        for j in range(4):
            going += [down_copy(j), *up_copies(j, block_of(j, info))]
        for copy in going:
            copy.wait()


def block_of(step, info):
    return lax.bitwise_xor(step // 2, 1 - info[1]) * 2 + step % 2


def mlp_call(info, pieces, middle_n, mixed_t, vecs, w_up, w_down):
    ncol = len(pieces)
    piece = pieces[1].shape
    tokens, model = middle_n.shape
    steps = w_down.shape[0] // model
    part, chunk = model // 4, model // 2
    rows = min(tokens, 256)
    stays = pl.BlockSpec(memory_space=pltpu.HBM)

    def block(j, info):
        return block_of(jnp.minimum(j, steps - 1), info)

    down, up = (4, 2 * part, model), (steps, model + part, chunk)
    return pl.pallas_call(
        functools.partial(mlp_kernel, ncol),
        grid_spec=pltpu.PrefetchScalarGridSpec(
            num_scalar_prefetch=1,
            grid=(steps + 1,),
            in_specs=[stays] * ncol
            + [
                whole(middle_n.shape),
                stays,
                whole(vecs.shape),
                pl.BlockSpec((model, model), lambda j, info: (0, block(j, info))),
                pl.BlockSpec((model, model), lambda j, info: (block(j, info), 0)),
            ],
            out_specs=[whole(piece)] * ncol + [stays, whole((16, model))] + [stays] * 4,
            scratch_shapes=[
                pltpu.VMEM((ncol,) + piece, BF16),
                pltpu.VMEM((tokens, model), BF16),
                pltpu.VMEM((model, tokens), BF16),
                pltpu.VMEM((tokens, model), BF16),
                pltpu.VMEM((model, tokens), BF16),
                pltpu.VMEM((tokens, model), BF16),
                pltpu.VMEM((tokens, model), BF16),
                pltpu.VMEM((tokens, model), F32),
                pltpu.VMEM((tokens, model), F32),
                pltpu.VMEM((model, tokens), BF16),
                pltpu.VMEM((2, steps, model, chunk), BF16),
                pltpu.VMEM((steps, 4, part, model), BF16),
                pltpu.VMEM((2, 4, part, chunk), BF16),
                pltpu.SemaphoreType.DMA((ncol + 1,)),
                pltpu.SemaphoreType.DMA((2, steps)),
                pltpu.SemaphoreType.DMA((steps,)),
                pltpu.SemaphoreType.DMA((2, 4)),
                pltpu.SemaphoreType.DMA((tokens // rows,)),
            ],
        ),
        out_shape=[pltpu.HBM(piece, BF16)] * ncol
        + [pltpu.HBM((tokens, model), F32), jax.ShapeDtypeStruct((16, model), F32)]
        + [pltpu.HBM(s, BF16) for s in (down, down, up, up)],
        compiler_params=params(60),
        cost_estimate=cost(40),
        name="mlp",
    )(info, *[in_hbm(p) for p in pieces], in_hbm(middle_n), in_hbm(mixed_t), vecs, in_hbm(w_up), in_hbm(w_down))


def attend_back_kernel(ncol, block, first, info, lens, *refs):
    pieces = refs[:ncol]
    ranks, vecs, w_qkv_in, w_out, qkv_t, lse, mixed_t, gmiddle_n = refs[ncol : ncol + 8]
    gproj_t, normed_n, sums, *outs = refs[-15 - ncol : -12]
    gmixed_t, gacc, columns, kv_n, mask, scores, gprobs, probs, gscores, inner, w_qkv, sem = refs[-12:]
    size, model = gmiddle_n.shape
    head = model // HEADS
    step = pl.program_id(0)

    coming = pltpu.make_async_copy(w_qkv_in, w_qkv, sem.at[0])

    @pl.when(step == 0)
    def _():
        coming.start()
        sums[...] = jnp.zeros_like(sums)
        columns[...] = jnp.zeros_like(columns)

    gmixed_t[...] = dot_nt(w_out[...], gmiddle_n[...].astype(BF16)).astype(BF16)
    kv_n[...] = qkv_t[model:].astype(F32).T.astype(BF16)
    mask_lanes(ranks, lens[first + step], mask)
    product = gmixed_t[...].astype(F32) * mixed_t[...].astype(F32)
    for h in range(HEADS):
        inner[h : h + 1] = row_sum(product[h * head : (h + 1) * head])
    many = size != block
    if many:
        gacc[...] = jnp.zeros_like(gacc)

    def begin(pair, at, slot):
        low, high = pair * 2 * head, (pair * 2 + 1) * head
        where = pl.ds(at, block)
        right = pair_diagonal(qkv_t[pl.ds(low, head), where], qkv_t[pl.ds(high, head), where])
        scores[slot] = dot(kv_n[:, pl.ds(low, 2 * head)], right)
        right = pair_diagonal(gmixed_t[pl.ds(low, head), where], gmixed_t[pl.ds(high, head), where])
        gprobs[slot] = dot(kv_n[:, pl.ds(model + low, 2 * head)], right)

    def weigh(pair, at, slot):
        where = pl.ds(at, block)
        stats, means = (
            jnp.concatenate([rows[pl.ds(pair * 2 + i, 1), where] for i in range(2)], axis=1) for rows in (lse.at[0], inner)
        )
        value = jnp.exp(scores[slot] + across(mask[...], 2 * block) - stats)
        probs[slot] = value.astype(BF16)
        gscores[slot] = (value * (gprobs[slot] - means)).astype(BF16)

    def spread(pair, at, slot):
        where = pl.ds(at, block)
        for side in range(2):
            start, cut = (pair * 2 + side) * head, slice(side * block, (side + 1) * block)
            grad_side = gscores[slot, :, cut]
            grad_q = dot(qkv_t[pl.ds(model + start, head), :], grad_side) * head**-0.5
            grad_k = dot_nt(qkv_t[pl.ds(start, head), where], grad_side)
            grad_v = dot_nt(gmixed_t[pl.ds(start, head), where], probs[slot, :, cut])
            gproj_t[pl.ds(start, head), where] = grad_q.astype(BF16)
            if many:
                gacc[pl.ds(start, head), :] += grad_k
                gacc[pl.ds(model + start, head), :] += grad_v
            else:
                gproj_t[pl.ds(model + start, head), :] = grad_k.astype(BF16)
                gproj_t[pl.ds(2 * model + start, head), :] = grad_v.astype(BF16)

    pairs_and_blocks(size, block, (begin, weigh, spread))
    if many:
        gproj_t[model:] = gacc[...].astype(BF16)
    columns[:model] += lane_sums(gproj_t[:model].astype(F32))
    columns[model:] += lane_sums(gproj_t[2 * model :].astype(F32))

    @pl.when(step == 0)
    def _():
        coming.wait()

    grad = dot(w_qkv[...], gproj_t[...]).T
    xhat, root = standardise(token_rows(pieces).astype(F32))
    gain = vecs[GAIN_ONE : GAIN_ONE + 1]
    normed_n[...] = (xhat * gain + vecs[SHIFT_ONE : SHIFT_ONE + 1]).astype(BF16)
    sums[0:1] += row_sum(grad * xhat)
    sums[1:2] += row_sum(grad)
    total = gmiddle_n[...] + standardise_back(grad, gain, xhat, root)
    result = total.astype(BF16)
    width = size // ncol
    for k in range(ncol):
        outs[k][0] = result[k * width : (k + 1) * width]

    @pl.when(step == pl.num_programs(0) - 1)
    def _():
        for i in range(2):
            sums[2 + i : 3 + i] = row_sum(columns[i * model : (i + 1) * model].T)


def attend_back_call(
    info, lens, pieces, ranks, vecs, w_qkv, w_out, qkv_t, lse, mixed_t, gmiddle_n, first, frames, per, earlier=()
):
    ncol = len(pieces)
    width, model = pieces[1].shape[1:]
    size = ncol * width
    tokens = per * size
    block = min(size, 256)
    acc = (2 * model, size) if size != block else (8, 128)

    def later(spec_lanes, shape):
        if spec_lanes:
            return pl.BlockSpec(shape, lambda f, *_: (0, first + f))
        return pl.BlockSpec(shape, lambda f, *_: (first + f,) + (0,) * (len(shape) - 1))

    own = pl.BlockSpec((1, width, model), lambda f, info, *_: (info[0] * per + first + f, 0, 0))
    piece = later(False, (1, width, model))
    return pl.pallas_call(
        functools.partial(attend_back_kernel, ncol, block, first),
        grid_spec=pltpu.PrefetchScalarGridSpec(
            num_scalar_prefetch=2,
            grid=(frames,),
            in_specs=[own]
            + [piece] * (ncol - 1)
            + [
                whole(ranks.shape),
                whole(vecs.shape),
                pl.BlockSpec(memory_space=pltpu.HBM),
                whole(w_out.shape),
                later(True, (3 * model, size)),
                later(False, (1, 16, size)),
                later(True, (model, size)),
                later(False, (size, model)),
            ]
            + [pl.BlockSpec(memory_space=pl.ANY)] * len(earlier),
            out_specs=[later(True, (3 * model, size)), later(False, (size, model)), whole((16, model))] + [piece] * ncol,
            scratch_shapes=[
                pltpu.VMEM((model, size), BF16),
                pltpu.VMEM(acc, F32),
                pltpu.VMEM((2 * model, 128), F32),
                pltpu.VMEM((size, 2 * model), BF16),
                pltpu.VMEM((size, 128), F32),
                pltpu.VMEM((slots(size, block), size, 2 * block), F32),
                pltpu.VMEM((slots(size, block), size, 2 * block), F32),
                pltpu.VMEM((slots(size, block), size, 2 * block), BF16),
                pltpu.VMEM((slots(size, block), size, 2 * block), BF16),
                pltpu.VMEM((16, size), F32),
                pltpu.VMEM(w_qkv.shape, BF16),
                pltpu.SemaphoreType.DMA((1,)),
            ],
        ),
        out_shape=[
            pltpu.HBM((3 * model, tokens), BF16),
            pltpu.HBM((tokens, model), BF16),
            pltpu.HBM((16, model), F32),
        ]
        + [pltpu.HBM((per, width, model), BF16)] * ncol,
        input_output_aliases={ncol + 10 + i: i + (i > 1) for i in range(len(earlier))},
        compiler_params=params(40 if size == block else 62),
        cost_estimate=cost(15),
        name="attend_back",
    )(info, lens, *pieces, ranks, vecs, in_hbm(w_qkv), in_hbm(w_out), in_hbm(qkv_t), lse, in_hbm(mixed_t), in_hbm(gmiddle_n), *earlier)


def take_kernel(info, *refs):
    half = len(refs) // 2
    for source, target in zip(refs[:half], refs[half:]):
        target[...] = source[...]


def take_frames(info, array, ncol, group=0, groups=1):
    per = array.shape[0] // ncol // groups
    shape = (per,) + array.shape[1:]
    specs = [
        pl.BlockSpec(shape, lambda i, info, k=k: (lax.bitwise_xor(info[0], k) * groups + group, 0, 0))
        for k in range(1, ncol)
    ]
    return pl.pallas_call(
        take_kernel,
        grid_spec=pltpu.PrefetchScalarGridSpec(
            num_scalar_prefetch=1,
            grid=(1,),
            in_specs=specs,
            out_specs=[pl.BlockSpec(shape, lambda i, *_: (0, 0, 0))] * (ncol - 1),
        ),
        out_shape=[pltpu.HBM(shape, array.dtype)] * (ncol - 1),
        compiler_params=params(8),
        cost_estimate=cost(1),
        name="take_frames",
    )(info, *[in_hbm(array)] * (ncol - 1))


def place_kernel(info, *refs):
    *pieces, out = refs
    for k, piece in enumerate(pieces):

        @pl.when(pl.program_id(0) == k)
        def _(piece=piece):
            out[...] = piece[...].astype(out.dtype)


def place_frames(info, pieces, dtype):
    shape = pieces[0].shape
    return pl.pallas_call(
        place_kernel,
        grid_spec=pltpu.PrefetchScalarGridSpec(
            num_scalar_prefetch=1,
            grid=(len(pieces),),
            in_specs=[whole(shape)] * len(pieces),
            out_specs=pl.BlockSpec(shape, lambda k, info: (lax.bitwise_xor(info[0], k), 0, 0)),
        ),
        out_shape=pltpu.HBM((len(pieces) * shape[0],) + shape[1:], dtype),
        compiler_params=params(12),
        cost_estimate=cost(2),
        name="place_frames",
    )(info, *pieces)


def pick(array, index, axis):
    return lax.dynamic_index_in_dim(array, index, axis, keepdims=False)


class Comm:
    def __init__(self, mesh):
        self.ncol = mesh.shape["col"]
        self.nclip = mesh.shape["clip"]
        self.nz = self.nclip // 2
        self.me = lax.axis_index("col")
        self.clip = lax.axis_index("clip")
        self.core = lax.rem(self.clip, 2)
        self.z = lax.div(self.clip, 2)

    def col_swap(self, array, distance):
        return lax.ppermute(array, "col", [(i, i ^ distance) for i in range(self.ncol)])

    def core_swap(self, array):
        return lax.ppermute(array, "clip", [(i, i ^ 1) for i in range(self.nclip)])

    def z_move(self, array, pairs):
        moves = [(2 * a + c, 2 * b + c) for a, b in pairs for c in range(2)]
        return lax.ppermute(array, "clip", moves)

    def z_swap(self, array, distance):
        return lax.ppermute(array, "clip", [(i, i ^ (2 * distance)) for i in range(self.nclip)])

    def halve(self, terms, bits):
        nbits = self.ncol.bit_length() - 1
        present = list(range(nbits - 1, -1, -1))
        for bit in bits:
            axis = present.index(bit)
            mine = lax.rem(lax.shift_right_logical(self.me, bit), 2)
            away = [pick(t, 1 - mine, axis) for t in terms]
            total = away[0]
            if len(away) > 1:
                total = add_low(away[0], away[1])
            landed = self.col_swap(total, 1 << bit)
            near = [pick(t, mine, axis) for t in terms]
            if len(near) > 1:
                near = [add_low(near[0], near[1])]
            terms = [near[0], landed]
            present.pop(axis)
        return add_low(terms[0], terms[1])

    def reduce_rows(self, grad):
        rows, depth = grad.shape
        part = rows // self.ncol // 4
        nbits = self.ncol.bit_length() - 1
        split = grad.reshape(self.ncol, 2, 2, part, depth)
        keep = pick(split, self.core, 1)
        landed = self.core_swap(pick(split, 1 - self.core, 1))
        order = list(range(nbits))
        half = nbits // 2
        orders = (order, order[half:] + order[:half])
        done = []
        for side in range(2):
            terms = [
                t[:, side].reshape((2,) * nbits + (part, depth)) for t in (keep, landed)
            ]
            done.append(self.halve(terms, orders[side]))
        total = jnp.concatenate(done, axis=0)
        total = self.sum_line(total)
        other = self.core_swap(total)
        first = self.core == 0
        return jnp.concatenate(
            [jnp.where(first, total, other), jnp.where(first, other, total)], axis=0
        )

    def sum_line(self, total):
        nz = self.nz
        for step in range(nz // 2 - 1):
            total = add_low(total, self.z_move(total, [(step, step + 1), (nz - 1 - step, nz - 2 - step)]))
        low, high = nz // 2 - 1, nz // 2
        total = add_low(total, self.z_move(total, [(low, high), (high, low)]))
        for step in range(nz // 2 - 1, 0, -1):
            landed = self.z_move(total, [(step, step - 1), (nz - 1 - step, nz - step)])
            takes = jnp.logical_or(self.z == step - 1, self.z == nz - step)
            total = jnp.where(takes, landed, total)
        return total


def qkv_kernel(info, gproj_t, normed_n, mlp_sums, *refs):
    *att, keep, send, total, vectors = refs
    c = pl.program_id(0)
    model = mlp_sums.shape[1]
    rows = total.shape[0] // 2
    part = model // 4
    total[...] = dot(gproj_t[...], normed_n[...])

    for i in range(4):

        @pl.when(c == i)
        def _(i=i):
            att_sums = att[0][...]
            for more in att[1:]:
                att_sums = att_sums + more[...]
            vectors[...] = jnp.zeros_like(vectors)
            vectors[0, 0:4, :part] = mlp_sums[0:4, i * part : (i + 1) * part]
            vectors[0, 4:5, :] = mlp_sums[4 + i : 5 + i]
            vectors[1, 0:2, :part] = att_sums[0:2, i * part : (i + 1) * part]
            start = i % 2 * 2 * part
            vectors[1, 2:3, : 2 * part] = att_sums[2 + i // 2 : 3 + i // 2, start : start + 2 * part]

    for side, target in enumerate((keep, send)):
        which = lax.bitwise_xor(info[1], side)
        target[0, :rows] = total[pl.ds(pl.multiple_of(which * rows, rows), rows), :].astype(BF16)
        target[0, rows:] = vectors[which].astype(BF16)


VECTOR_ROWS = 32


def qkv_call(info, gproj_t, normed_n, mlp_sums, att_sums):
    model = mlp_sums.shape[1]
    rows = 3 * model // 4
    block = (1, rows // 2 + VECTOR_ROWS, model)
    out = jax.ShapeDtypeStruct((4,) + block[1:], BF16)
    others = (normed_n, mlp_sums, *att_sums)
    return pl.pallas_call(
        qkv_kernel,
        grid_spec=pltpu.PrefetchScalarGridSpec(
            num_scalar_prefetch=1,
            grid=(4,),
            in_specs=[pl.BlockSpec((rows, gproj_t.shape[1]), lambda c, info: (c, 0))]
            + [whole(o.shape) for o in others],
            out_specs=[pl.BlockSpec(block, lambda c, info: (c, 0, 0))] * 2,
            scratch_shapes=[pltpu.VMEM((rows, model), F32), pltpu.VMEM((2, VECTOR_ROWS, model), F32)],
        ),
        out_shape=[out, out],
        compiler_params=params(24),
        cost_estimate=cost(6),
        name="grad_qkv",
    )(info, in_hbm(gproj_t), in_hbm(normed_n), *others[1:])


def sum_core_kernel(info, *refs):
    for i in range(4):
        refs[8 + i][...] = add_low(refs[i][...], refs[4 + i][...])


def sum_core(info, keep, landed):
    rows, depth = keep.shape[1] // 2, keep.shape[2]
    block = (1, rows, depth)

    def by_x(i, info, flip, side):
        return (2 * i + lax.bitwise_xor(info[2], flip), side, 0)

    def by_y(i, info, flip, side):
        return (2 * lax.bitwise_xor(info[3], flip) + i, side, 0)

    specs = [
        pl.BlockSpec(block, functools.partial(lambda i, info, fn, flip, side: fn(i, info, flip, side), fn=fn, flip=flip, side=side))
        for side, fn in enumerate((by_x, by_y))
        for flip in (1, 0)
    ]
    out = jax.ShapeDtypeStruct((2, rows, depth), BF16)
    return pl.pallas_call(
        sum_core_kernel,
        grid_spec=pltpu.PrefetchScalarGridSpec(
            num_scalar_prefetch=1,
            grid=(2,),
            in_specs=specs * 2,
            out_specs=[pl.BlockSpec(block, lambda i, info: (i, 0, 0))] * 4,
        ),
        out_shape=[out] * 4,
        compiler_params=params(16),
        cost_estimate=cost(2),
        name="sum_core",
    )(info, *[keep] * 4, *[landed] * 4)


def sum_first_kernel(info, keep_a, land_a, keep_b, land_b, send_a, stay_a, send_b, stay_b):
    for keep, land, send, stay, mine in (
        (keep_a, land_a, send_a, stay_a, info[3]),
        (keep_b, land_b, send_b, stay_b, info[2]),
    ):
        send[...] = add_low(keep[1 - mine], land[1 - mine])
        stay[...] = add_low(keep[mine], land[mine])


def sum_first(info, keep_a, land_a, keep_b, land_b):
    rows, depth = keep_a.shape[1:]
    out = jax.ShapeDtypeStruct((rows, depth), BF16)
    return pl.pallas_call(
        sum_first_kernel,
        grid_spec=pltpu.PrefetchScalarGridSpec(
            num_scalar_prefetch=1,
            grid=(1,),
            in_specs=[whole(keep_a.shape)] * 4,
            out_specs=[whole((rows, depth))] * 4,
        ),
        out_shape=[out] * 4,
        compiler_params=params(16),
        cost_estimate=cost(1),
        name="sum_first",
    )(info, keep_a, land_a, keep_b, land_b)


def sum_second_kernel(info, stay_a, land_a, stay_b, land_b, own, send):
    low, high = add_low(stay_a[...], land_a[...]), add_low(stay_b[...], land_b[...])
    own[...] = jnp.where(info[4] == 0, low, high)
    send[...] = jnp.where(info[4] == 0, high, low)


def sum_second(info, stay_a, land_a, stay_b, land_b):
    shape = stay_a.shape
    return pl.pallas_call(
        sum_second_kernel,
        grid_spec=pltpu.PrefetchScalarGridSpec(
            num_scalar_prefetch=1, grid=(1,), in_specs=[whole(shape)] * 4, out_specs=[whole(shape)] * 2
        ),
        out_shape=[jax.ShapeDtypeStruct(shape, BF16)] * 2,
        compiler_params=params(16),
        cost_estimate=cost(1),
        name="sum_second",
    )(info, stay_a, land_a, stay_b, land_b)


def collect(info, parts, full):
    rows = parts[0].shape[0]
    for i, part in enumerate(parts):
        at = lax.bitwise_xor(info[4], i % 2) * rows
        full[lax.bitwise_xor(info[1], i // 2), pl.ds(pl.multiple_of(at, rows), rows), :] = part[...]


def finish_down_kernel(info, *refs):
    *parts, down_t, full = refs
    collect(info, parts, full)
    model, part = full.shape[2], down_t.shape[0]
    blocks = full.shape[1] // part
    for half in range(2):
        for j in range(blocks):
            at = (half * blocks + j) * model
            down_t[:, at : at + model] = full[half, j * part : (j + 1) * part].astype(F32)


def finish_up_kernel(info, *refs):
    *parts, up, out_t, full = refs
    collect(info, parts, full)
    model, chunk = up.shape[0], full.shape[2]
    for half in range(2):
        cut = slice(half * chunk, (half + 1) * chunk)
        up[:, cut] = full[half, :model].astype(F32)
        out_t[:, cut] = full[half, model:].astype(F32)


def finish_qkv_kernel(info, *refs):
    *parts, qkv_t, gain_one, shift_one, bias_qv, gain_two, shift_two, bias_out, bias_down, bias_up, full = refs
    collect(info, parts, full)
    rows = qkv_t.shape[0] // 2
    for half in range(2):
        qkv_t[half * rows : (half + 1) * rows] = full[half, :rows].astype(F32)
    mlp_rows = full[0, rows : rows + 16].astype(F32)
    att_rows = full[1, rows : rows + 16].astype(F32)
    for source, targets in ((mlp_rows, (gain_two, shift_two, bias_out, bias_down, bias_up)), (att_rows, (gain_one, shift_one, bias_qv))):
        for i, target in enumerate(targets):
            target[...] = source[i, : target.shape[0]]


def finish(kernel, name, info, parts, shapes):
    rows, depth = parts[0].shape
    return pl.pallas_call(
        kernel,
        grid_spec=pltpu.PrefetchScalarGridSpec(
            num_scalar_prefetch=1,
            grid=(1,),
            in_specs=[whole((rows, depth))] * 4,
            out_specs=[whole(s) for s in shapes],
            scratch_shapes=[pltpu.VMEM((2, 2 * rows, depth), BF16)],
        ),
        out_shape=[pltpu.HBM(s, F32) for s in shapes],
        compiler_params=params(24),
        cost_estimate=cost(2),
        name=name,
    )(info, *parts)


def wait_for(values, *others):
    flat, tree = jax.tree.flatten(values)
    held = lax.optimization_barrier((tuple(flat), others))[0]
    return jax.tree.unflatten(tree, held)


def join(*values):
    flat, tree = jax.tree.flatten(values)
    return jax.tree.unflatten(tree, lax.optimization_barrier(tuple(flat)))


def make(mesh):
    def on_device(
        frames,
        cotangent,
        frame_len,
        column_rank,
        gain_one,
        shift_one,
        w_qkv,
        bias_qv,
        w_out,
        bias_out,
        gain_two,
        shift_two,
        w_up,
        bias_up,
        w_down,
        bias_down,
    ):
        comm = Comm(mesh)
        ncol, me = comm.ncol, comm.me
        count, width, model = frames.shape
        hidden_size = w_down.shape[0]
        per = count // ncol
        size = ncol * width
        groups = 2 if per % 2 == 0 else 1
        part = per // groups
        middle_z = jnp.logical_or(comm.z == 1, comm.z == 2)
        info = jnp.stack([me, comm.core, lax.rem(me, 2), lax.div(me, 2), middle_z.astype(me.dtype)]).astype(jnp.int32)
        order = lax.bitwise_xor(me, jnp.arange(ncol, dtype=jnp.int32))
        ranks = column_rank.reshape(ncol, width)[order].reshape(size, 1)
        lens = pick(frame_len.reshape(ncol, per), me, 0)
        given = [gain_one, shift_one, bias_out, gain_two, shift_two, bias_down, bias_qv, bias_up]
        total, at, vecs = sum(v.size for v in given), 0, 0.0
        for v in given:
            vecs = vecs + jnp.pad(v.astype(F32), (at, total - at - v.size))
            at += v.size
        vecs = vecs.reshape(-1, model)

        def swap(pieces):
            return [comm.col_swap(p, k + 1) for k, p in enumerate(pieces)]

        paired = ncol == 4 and comm.nz == 4

        class Chunk:
            land = ()

            def core(self, keep, land):
                sa, self.ka, sb, self.kb = sum_core(info, keep, land)
                self.land = [comm.col_swap(sa, 1), comm.col_swap(sb, 2)]

            def first(self):
                sa, self.ka, sb, self.kb = sum_first(info, self.ka, self.land[0], self.kb, self.land[1])
                self.land = [comm.col_swap(sa, 2), comm.col_swap(sb, 1)]

            def second(self):
                self.own, send = sum_second(info, self.ka, self.land[0], self.kb, self.land[1])
                self.land = comm.z_swap(send, 1)

            def inner(self):
                self.own = add_low(self.own, self.land)
                self.land = comm.z_swap(self.own, 3)

            def outer(self):
                self.own = add_low(self.own, self.land)
                self.land = [comm.z_swap(self.own, 1), comm.core_swap(self.own)]

            def swap(self):
                self.parts = [self.own] + self.land
                self.land = comm.core_swap(self.parts[1])

            def last(self, kernel, name, shapes):
                return finish(kernel, name, info, self.parts + [self.land], shapes)

        landed = swap(take_frames(info, frames, ncol))
        cot_send = take_frames(info, cotangent, ncol)
        landed[0], cot_send, ranks, vecs, lens = join(landed[0], cot_send, ranks, vecs, lens)
        cot_land = swap(cot_send)
        rows = [frames, *join(*landed)]
        kept = attend_call(info, lens, rows, ranks, vecs, w_qkv, w_out, 0, per, per)
        kept, landed = join(kept, cot_land)
        qkv_t, mixed_t, middle_n, lse = kept
        cots = [cotangent, *landed]
        results = mlp_call(info, cots, middle_n, mixed_t, vecs, w_up, w_down)
        *outs, gmiddle_n, mlp_sums, down_keep, down_send, up_keep, up_send = join(*results)

        def back(gmiddle_n, g, earlier=()):
            return attend_back_call(
                info, lens, rows, ranks, vecs, w_qkv, w_out, qkv_t, lse, mixed_t, gmiddle_n, g * part, part, per, earlier
            )

        if not paired:
            out_land = swap(outs[1:])
            att_sums, earlier = 0.0, ()
            for g in range(groups):
                gproj_t, normed, sums, *gouts = back(gmiddle_n, g, earlier)
                att_sums, earlier = att_sums + sums, (gproj_t, normed, *gouts)
            output = place_frames(info, [outs[0]] + out_land, BF16)
            grad_input = place_frames(info, [gouts[0]] + swap(gouts[1:]), F32)
            first = comm.core == 0
            steps, part = hidden_size // model, model // 4

            def halves(keep, send):
                return jnp.stack([jnp.where(first, keep, send), jnp.where(first, send, keep)])

            def reduced(grad):
                return comm.reduce_rows(grad.astype(BF16)).astype(F32).T

            grad = halves(up_keep, up_send)
            grad_w_up = reduced(grad[:, :, :model].transpose(1, 0, 3, 2).reshape(hidden_size, model))
            grad_w_out = reduced(grad[:, :, model:].transpose(1, 2, 0, 3).reshape(model, model))
            grad = halves(down_keep, down_send).reshape(2, 4, steps // 2, part, model).transpose(1, 3, 0, 2, 4)
            grad_w_down = reduced(grad.reshape(model, hidden_size))
            grad_w_qkv = reduced(dot(gproj_t, normed))
            sums = jnp.concatenate([mlp_sums, att_sums])
            sums = reduced(jnp.concatenate([sums] * ncol)).T

            def own(row, rows=1):
                return pick(sums[row : row + rows].reshape(ncol, -1), me, 0)

            return (
                output, grad_input, own(16), own(17), grad_w_qkv, own(18, 2), grad_w_out, own(2), own(0), own(1),
                grad_w_up, own(4, steps), grad_w_down, own(3),
            )

        down, up, qkv = Chunk(), Chunk(), Chunk()
        down_land, up_land = comm.core_swap(down_send), comm.core_swap(up_send)
        down.core(down_keep, down_land)
        results = back(wait_for(gmiddle_n, down.ka), 0)
        down.land, up_land, results = join(down.land, up_land, results)
        gproj_t, normed, att_sums_a, *gouts = results

        down.first()
        up.core(up_keep, wait_for(up_land, down.ka))
        results = back(wait_for(gmiddle_n, up.ka), 1, (gproj_t, normed, *gouts))
        gproj_t, normed, att_sums_b, *gouts = results
        results_q = qkv_call(info, gproj_t, normed, mlp_sums, (att_sums_a, att_sums_b))
        down.land, up.land, gouts, results_q = join(down.land, up.land, gouts, results_q)
        qkv_keep, qkv_send = results_q

        qkv_land = comm.core_swap(qkv_send)
        up.land = wait_for(up.land, qkv_send)
        up.first()
        down.land = wait_for(down.land, up.ka)
        down.second()
        qkv_land, up.land, down.land, down.own, outs = join(qkv_land, up.land, down.land, down.own, outs)

        qkv.core(qkv_keep, qkv_land)
        down.land = wait_for(down.land, qkv.ka)
        down.inner()
        up.land = wait_for(up.land, down.own)
        up.second()
        qkv.land, up.land, down.own, up.own, outs = join(qkv.land, up.land, down.own, up.own, outs)

        qkv.first()
        up.land = wait_for(up.land, qkv.ka)
        up.inner()
        out_land = swap(outs[1:])
        qkv.land, down.land, down.own, up.own, gouts = join(qkv.land, down.land, down.own, up.own, gouts)

        qkv.second()
        gouts, down.land = wait_for((gouts, down.land), qkv.own)
        gin_land = swap(gouts[1:])
        down.outer()
        qkv.land, up.land, qkv.own, down.own = join(qkv.land, up.land, qkv.own, down.own)

        qkv.inner()
        up.land = wait_for(up.land, qkv.own)
        up.outer()
        qkv.land, down.land, out_land, gin_land, qkv.own, up.own = join(qkv.land, down.land, out_land, gin_land, qkv.own, up.own)

        qkv.outer()
        up.land = wait_for(up.land, qkv.own)
        up.swap()
        down.land = wait_for(down.land, up.parts[1])
        down.swap()
        output = place_frames(info, [outs[0], *wait_for(out_land, up.parts[1])], BF16)
        grad_input = place_frames(info, [gouts[0], *wait_for(gin_land, up.parts[1])], F32)
        down.parts, down.land = wait_for((down.parts, down.land), grad_input)
        (grad_w_down,) = down.last(finish_down_kernel, "finish_down", [(model // 4, hidden_size)])
        qkv.land, up.land, up.parts, qkv.own, output, grad_w_down = join(qkv.land, up.land, up.parts, qkv.own, output, grad_w_down)

        qkv.swap()
        up.parts, up.land = wait_for((up.parts, up.land), qkv.parts[0])
        grad_w_up, grad_w_out = up.last(
            finish_up_kernel, "finish_up", [(model, hidden_size // 4), (model // 4, model)]
        )
        qkv.land, qkv.parts, grad_w_up = join(qkv.land, qkv.parts, grad_w_up)
        part = model // 4
        vectors = [(part,), (part,), (2 * part,), (part,), (part,), (part,), (part,), (hidden_size // 4,)]
        grad_w_qkv, g_gain_one, g_shift_one, g_bias_qv, g_gain_two, g_shift_two, g_bias_out, g_bias_down, g_bias_up = qkv.last(
            finish_qkv_kernel, "finish_qkv", [(3 * model // 4, model)] + vectors
        )
        grad_w_qkv, grad_w_out, grad_w_down = grad_w_qkv.T, grad_w_out.T, grad_w_down.T
        return (
            output,
            grad_input,
            g_gain_one,
            g_shift_one,
            grad_w_qkv,
            g_bias_qv,
            grad_w_out,
            g_bias_out,
            g_gain_two,
            g_shift_two,
            grad_w_up,
            g_bias_up,
            grad_w_down,
            g_bias_down,
        )

    return on_device


def solution(mesh):
    return jax.shard_map(
        make(mesh),
        mesh=mesh,
        in_specs=(P("clip", "col", None), P("clip", "col", None), P("clip")) + (P(),) * 13,
        out_specs=(
            P("clip", "col", None),
            P("clip", "col", None),
            P("col"),
            P("col"),
            P(None, "col"),
            P("col"),
            P(None, "col"),
            P("col"),
            P("col"),
            P("col"),
            P(None, "col"),
            P("col"),
            P(None, "col"),
            P("col"),
        ),
        check_vma=False,
    )
```

```python
import functools
import jax
import jax.numpy as jnp
from jax import lax
from jax.experimental import pallas as pl
from jax.experimental.pallas import tpu as pltpu
from jax.sharding import PartitionSpec as P

HEADS = 12
EPSILON = 1e-06
MASKED = -1e30
F32 = jnp.float32
BF16 = jnp.bfloat16
INV_SQRT2 = 0.5**0.5
INV_SQRT_2PI = 0.3989422804014327
MIB = 1 << 20
PACE = 1_500_000
GAIN_ONE, SHIFT_ONE, BIAS_OUT, GAIN_TWO, SHIFT_TWO, BIAS_DOWN, BIAS_Q, BIAS_V, BIAS_UP = range(9)


def dot(left, right):
    return lax.dot_general(left, right, (((1,), (0,)), ((), ())), preferred_element_type=F32)


def dot_nt(left, right):
    return lax.dot_general(left, right, (((1,), (1,)), ((), ())), preferred_element_type=F32)


def add_low(left, right):
    return (left.astype(F32) + right.astype(F32)).astype(BF16)


def in_hbm(array):
    return pltpu.with_memory_space_constraint(array, pltpu.HBM)


def whole(shape):
    return pl.BlockSpec(shape, lambda *_: (0,) * len(shape), pipeline_mode=pl.Buffered(1))


def lanes(rows, size):
    return pl.BlockSpec((rows, size), lambda f, *_: (0, f))


def tokens_of(size, columns):
    return pl.BlockSpec((size, columns), lambda f, *_: (f, 0))


def params(limit, steps=1):
    return pltpu.CompilerParams(
        vmem_limit_bytes=limit * MIB, dimension_semantics=("arbitrary",) * steps
    )


def cost(micros):
    return pl.CostEstimate(flops=0, bytes_accessed=int(micros * PACE), transcendentals=0)


def standardise(value):
    centred = value - jnp.mean(value, axis=1, keepdims=True)
    root = lax.rsqrt(jnp.mean(centred * centred, axis=1, keepdims=True) + EPSILON)
    return centred * root, root


def standardise_back(grad, gain, xhat, root):
    scaled = grad * gain
    first = jnp.mean(scaled, axis=1, keepdims=True)
    second = jnp.mean(scaled * xhat, axis=1, keepdims=True)
    return root * (scaled - first - xhat * second)


def lane_sums(value):
    total = value[:, :128]
    for at in range(128, value.shape[1], 128):
        total = total + value[:, at : at + 128]
    return total


def row_sum(value):
    return jnp.sum(value, axis=0, keepdims=True)


def pair_diagonal(upper, lower):
    zero = jnp.zeros_like(upper)
    return jnp.concatenate(
        [jnp.concatenate([upper, zero], axis=0), jnp.concatenate([zero, lower], axis=0)], axis=1
    )


def token_rows(pieces):
    return jnp.concatenate([piece[0] for piece in pieces], axis=0)


def pairs_and_blocks(size, block, stages):
    if size == block:
        for stage in stages:
            for pair in range(HEADS // 2):
                stage(pair, 0, pair)
    else:

        @pl.loop(0, HEADS // 2 * (size // block))
        def _(step):
            blocks = size // block
            pair = step // blocks
            for stage in stages:
                stage(pair, pl.multiple_of((step - pair * blocks) * block, block), 0)


def slots(size, block):
    return HEADS // 2 if size == block else 1


def mask_lanes(ranks, length, target):
    target[...] = jnp.broadcast_to(jnp.where(ranks[...] < length, 0.0, MASKED), target.shape)


def across(value, width):
    return jnp.concatenate([value] * (width // value.shape[1]), axis=1)


def _(step):
            blocks = size // block
            pair = step // blocks
            one(pair, pl.multiple_of((step - pair * blocks) * block, block))


def attend_kernel(ncol, block, first, info, lens, *refs):
    pieces = refs[:ncol]
    ranks, vecs, w_qkv, w_out = refs[ncol : ncol + 4]
    qkv_t, mixed_t, middle_n, lse, mixed_f, keys_n, mask, scores, probs, inverse = refs[-10:]
    size, model = middle_n.shape
    head = model // HEADS
    rows = token_rows(pieces).astype(F32)
    xhat, _ = standardise(rows)
    normed = (xhat * vecs[GAIN_ONE : GAIN_ONE + 1] + vecs[SHIFT_ONE : SHIFT_ONE + 1]).astype(BF16)
    queries = dot(normed, w_qkv[:, :model]) + vecs[BIAS_Q : BIAS_Q + 1]
    qkv_t[:model] = queries.T.astype(BF16) * BF16(head**-0.5)
    keys = dot(normed, w_qkv[:, model : 2 * model])
    keys_n[...] = keys.astype(BF16)
    qkv_t[model : 2 * model] = keys.T.astype(BF16)
    values = dot(normed, w_qkv[:, 2 * model :]) + vecs[BIAS_V : BIAS_V + 1]
    qkv_t[2 * model :] = values.T.astype(BF16)
    mask_lanes(ranks, lens[first + pl.program_id(0)], mask)

    def begin(pair, at, slot):
        low, high = pair * 2 * head, (pair * 2 + 1) * head
        where = pl.ds(at, block)
        right = pair_diagonal(qkv_t[pl.ds(low, head), where], qkv_t[pl.ds(high, head), where])
        scores[slot] = dot(keys_n[:, pl.ds(low, 2 * head)], right)

    def weigh(pair, at, slot):
        value = scores[slot] + across(mask[...], 2 * block)
        top = jnp.max(value, axis=0, keepdims=True)
        weight = jnp.exp(value - top)
        total = jnp.sum(weight, axis=0, keepdims=True)
        probs[slot] = weight.astype(BF16)
        inverse[slot] = 1.0 / total
        stats = top + jnp.log(total)
        for side in range(2):
            lse[0, pl.ds(pair * 2 + side, 1), pl.ds(at, block)] = stats[:, side * block : (side + 1) * block]

    def mix(pair, at, slot):
        for side in range(2):
            start, cut = (pair * 2 + side) * head, slice(side * block, (side + 1) * block)
            value = qkv_t[pl.ds(2 * model + start, head), :]
            mixed_f[pl.ds(start, head), pl.ds(at, block)] = dot(value, probs[slot, :, cut]) * inverse[slot, :, cut]

    pairs_and_blocks(size, block, (begin, weigh, mix))
    mixed_t[...] = mixed_f[...].astype(BF16)
    middle = rows + dot(mixed_f[...].T.astype(BF16), w_out[...]) + vecs[BIAS_OUT : BIAS_OUT + 1]
    middle_n[...] = middle


def attend_call(info, lens, pieces, ranks, vecs, w_qkv, w_out, first, frames, per, earlier=()):
    ncol = len(pieces)
    width, model = pieces[1].shape[1:]
    size = ncol * width
    tokens = per * size
    block = min(size, 256)
    own = pl.BlockSpec((1, width, model), lambda f, info, *_: (info[0] * per + first + f, 0, 0))
    other = pl.BlockSpec((1, width, model), lambda f, *_: (f, 0, 0))

    def rows_of(columns):
        return pl.BlockSpec((size, columns), lambda f, *_: (first + f, 0))

    def lanes_of(rows):
        return pl.BlockSpec((rows, size), lambda f, *_: (0, first + f))

    return pl.pallas_call(
        functools.partial(attend_kernel, ncol, block, first),
        grid_spec=pltpu.PrefetchScalarGridSpec(
            num_scalar_prefetch=2,
            grid=(frames,),
            in_specs=[own]
            + [other] * (ncol - 1)
            + [whole(ranks.shape), whole(vecs.shape), whole(w_qkv.shape), whole(w_out.shape)]
            + [pl.BlockSpec(memory_space=pl.ANY)] * len(earlier),
            out_specs=[
                lanes_of(3 * model),
                lanes_of(model),
                rows_of(model),
                pl.BlockSpec((1, 16, size), lambda f, *_: (first + f, 0, 0)),
            ],
            scratch_shapes=[
                pltpu.VMEM((model, size), F32),
                pltpu.VMEM((size, model), BF16),
                pltpu.VMEM((size, 128), F32),
                pltpu.VMEM((slots(size, block), size, 2 * block), F32),
                pltpu.VMEM((slots(size, block), size, 2 * block), BF16),
                pltpu.VMEM((slots(size, block), 1, 2 * block), F32),
            ],
        ),
        out_shape=[
            pltpu.HBM((3 * model, tokens), BF16),
            pltpu.HBM((model, tokens), BF16),
            pltpu.HBM((tokens, model), F32),
            pltpu.HBM((per, 16, size), F32),
        ],
        input_output_aliases={ncol + 6 + i: i for i in range(len(earlier))},
        compiler_params=params(40),
        cost_estimate=cost(10),
        name="attend",
    )(info, lens, *pieces, ranks, vecs, in_hbm(w_qkv), in_hbm(w_out), *earlier)


def gather_tokens(pieces, target):
    frames, width = pieces[1].shape[:2]
    at = 0
    for f in range(frames):
        for piece in pieces:
            target[at : at + width] = piece[f]
            at += width


def halves_apart(info, value):
    first, chunk = info[1] == 0, value.shape[1] // 2
    low, high = value[:, :chunk], value[:, chunk:]
    return jnp.where(first, low, high), jnp.where(first, high, low)


def mlp_kernel(ncol, info, *refs):
    own_in, *pieces_in = refs[:ncol]
    middle_n, mixed_in, vecs, w_up, w_down = refs[ncol : ncol + 5]
    outs = refs[ncol + 5 : 2 * ncol + 5]
    gmiddle_out, sums, down_keep, down_send, up_keep, up_send = refs[2 * ncol + 5 : 2 * ncol + 11]
    (
        cot_p, cot_n, cot_t, second_n, second_t, active_n, hidden_n, total, grad, mixed_t, up_slots, down_slots, out_slots,
        in_sems, up_sems, down_sems, out_sems, g_sems,
    ) = refs[2 * ncol + 11 :]
    tokens, model = total.shape
    frames, width = outs[0].shape[:2]
    part = model // 4
    rows = min(tokens, 256)
    step, steps = pl.program_id(0), pl.num_programs(0) - 1
    gain = vecs[GAIN_TWO : GAIN_TWO + 1]
    coming = [
        pltpu.make_async_copy(own_in.at[pl.ds(info[0] * frames, frames)], cot_p.at[0], in_sems.at[0]),
        *[pltpu.make_async_copy(p, cot_p.at[i + 1], in_sems.at[i + 1]) for i, p in enumerate(pieces_in)],
        pltpu.make_async_copy(mixed_in, mixed_t, in_sems.at[ncol]),
    ]

    def down_copy(j):
        target = down_keep if j >= 2 else down_send
        return pltpu.make_async_copy(down_slots.at[j], target.at[:, pl.ds(j % 2 * part, part), :], down_sems.at[j])

    def up_copies(j, block):
        return [
            pltpu.make_async_copy(up_slots.at[side, j], target.at[block, pl.ds(0, model), :], up_sems.at[side, j])
            for side, target in enumerate((up_keep, up_send))
        ]

    @pl.when(step == 0)
    def _():
        for copy in coming:
            copy.start()
        sums[...] = jnp.zeros_like(sums)
        for at in range(0, tokens, rows):
            cut = slice(at, at + rows)
            middle = middle_n[cut]
            xhat, _ = standardise(middle)
            second = xhat * gain + vecs[SHIFT_TWO : SHIFT_TWO + 1]
            second_n[cut] = second.astype(BF16)
            second_t[:, cut] = second.T.astype(BF16)
            total[cut] = middle + vecs[BIAS_DOWN : BIAS_DOWN + 1]
            grad[cut] = jnp.zeros((rows, model), F32)
        for copy in coming[:ncol]:
            copy.wait()
        gather_tokens([cot_p.at[i] for i in range(ncol)], cot_n)
        cot_t[...] = cot_n[...].astype(F32).T.astype(BF16)

    @pl.when(step < steps)
    def _():
        block = block_of(step, info)
        bias = vecs[pl.ds(BIAS_UP + block, 1), :]
        for at in range(0, tokens, rows):
            cut = slice(at, at + rows)
            hidden = dot(second_n[cut], w_up[...]) + bias
            half = 0.5 + 0.5 * lax.erf(hidden * INV_SQRT2)
            active = (hidden * half).astype(BF16)
            bell = jnp.exp(hidden * hidden * -0.5) * INV_SQRT_2PI
            slope = half + hidden * bell
            active_n[cut] = active
            total[cut] += dot(active, w_down[...])
            low = (dot_nt(cot_n[cut], w_down[...]) * slope).astype(BF16)
            hidden_n[cut] = low
            sums[pl.ds(4 + block, 1), :] += row_sum(low.astype(F32))
            grad[cut] += dot_nt(low, w_up[...])
        result = dot(cot_t[...], active_n[...]).astype(BF16)
        for c in range(4):
            down_slots[step, c] = result[c * part : (c + 1) * part]
        up_slots[0, step], up_slots[1, step] = halves_apart(info, dot(second_t[...], hidden_n[...]).astype(BF16))
        for copy in up_copies(step, block):
            copy.start()

    for j in range(4):

        @pl.when(step == j)
        def _(j=j):
            down_copy(j).start()

    @pl.when(step == steps)
    def _():
        at = 0
        for f in range(frames):
            for out in outs:
                out[f] = total[at : at + width].astype(BF16)
                at += width
        going = []
        for i, at in enumerate(range(0, tokens, rows)):
            cut = slice(at, at + rows)
            xhat, root = standardise(middle_n[cut])
            cot_f32, back = cot_n[cut].astype(F32), grad[cut]
            grad_middle = cot_f32 + standardise_back(back, gain, xhat, root)
            total[cut] = grad_middle
            copy = pltpu.make_async_copy(total.at[pl.ds(at, rows)], gmiddle_out.at[pl.ds(at, rows)], g_sems.at[i])
            copy.start()
            going.append(copy)
            low = grad_middle.astype(BF16)
            hidden_n[cut] = low
            sums[0:1] += row_sum(back * xhat)
            sums[1:2] += row_sum(back)
            sums[2:3] += row_sum(low.astype(F32))
            sums[3:4] += row_sum(cot_f32)
        coming[ncol].wait()
        both = halves_apart(info, dot(mixed_t[...], hidden_n[...]).T.astype(BF16))
        for side, target in enumerate((up_keep, up_send)):
            for c in range(4):
                out_slots[side, c] = both[side][c * part : (c + 1) * part]
                copy = pltpu.make_async_copy(out_slots.at[side, c], target.at[c, pl.ds(model, part), :], out_sems.at[side, c])
                copy.start()
                going.append(copy)
        for j in range(4):
            going += [down_copy(j), *up_copies(j, block_of(j, info))]
        for copy in going:
            copy.wait()


def block_of(step, info):
    return lax.bitwise_xor(step // 2, 1 - info[1]) * 2 + step % 2


def mlp_call(info, pieces, middle_n, mixed_t, vecs, w_up, w_down):
    ncol = len(pieces)
    piece = pieces[1].shape
    tokens, model = middle_n.shape
    steps = w_down.shape[0] // model
    part, chunk = model // 4, model // 2
    rows = min(tokens, 256)
    stays = pl.BlockSpec(memory_space=pltpu.HBM)

    def block(j, info):
        return block_of(jnp.minimum(j, steps - 1), info)

    down, up = (4, 2 * part, model), (steps, model + part, chunk)
    return pl.pallas_call(
        functools.partial(mlp_kernel, ncol),
        grid_spec=pltpu.PrefetchScalarGridSpec(
            num_scalar_prefetch=1,
            grid=(steps + 1,),
            in_specs=[stays] * ncol
            + [
                whole(middle_n.shape),
                stays,
                whole(vecs.shape),
                pl.BlockSpec((model, model), lambda j, info: (0, block(j, info))),
                pl.BlockSpec((model, model), lambda j, info: (block(j, info), 0)),
            ],
            out_specs=[whole(piece)] * ncol + [stays, whole((16, model))] + [stays] * 4,
            scratch_shapes=[
                pltpu.VMEM((ncol,) + piece, BF16),
                pltpu.VMEM((tokens, model), BF16),
                pltpu.VMEM((model, tokens), BF16),
                pltpu.VMEM((tokens, model), BF16),
                pltpu.VMEM((model, tokens), BF16),
                pltpu.VMEM((tokens, model), BF16),
                pltpu.VMEM((tokens, model), BF16),
                pltpu.VMEM((tokens, model), F32),
                pltpu.VMEM((tokens, model), F32),
                pltpu.VMEM((model, tokens), BF16),
                pltpu.VMEM((2, steps, model, chunk), BF16),
                pltpu.VMEM((steps, 4, part, model), BF16),
                pltpu.VMEM((2, 4, part, chunk), BF16),
                pltpu.SemaphoreType.DMA((ncol + 1,)),
                pltpu.SemaphoreType.DMA((2, steps)),
                pltpu.SemaphoreType.DMA((steps,)),
                pltpu.SemaphoreType.DMA((2, 4)),
                pltpu.SemaphoreType.DMA((tokens // rows,)),
            ],
        ),
        out_shape=[pltpu.HBM(piece, BF16)] * ncol
        + [pltpu.HBM((tokens, model), F32), jax.ShapeDtypeStruct((16, model), F32)]
        + [pltpu.HBM(s, BF16) for s in (down, down, up, up)],
        compiler_params=params(60),
        cost_estimate=cost(40),
        name="mlp",
    )(info, *[in_hbm(p) for p in pieces], in_hbm(middle_n), in_hbm(mixed_t), vecs, in_hbm(w_up), in_hbm(w_down))


def attend_back_kernel(ncol, block, first, info, lens, *refs):
    pieces = refs[:ncol]
    ranks, vecs, w_qkv_in, w_out, qkv_t, lse, mixed_t, gmiddle_n = refs[ncol : ncol + 8]
    gproj_t, normed_n, sums, *outs = refs[-15 - ncol : -12]
    gmixed_t, gacc, columns, kv_n, mask, scores, gprobs, probs, gscores, inner, w_qkv, sem = refs[-12:]
    size, model = gmiddle_n.shape
    head = model // HEADS
    step = pl.program_id(0)

    coming = pltpu.make_async_copy(w_qkv_in, w_qkv, sem.at[0])

    @pl.when(step == 0)
    def _():
        coming.start()
        sums[...] = jnp.zeros_like(sums)
        columns[...] = jnp.zeros_like(columns)

    gmixed_t[...] = dot_nt(w_out[...], gmiddle_n[...].astype(BF16)).astype(BF16)
    kv_n[...] = qkv_t[model:].astype(F32).T.astype(BF16)
    mask_lanes(ranks, lens[first + step], mask)
    product = gmixed_t[...].astype(F32) * mixed_t[...].astype(F32)
    for h in range(HEADS):
        inner[h : h + 1] = row_sum(product[h * head : (h + 1) * head])
    many = size != block
    if many:
        gacc[...] = jnp.zeros_like(gacc)

    def begin(pair, at, slot):
        low, high = pair * 2 * head, (pair * 2 + 1) * head
        where = pl.ds(at, block)
        right = pair_diagonal(qkv_t[pl.ds(low, head), where], qkv_t[pl.ds(high, head), where])
        scores[slot] = dot(kv_n[:, pl.ds(low, 2 * head)], right)
        right = pair_diagonal(gmixed_t[pl.ds(low, head), where], gmixed_t[pl.ds(high, head), where])
        gprobs[slot] = dot(kv_n[:, pl.ds(model + low, 2 * head)], right)

    def weigh(pair, at, slot):
        where = pl.ds(at, block)
        stats, means = (
            jnp.concatenate([rows[pl.ds(pair * 2 + i, 1), where] for i in range(2)], axis=1) for rows in (lse.at[0], inner)
        )
        value = jnp.exp(scores[slot] + across(mask[...], 2 * block) - stats)
        probs[slot] = value.astype(BF16)
        gscores[slot] = (value * (gprobs[slot] - means)).astype(BF16)

    def spread(pair, at, slot):
        where = pl.ds(at, block)
        for side in range(2):
            start, cut = (pair * 2 + side) * head, slice(side * block, (side + 1) * block)
            grad_side = gscores[slot, :, cut]
            grad_q = dot(qkv_t[pl.ds(model + start, head), :], grad_side) * head**-0.5
            grad_k = dot_nt(qkv_t[pl.ds(start, head), where], grad_side)
            grad_v = dot_nt(gmixed_t[pl.ds(start, head), where], probs[slot, :, cut])
            gproj_t[pl.ds(start, head), where] = grad_q.astype(BF16)
            if many:
                gacc[pl.ds(start, head), :] += grad_k
                gacc[pl.ds(model + start, head), :] += grad_v
            else:
                gproj_t[pl.ds(model + start, head), :] = grad_k.astype(BF16)
                gproj_t[pl.ds(2 * model + start, head), :] = grad_v.astype(BF16)

    pairs_and_blocks(size, block, (begin, weigh, spread))
    if many:
        gproj_t[model:] = gacc[...].astype(BF16)
    columns[:model] += lane_sums(gproj_t[:model].astype(F32))
    columns[model:] += lane_sums(gproj_t[2 * model :].astype(F32))

    @pl.when(step == 0)
    def _():
        coming.wait()

    grad = dot(w_qkv[...], gproj_t[...]).T
    xhat, root = standardise(token_rows(pieces).astype(F32))
    gain = vecs[GAIN_ONE : GAIN_ONE + 1]
    normed_n[...] = (xhat * gain + vecs[SHIFT_ONE : SHIFT_ONE + 1]).astype(BF16)
    sums[0:1] += row_sum(grad * xhat)
    sums[1:2] += row_sum(grad)
    total = gmiddle_n[...] + standardise_back(grad, gain, xhat, root)
    result = total.astype(BF16)
    width = size // ncol
    for k in range(ncol):
        outs[k][0] = result[k * width : (k + 1) * width]

    @pl.when(step == pl.num_programs(0) - 1)
    def _():
        for i in range(2):
            sums[2 + i : 3 + i] = row_sum(columns[i * model : (i + 1) * model].T)


def attend_back_call(
    info, lens, pieces, ranks, vecs, w_qkv, w_out, qkv_t, lse, mixed_t, gmiddle_n, first, frames, per, earlier=()
):
    ncol = len(pieces)
    width, model = pieces[1].shape[1:]
    size = ncol * width
    tokens = per * size
    block = min(size, 256)
    acc = (2 * model, size) if size != block else (8, 128)

    def later(spec_lanes, shape):
        if spec_lanes:
            return pl.BlockSpec(shape, lambda f, *_: (0, first + f))
        return pl.BlockSpec(shape, lambda f, *_: (first + f,) + (0,) * (len(shape) - 1))

    own = pl.BlockSpec((1, width, model), lambda f, info, *_: (info[0] * per + first + f, 0, 0))
    piece = later(False, (1, width, model))
    return pl.pallas_call(
        functools.partial(attend_back_kernel, ncol, block, first),
        grid_spec=pltpu.PrefetchScalarGridSpec(
            num_scalar_prefetch=2,
            grid=(frames,),
            in_specs=[own]
            + [piece] * (ncol - 1)
            + [
                whole(ranks.shape),
                whole(vecs.shape),
                pl.BlockSpec(memory_space=pltpu.HBM),
                whole(w_out.shape),
                later(True, (3 * model, size)),
                later(False, (1, 16, size)),
                later(True, (model, size)),
                later(False, (size, model)),
            ]
            + [pl.BlockSpec(memory_space=pl.ANY)] * len(earlier),
            out_specs=[later(True, (3 * model, size)), later(False, (size, model)), whole((16, model))] + [piece] * ncol,
            scratch_shapes=[
                pltpu.VMEM((model, size), BF16),
                pltpu.VMEM(acc, F32),
                pltpu.VMEM((2 * model, 128), F32),
                pltpu.VMEM((size, 2 * model), BF16),
                pltpu.VMEM((size, 128), F32),
                pltpu.VMEM((slots(size, block), size, 2 * block), F32),
                pltpu.VMEM((slots(size, block), size, 2 * block), F32),
                pltpu.VMEM((slots(size, block), size, 2 * block), BF16),
                pltpu.VMEM((slots(size, block), size, 2 * block), BF16),
                pltpu.VMEM((16, size), F32),
                pltpu.VMEM(w_qkv.shape, BF16),
                pltpu.SemaphoreType.DMA((1,)),
            ],
        ),
        out_shape=[
            pltpu.HBM((3 * model, tokens), BF16),
            pltpu.HBM((tokens, model), BF16),
            pltpu.HBM((16, model), F32),
        ]
        + [pltpu.HBM((per, width, model), BF16)] * ncol,
        input_output_aliases={ncol + 10 + i: i + (i > 1) for i in range(len(earlier))},
        compiler_params=params(40 if size == block else 62),
        cost_estimate=cost(15),
        name="attend_back",
    )(info, lens, *pieces, ranks, vecs, in_hbm(w_qkv), in_hbm(w_out), in_hbm(qkv_t), lse, in_hbm(mixed_t), in_hbm(gmiddle_n), *earlier)


def take_kernel(info, *refs):
    half = len(refs) // 2
    for source, target in zip(refs[:half], refs[half:]):
        target[...] = source[...]


def take_frames(info, array, ncol, group=0, groups=1):
    per = array.shape[0] // ncol // groups
    shape = (per,) + array.shape[1:]
    specs = [
        pl.BlockSpec(shape, lambda i, info, k=k: (lax.bitwise_xor(info[0], k) * groups + group, 0, 0))
        for k in range(1, ncol)
    ]
    return pl.pallas_call(
        take_kernel,
        grid_spec=pltpu.PrefetchScalarGridSpec(
            num_scalar_prefetch=1,
            grid=(1,),
            in_specs=specs,
            out_specs=[pl.BlockSpec(shape, lambda i, *_: (0, 0, 0))] * (ncol - 1),
        ),
        out_shape=[pltpu.HBM(shape, array.dtype)] * (ncol - 1),
        compiler_params=params(8),
        cost_estimate=cost(1),
        name="take_frames",
    )(info, *[in_hbm(array)] * (ncol - 1))


def place_kernel(info, *refs):
    *pieces, out = refs
    for k, piece in enumerate(pieces):

        @pl.when(pl.program_id(0) == k)
        def _(piece=piece):
            out[...] = piece[...].astype(out.dtype)


def place_frames(info, pieces, dtype):
    shape = pieces[0].shape
    return pl.pallas_call(
        place_kernel,
        grid_spec=pltpu.PrefetchScalarGridSpec(
            num_scalar_prefetch=1,
            grid=(len(pieces),),
            in_specs=[whole(shape)] * len(pieces),
            out_specs=pl.BlockSpec(shape, lambda k, info: (lax.bitwise_xor(info[0], k), 0, 0)),
        ),
        out_shape=pltpu.HBM((len(pieces) * shape[0],) + shape[1:], dtype),
        compiler_params=params(12),
        cost_estimate=cost(2),
        name="place_frames",
    )(info, *pieces)


def pick(array, index, axis):
    return lax.dynamic_index_in_dim(array, index, axis, keepdims=False)


class Comm:
    def __init__(self, mesh):
        self.ncol = mesh.shape["col"]
        self.nclip = mesh.shape["clip"]
        self.nz = self.nclip // 2
        self.me = lax.axis_index("col")
        self.clip = lax.axis_index("clip")
        self.core = lax.rem(self.clip, 2)
        self.z = lax.div(self.clip, 2)

    def col_swap(self, array, distance):
        return lax.ppermute(array, "col", [(i, i ^ distance) for i in range(self.ncol)])

    def core_swap(self, array):
        return lax.ppermute(array, "clip", [(i, i ^ 1) for i in range(self.nclip)])

    def z_move(self, array, pairs):
        moves = [(2 * a + c, 2 * b + c) for a, b in pairs for c in range(2)]
        return lax.ppermute(array, "clip", moves)

    def z_swap(self, array, distance):
        return lax.ppermute(array, "clip", [(i, i ^ (2 * distance)) for i in range(self.nclip)])

    def halve(self, terms, bits):
        nbits = self.ncol.bit_length() - 1
        present = list(range(nbits - 1, -1, -1))
        for bit in bits:
            axis = present.index(bit)
            mine = lax.rem(lax.shift_right_logical(self.me, bit), 2)
            away = [pick(t, 1 - mine, axis) for t in terms]
            total = away[0]
            if len(away) > 1:
                total = add_low(away[0], away[1])
            landed = self.col_swap(total, 1 << bit)
            near = [pick(t, mine, axis) for t in terms]
            if len(near) > 1:
                near = [add_low(near[0], near[1])]
            terms = [near[0], landed]
            present.pop(axis)
        return add_low(terms[0], terms[1])

    def reduce_rows(self, grad):
        rows, depth = grad.shape
        part = rows // self.ncol // 4
        nbits = self.ncol.bit_length() - 1
        split = grad.reshape(self.ncol, 2, 2, part, depth)
        keep = pick(split, self.core, 1)
        landed = self.core_swap(pick(split, 1 - self.core, 1))
        order = list(range(nbits))
        half = nbits // 2
        orders = (order, order[half:] + order[:half])
        done = []
        for side in range(2):
            terms = [
                t[:, side].reshape((2,) * nbits + (part, depth)) for t in (keep, landed)
            ]
            done.append(self.halve(terms, orders[side]))
        total = jnp.concatenate(done, axis=0)
        total = self.sum_line(total)
        other = self.core_swap(total)
        first = self.core == 0
        return jnp.concatenate(
            [jnp.where(first, total, other), jnp.where(first, other, total)], axis=0
        )

    def sum_line(self, total):
        nz = self.nz
        for step in range(nz // 2 - 1):
            total = add_low(total, self.z_move(total, [(step, step + 1), (nz - 1 - step, nz - 2 - step)]))
        low, high = nz // 2 - 1, nz // 2
        total = add_low(total, self.z_move(total, [(low, high), (high, low)]))
        for step in range(nz // 2 - 1, 0, -1):
            landed = self.z_move(total, [(step, step - 1), (nz - 1 - step, nz - step)])
            takes = jnp.logical_or(self.z == step - 1, self.z == nz - step)
            total = jnp.where(takes, landed, total)
        return total


def qkv_kernel(info, gproj_t, normed_n, mlp_sums, *refs):
    *att, keep, send, vectors = refs
    c = pl.program_id(0)
    model = mlp_sums.shape[1]
    rows = gproj_t.shape[0] // 2
    part = model // 4

    for i in range(4):

        @pl.when(c == i)
        def _(i=i):
            att_sums = att[0][...]
            for more in att[1:]:
                att_sums = att_sums + more[...]
            vectors[...] = jnp.zeros_like(vectors)
            vectors[0, 0:4, :part] = mlp_sums[0:4, i * part : (i + 1) * part]
            vectors[0, 4:5, :] = mlp_sums[4 + i : 5 + i]
            vectors[1, 0:2, :part] = att_sums[0:2, i * part : (i + 1) * part]
            start = i % 2 * 2 * part
            vectors[1, 2:3, : 2 * part] = att_sums[2 + i // 2 : 3 + i // 2, start : start + 2 * part]

    for side, target in enumerate((keep, send)):
        which = lax.bitwise_xor(info[1], side)
        half = gproj_t[pl.ds(pl.multiple_of(which * rows, rows), rows), :]
        target[0, :rows] = dot(half, normed_n[...]).astype(BF16)
        target[0, rows:] = vectors[which].astype(BF16)


VECTOR_ROWS = 32


def qkv_call(info, gproj_t, normed_n, mlp_sums, att_sums):
    model = mlp_sums.shape[1]
    rows = 3 * model // 4
    block = (1, rows // 2 + VECTOR_ROWS, model)
    out = jax.ShapeDtypeStruct((4,) + block[1:], BF16)
    others = (normed_n, mlp_sums, *att_sums)
    return pl.pallas_call(
        qkv_kernel,
        grid_spec=pltpu.PrefetchScalarGridSpec(
            num_scalar_prefetch=1,
            grid=(4,),
            in_specs=[pl.BlockSpec((rows, gproj_t.shape[1]), lambda c, info: (c, 0))]
            + [whole(o.shape) for o in others],
            out_specs=[pl.BlockSpec(block, lambda c, info: (c, 0, 0))] * 2,
            scratch_shapes=[pltpu.VMEM((2, VECTOR_ROWS, model), F32)],
        ),
        out_shape=[out, out],
        compiler_params=params(24),
        cost_estimate=cost(6),
        name="grad_qkv",
    )(info, in_hbm(gproj_t), in_hbm(normed_n), *others[1:])


def sum_core_kernel(info, *refs):
    for i in range(4):
        refs[8 + i][...] = add_low(refs[i][...], refs[4 + i][...])


def sum_core(info, keep, landed):
    rows, depth = keep.shape[1] // 2, keep.shape[2]
    block = (1, rows, depth)

    def by_x(i, info, flip, side):
        return (2 * i + lax.bitwise_xor(info[2], flip), side, 0)

    def by_y(i, info, flip, side):
        return (2 * lax.bitwise_xor(info[3], flip) + i, side, 0)

    specs = [
        pl.BlockSpec(block, functools.partial(lambda i, info, fn, flip, side: fn(i, info, flip, side), fn=fn, flip=flip, side=side))
        for side, fn in enumerate((by_x, by_y))
        for flip in (1, 0)
    ]
    out = jax.ShapeDtypeStruct((2, rows, depth), BF16)
    return pl.pallas_call(
        sum_core_kernel,
        grid_spec=pltpu.PrefetchScalarGridSpec(
            num_scalar_prefetch=1,
            grid=(2,),
            in_specs=specs * 2,
            out_specs=[pl.BlockSpec(block, lambda i, info: (i, 0, 0))] * 4,
        ),
        out_shape=[out] * 4,
        compiler_params=params(16),
        cost_estimate=cost(2),
        name="sum_core",
    )(info, *[keep] * 4, *[landed] * 4)


def sum_first_kernel(info, keep_a, land_a, keep_b, land_b, send_a, stay_a, send_b, stay_b):
    for keep, land, send, stay, mine in (
        (keep_a, land_a, send_a, stay_a, info[3]),
        (keep_b, land_b, send_b, stay_b, info[2]),
    ):
        send[...] = add_low(keep[1 - mine], land[1 - mine])
        stay[...] = add_low(keep[mine], land[mine])


def sum_first(info, keep_a, land_a, keep_b, land_b):
    rows, depth = keep_a.shape[1:]
    out = jax.ShapeDtypeStruct((rows, depth), BF16)
    return pl.pallas_call(
        sum_first_kernel,
        grid_spec=pltpu.PrefetchScalarGridSpec(
            num_scalar_prefetch=1,
            grid=(1,),
            in_specs=[whole(keep_a.shape)] * 4,
            out_specs=[whole((rows, depth))] * 4,
        ),
        out_shape=[out] * 4,
        compiler_params=params(16),
        cost_estimate=cost(1),
        name="sum_first",
    )(info, keep_a, land_a, keep_b, land_b)


def sum_second_kernel(info, stay_a, land_a, stay_b, land_b, own, send):
    low, high = add_low(stay_a[...], land_a[...]), add_low(stay_b[...], land_b[...])
    own[...] = jnp.where(info[4] == 0, low, high)
    send[...] = jnp.where(info[4] == 0, high, low)


def sum_second(info, stay_a, land_a, stay_b, land_b):
    shape = stay_a.shape
    return pl.pallas_call(
        sum_second_kernel,
        grid_spec=pltpu.PrefetchScalarGridSpec(
            num_scalar_prefetch=1, grid=(1,), in_specs=[whole(shape)] * 4, out_specs=[whole(shape)] * 2
        ),
        out_shape=[jax.ShapeDtypeStruct(shape, BF16)] * 2,
        compiler_params=params(16),
        cost_estimate=cost(1),
        name="sum_second",
    )(info, stay_a, land_a, stay_b, land_b)


def collect(info, parts, full):
    rows = parts[0].shape[0]
    for i, part in enumerate(parts):
        at = lax.bitwise_xor(info[4], i % 2) * rows
        full[lax.bitwise_xor(info[1], i // 2), pl.ds(pl.multiple_of(at, rows), rows), :] = part[...]


def finish_down_kernel(info, *refs):
    *parts, down_t, full = refs
    collect(info, parts, full)
    model, part = full.shape[2], down_t.shape[0]
    blocks = full.shape[1] // part
    for half in range(2):
        for j in range(blocks):
            at = (half * blocks + j) * model
            down_t[:, at : at + model] = full[half, j * part : (j + 1) * part].astype(F32)


def finish_up_kernel(info, *refs):
    *parts, up, out_t, full = refs
    collect(info, parts, full)
    model, chunk = up.shape[0], full.shape[2]
    for half in range(2):
        cut = slice(half * chunk, (half + 1) * chunk)
        up[:, cut] = full[half, :model].astype(F32)
        out_t[:, cut] = full[half, model:].astype(F32)


def finish_qkv_kernel(info, *refs):
    *parts, qkv_t, gain_one, shift_one, bias_qv, gain_two, shift_two, bias_out, bias_down, bias_up, full = refs
    collect(info, parts, full)
    rows = qkv_t.shape[0] // 2
    for half in range(2):
        qkv_t[half * rows : (half + 1) * rows] = full[half, :rows].astype(F32)
    mlp_rows = full[0, rows : rows + 16].astype(F32)
    att_rows = full[1, rows : rows + 16].astype(F32)
    for source, targets in ((mlp_rows, (gain_two, shift_two, bias_out, bias_down, bias_up)), (att_rows, (gain_one, shift_one, bias_qv))):
        for i, target in enumerate(targets):
            target[...] = source[i, : target.shape[0]]


def finish(kernel, name, info, parts, shapes):
    rows, depth = parts[0].shape
    return pl.pallas_call(
        kernel,
        grid_spec=pltpu.PrefetchScalarGridSpec(
            num_scalar_prefetch=1,
            grid=(1,),
            in_specs=[whole((rows, depth))] * 4,
            out_specs=[whole(s) for s in shapes],
            scratch_shapes=[pltpu.VMEM((2, 2 * rows, depth), BF16)],
        ),
        out_shape=[pltpu.HBM(s, F32) for s in shapes],
        compiler_params=params(24),
        cost_estimate=cost(2),
        name=name,
    )(info, *parts)


def wait_for(values, *others):
    flat, tree = jax.tree.flatten(values)
    held = lax.optimization_barrier((tuple(flat), others))[0]
    return jax.tree.unflatten(tree, held)


def join(*values):
    flat, tree = jax.tree.flatten(values)
    return jax.tree.unflatten(tree, lax.optimization_barrier(tuple(flat)))


def make(mesh):
    def on_device(
        frames,
        cotangent,
        frame_len,
        column_rank,
        gain_one,
        shift_one,
        w_qkv,
        bias_qv,
        w_out,
        bias_out,
        gain_two,
        shift_two,
        w_up,
        bias_up,
        w_down,
        bias_down,
    ):
        comm = Comm(mesh)
        ncol, me = comm.ncol, comm.me
        count, width, model = frames.shape
        hidden_size = w_down.shape[0]
        per = count // ncol
        size = ncol * width
        groups = 2 if per % 2 == 0 else 1
        part = per // groups
        middle_z = jnp.logical_or(comm.z == 1, comm.z == 2)
        info = jnp.stack([me, comm.core, lax.rem(me, 2), lax.div(me, 2), middle_z.astype(me.dtype)]).astype(jnp.int32)
        order = lax.bitwise_xor(me, jnp.arange(ncol, dtype=jnp.int32))
        ranks = column_rank.reshape(ncol, width)[order].reshape(size, 1)
        lens = pick(frame_len.reshape(ncol, per), me, 0)
        given = [gain_one, shift_one, bias_out, gain_two, shift_two, bias_down, bias_qv, bias_up]
        total, at, vecs = sum(v.size for v in given), 0, 0.0
        for v in given:
            vecs = vecs + jnp.pad(v.astype(F32), (at, total - at - v.size))
            at += v.size
        vecs = vecs.reshape(-1, model)

        def swap(pieces):
            return [comm.col_swap(p, k + 1) for k, p in enumerate(pieces)]

        paired = ncol == 4 and comm.nz == 4

        class Chunk:
            land = ()

            def core(self, keep, land):
                sa, self.ka, sb, self.kb = sum_core(info, keep, land)
                self.land = [comm.col_swap(sa, 1), comm.col_swap(sb, 2)]

            def first(self):
                sa, self.ka, sb, self.kb = sum_first(info, self.ka, self.land[0], self.kb, self.land[1])
                self.land = [comm.col_swap(sa, 2), comm.col_swap(sb, 1)]

            def second(self):
                self.own, send = sum_second(info, self.ka, self.land[0], self.kb, self.land[1])
                self.land = comm.z_swap(send, 1)

            def inner(self):
                self.own = add_low(self.own, self.land)
                self.land = comm.z_swap(self.own, 3)

            def outer(self):
                self.own = add_low(self.own, self.land)
                self.land = [comm.z_swap(self.own, 1), comm.core_swap(self.own)]

            def swap(self):
                self.parts = [self.own] + self.land
                self.land = comm.core_swap(self.parts[1])

            def last(self, kernel, name, shapes):
                return finish(kernel, name, info, self.parts + [self.land], shapes)

        landed = swap(take_frames(info, frames, ncol))
        cot_send = take_frames(info, cotangent, ncol)
        landed[0], cot_send, ranks, vecs, lens = join(landed[0], cot_send, ranks, vecs, lens)
        cot_land = swap(cot_send)
        rows = [frames, *join(*landed)]
        kept = attend_call(info, lens, rows, ranks, vecs, w_qkv, w_out, 0, per, per)
        kept, landed = join(kept, cot_land)
        qkv_t, mixed_t, middle_n, lse = kept
        cots = [cotangent, *landed]
        results = mlp_call(info, cots, middle_n, mixed_t, vecs, w_up, w_down)
        *outs, gmiddle_n, mlp_sums, down_keep, down_send, up_keep, up_send = join(*results)

        def back(gmiddle_n, g, earlier=()):
            return attend_back_call(
                info, lens, rows, ranks, vecs, w_qkv, w_out, qkv_t, lse, mixed_t, gmiddle_n, g * part, part, per, earlier
            )

        if not paired:
            out_land = swap(outs[1:])
            att_sums, earlier = 0.0, ()
            for g in range(groups):
                gproj_t, normed, sums, *gouts = back(gmiddle_n, g, earlier)
                att_sums, earlier = att_sums + sums, (gproj_t, normed, *gouts)
            output = place_frames(info, [outs[0]] + out_land, BF16)
            grad_input = place_frames(info, [gouts[0]] + swap(gouts[1:]), F32)
            first = comm.core == 0
            steps, part = hidden_size // model, model // 4

            def halves(keep, send):
                return jnp.stack([jnp.where(first, keep, send), jnp.where(first, send, keep)])

            def reduced(grad):
                return comm.reduce_rows(grad.astype(BF16)).astype(F32).T

            grad = halves(up_keep, up_send)
            grad_w_up = reduced(grad[:, :, :model].transpose(1, 0, 3, 2).reshape(hidden_size, model))
            grad_w_out = reduced(grad[:, :, model:].transpose(1, 2, 0, 3).reshape(model, model))
            grad = halves(down_keep, down_send).reshape(2, 4, steps // 2, part, model).transpose(1, 3, 0, 2, 4)
            grad_w_down = reduced(grad.reshape(model, hidden_size))
            grad_w_qkv = reduced(dot(gproj_t, normed))
            sums = jnp.concatenate([mlp_sums, att_sums])
            sums = reduced(jnp.concatenate([sums] * ncol)).T

            def own(row, rows=1):
                return pick(sums[row : row + rows].reshape(ncol, -1), me, 0)

            return (
                output, grad_input, own(16), own(17), grad_w_qkv, own(18, 2), grad_w_out, own(2), own(0), own(1),
                grad_w_up, own(4, steps), grad_w_down, own(3),
            )

        down, up, qkv = Chunk(), Chunk(), Chunk()
        down_land, up_land = comm.core_swap(down_send), comm.core_swap(up_send)
        down.core(down_keep, down_land)
        results = back(wait_for(gmiddle_n, down.ka), 0)
        down.land, up_land, results = join(down.land, up_land, results)
        gproj_t, normed, att_sums_a, *gouts = results

        down.first()
        up.core(up_keep, wait_for(up_land, down.ka))
        results = back(wait_for(gmiddle_n, up.ka), 1, (gproj_t, normed, *gouts))
        gproj_t, normed, att_sums_b, *gouts = results
        results_q = qkv_call(info, gproj_t, normed, mlp_sums, (att_sums_a, att_sums_b))
        down.land, up.land, gouts, results_q = join(down.land, up.land, gouts, results_q)
        qkv_keep, qkv_send = results_q

        qkv_land = comm.core_swap(qkv_send)
        up.land = wait_for(up.land, qkv_send)
        up.first()
        down.land = wait_for(down.land, up.ka)
        down.second()
        qkv_land, up.land, down.land, down.own, outs = join(qkv_land, up.land, down.land, down.own, outs)

        qkv.core(qkv_keep, qkv_land)
        down.land = wait_for(down.land, qkv.ka)
        down.inner()
        up.land = wait_for(up.land, down.own)
        up.second()
        qkv.land, up.land, down.own, up.own, outs = join(qkv.land, up.land, down.own, up.own, outs)

        qkv.first()
        up.land = wait_for(up.land, qkv.ka)
        up.inner()
        out_land = swap(outs[1:])
        qkv.land, down.land, down.own, up.own, gouts = join(qkv.land, down.land, down.own, up.own, gouts)

        qkv.second()
        gouts, down.land = wait_for((gouts, down.land), qkv.own)
        gin_land = swap(gouts[1:])
        down.outer()
        qkv.land, up.land, qkv.own, down.own = join(qkv.land, up.land, qkv.own, down.own)

        qkv.inner()
        up.land = wait_for(up.land, qkv.own)
        up.outer()
        qkv.land, down.land, out_land, gin_land, qkv.own, up.own = join(qkv.land, down.land, out_land, gin_land, qkv.own, up.own)

        qkv.outer()
        up.land = wait_for(up.land, qkv.own)
        up.swap()
        down.land = wait_for(down.land, up.parts[1])
        down.swap()
        output = place_frames(info, [outs[0], *wait_for(out_land, up.parts[1])], BF16)
        grad_input = place_frames(info, [gouts[0], *wait_for(gin_land, up.parts[1])], F32)
        down.parts, down.land = wait_for((down.parts, down.land), grad_input)
        (grad_w_down,) = down.last(finish_down_kernel, "finish_down", [(model // 4, hidden_size)])
        qkv.land, up.land, up.parts, qkv.own, output, grad_w_down = join(qkv.land, up.land, up.parts, qkv.own, output, grad_w_down)

        qkv.swap()
        up.parts, up.land = wait_for((up.parts, up.land), qkv.parts[0])
        grad_w_up, grad_w_out = up.last(
            finish_up_kernel, "finish_up", [(model, hidden_size // 4), (model // 4, model)]
        )
        qkv.land, qkv.parts, grad_w_up = join(qkv.land, qkv.parts, grad_w_up)
        part = model // 4
        vectors = [(part,), (part,), (2 * part,), (part,), (part,), (part,), (part,), (hidden_size // 4,)]
        grad_w_qkv, g_gain_one, g_shift_one, g_bias_qv, g_gain_two, g_shift_two, g_bias_out, g_bias_down, g_bias_up = qkv.last(
            finish_qkv_kernel, "finish_qkv", [(3 * model // 4, model)] + vectors
        )
        grad_w_qkv, grad_w_out, grad_w_down = grad_w_qkv.T, grad_w_out.T, grad_w_down.T
        return (
            output,
            grad_input,
            g_gain_one,
            g_shift_one,
            grad_w_qkv,
            g_bias_qv,
            grad_w_out,
            g_bias_out,
            g_gain_two,
            g_shift_two,
            grad_w_up,
            g_bias_up,
            grad_w_down,
            g_bias_down,
        )

    return on_device


def solution(mesh):
    return jax.shard_map(
        make(mesh),
        mesh=mesh,
        in_specs=(P("clip", "col", None), P("clip", "col", None), P("clip")) + (P(),) * 13,
        out_specs=(
            P("clip", "col", None),
            P("clip", "col", None),
            P("col"),
            P("col"),
            P(None, "col"),
            P("col"),
            P(None, "col"),
            P("col"),
            P("col"),
            P("col"),
            P(None, "col"),
            P("col"),
            P(None, "col"),
            P("col"),
        ),
        check_vma=False,
    )
```
